32 devices in a mesh: dp: 8 (over z, y), mp: 4 (over x, core).
Axes of the slice: x: 2, y: 2, z: 4, core: 2. Of those that a mesh axis runs over, the one named last changes fastest.
Arguments:
- tokens: bfloat16 [7168, 2304], P('dp'), may hold values from -6 to 6
- segments: int32 [7168], P('dp'), may hold values from -1 to 3, as said below
- cotangent: bfloat16 [7168, 2304], P('dp'), may hold values from -6 to 6
- query_weight: float32 [2304, 2048], P('dp', 'mp'), may hold values from -0.21875 to 0.21875
- keyval_weight: float32 [2, 2304, 1024], P(None, 'dp', 'mp'), may hold values from -0.21875 to 0.21875
- output_weight: float32 [2048, 2304], P('mp', 'dp'), may hold values from -0.125 to 0.125
- gateup_weight: float32 [2, 2304, 9216], P(None, 'dp', 'mp'), may hold values from -0.125 to 0.125
- down_weight: float32 [9216, 2304], P('mp', 'dp'), may hold values from -0.0625 to 0.0625
- norm_gains: float32 [4, 2304], P(None, 'dp'), may hold values from -0.5 to 0.5
- moment_query: float32 [2304, 2048], P('dp', 'mp'), may hold values from -18 to 18
- moment_keyval: float32 [2, 2304, 1024], P(None, 'dp', 'mp'), may hold values from -18 to 18
- moment_output: float32 [2048, 2304], P('mp', 'dp'), may hold values from -18 to 18
- moment_gateup: float32 [2, 2304, 9216], P(None, 'dp', 'mp'), may hold values from -18 to 18
- moment_down: float32 [9216, 2304], P('mp', 'dp'), may hold values from -18 to 18
- moment_gains: float32 [4, 2304], P(None, 'dp'), may hold values from -18 to 18
- square_query: float32 [2304, 2048], P('dp', 'mp'), may hold values from 10 to 3000
- square_keyval: float32 [2, 2304, 1024], P(None, 'dp', 'mp'), may hold values from 10 to 3000
- square_output: float32 [2048, 2304], P('mp', 'dp'), may hold values from 10 to 3000
- square_gateup: float32 [2, 2304, 9216], P(None, 'dp', 'mp'), may hold values from 10 to 3000
- square_down: float32 [9216, 2304], P('mp', 'dp'), may hold values from 10 to 3000
- square_gains: float32 [4, 2304], P(None, 'dp'), may hold values from 10 to 3000
Outputs:
- block_out: bfloat16 [7168, 2304], P('dp')
- input_grad: float32 [7168, 2304], P('dp')
- grad_query: float32 [2304, 2048], P('dp', 'mp')
- grad_keyval: float32 [2, 2304, 1024], P(None, 'dp', 'mp')
- grad_output: float32 [2048, 2304], P('mp', 'dp')
- grad_gateup: float32 [2, 2304, 9216], P(None, 'dp', 'mp')
- grad_down: float32 [9216, 2304], P('mp', 'dp')
- grad_gains: float32 [4, 2304], P(None, 'dp')
- change_query: float32 [2304, 2048], P('dp', 'mp')
- change_keyval: float32 [2, 2304, 1024], P(None, 'dp', 'mp')
- change_output: float32 [2048, 2304], P('mp', 'dp')
- change_gateup: float32 [2, 2304, 9216], P(None, 'dp', 'mp')
- change_down: float32 [9216, 2304], P('mp', 'dp')
- change_gains: float32 [4, 2304], P(None, 'dp')
- momenta_query: float32 [2304, 2048], P('dp', 'mp')
- momenta_keyval: float32 [2, 2304, 1024], P(None, 'dp', 'mp')
- momenta_output: float32 [2048, 2304], P('mp', 'dp')
- momenta_gateup: float32 [2, 2304, 9216], P(None, 'dp', 'mp')
- momenta_down: float32 [9216, 2304], P('mp', 'dp')
- momenta_gains: float32 [4, 2304], P(None, 'dp')
- squares_query: float32 [2304, 2048], P('dp', 'mp')
- squares_keyval: float32 [2, 2304, 1024], P(None, 'dp', 'mp')
- squares_output: float32 [2048, 2304], P('mp', 'dp')
- squares_gateup: float32 [2, 2304, 9216], P(None, 'dp', 'mp')
- squares_down: float32 [9216, 2304], P('mp', 'dp')
- squares_gains: float32 [4, 2304], P(None, 'dp')
The draws below stay inside these ranges and needn't reach their ends.
Inputs may be any that keep to these rules, and one draw needn't show every extreme that they name: `segments`: within each block of 896 slots of one index of dp, ids are non-decreasing from 0 over the leading slots and -1 on the padding slots at the block's end; in some block one sequence of 896 tokens fills it, some block is half padding, and in some block ids reach 3.
All inputs are finite; a program needn't handle non-finite values.
Results may differ from the reference program's by a relative error of at most 0.035.
The reference program's roundings to bfloat16 on the way count: a program that leaves them out, or rounds other values in their place, can miss the bound.
Values may be sent and summed in bfloat16 or wider, within the bound.
No kernel may reach another device: no remote copies, remote signals or barrier semaphores. Data moves between devices by JAX's collectives and lax.ppermute only.
A program may use at most 320 MiB of HBM per device.

```python
import math
import jax
import jax.numpy as jnp
from jax import lax

D = 2304
HEADS = 8
KV_HEADS = 4
HEAD_DIM = 256
FF = 9216
WINDOW = 4096
ADAM_STEP = 5
GROUP_TOK = 896
GROUPS = 8
TOKENS = 7168


def draw_segments(key, part):
    key_fill = jax.random.fold_in(key, 101)
    key_pick = jax.random.fold_in(key, 202)
    key_cuts = jax.random.fold_in(key, 303)
    filled = jax.random.randint(key_fill, (GROUPS,), GROUP_TOK // 2, GROUP_TOK + 1)
    chosen = jax.random.randint(key_pick, (), 0, GROUPS)
    groups_at = jnp.arange(GROUPS, dtype=jnp.int32)
    filled = jnp.where(groups_at == chosen, GROUP_TOK, filled)
    filled = jnp.where(groups_at == (chosen + 1) % GROUPS, GROUP_TOK // 2, filled)
    borders = jax.random.randint(key_cuts, (GROUPS, 3), 1, GROUP_TOK)
    borders = jnp.where((groups_at == chosen)[:, None], GROUP_TOK, borders)
    fixed_cuts = jnp.array([GROUP_TOK // 8, GROUP_TOK // 4, 3 * GROUP_TOK // 8], dtype=jnp.int32)
    borders = jnp.where((groups_at == (chosen + 2) % GROUPS)[:, None], fixed_cuts[None, :], borders)
    places = jnp.arange(GROUP_TOK, dtype=jnp.int32)
    labels = jnp.sum((borders[:, None, :] <= places[None, :, None]).astype(jnp.int32), axis=-1)
    labels = jnp.where(places[None, :] < filled[:, None], labels, -1)
    return labels.reshape(GROUPS * GROUP_TOK).astype(jnp.int32)


def block_scale(own_key, extent, split, least, top_value):
    def one(dim, shards_of):
        draws = jax.random.uniform(jax.random.fold_in(jax.random.fold_in(own_key, 6), dim), (shards_of,), jnp.float32, least / len(split), top_value / len(split))
        return jnp.repeat(jnp.exp(draws), extent[dim] // shards_of).reshape((-1,) + (1,) * (len(extent) - dim - 1))

    factor_of = one(*split[0])
    for cut in split[1:]:
        factor_of = factor_of * one(*cut)
    return factor_of


def normal_values(key, extent, width, limit, shards=(), kind=jnp.bfloat16):
    entries = jax.random.normal(key, extent, jnp.float32) * width
    if len(shards) > 0:
        entries = block_scale(key, extent, shards, -0.22, 0.18) * entries
    return jnp.clip(entries, min=-limit, max=limit).astype(kind)


def setup_inputs(seed: int = 0) -> dict:
    keys = jax.random.split(jax.random.key(seed), 22)
    return {
        "tokens": normal_values(keys[0], (TOKENS, D), 1.0, 6.0, ((0, 8),)),
        "segments": draw_segments(jax.random.fold_in(keys[21], 71), 0),
        "cotangent": normal_values(keys[2], (TOKENS, D), 1.0, 6.0, ((0, 8),)),
        "query_weight": normal_values(keys[3], (D, HEADS * HEAD_DIM), (D // 3) ** -0.5, 0.21875, ((0, 8), (1, 4)), jnp.float32),
        "keyval_weight": normal_values(keys[4], (2, D, KV_HEADS * HEAD_DIM), (D // 3) ** -0.5, 0.21875, ((1, 8), (2, 4)), jnp.float32),
        "output_weight": normal_values(keys[5], (HEADS * HEAD_DIM, D), (HEADS * HEAD_DIM) ** -0.5, 0.125, ((0, 4), (1, 8)), jnp.float32),
        "gateup_weight": normal_values(keys[6], (2, D, FF), D ** -0.5, 0.125, ((1, 8), (2, 4)), jnp.float32),
        "down_weight": normal_values(keys[7], (FF, D), FF ** -0.5, 0.0625, ((0, 4), (1, 8)), jnp.float32),
        "norm_gains": jnp.clip(jax.random.uniform(keys[8], (4, D), jnp.float32, -0.5, 0.5) * block_scale(keys[8], (4, D), ((1, 8),), -0.4, 0.0), -0.5, 0.5),
        "moment_query": normal_values(keys[9], (D, HEADS * HEAD_DIM), 3.0, 18.0, ((0, 8), (1, 4)), jnp.float32),
        "moment_keyval": normal_values(keys[10], (2, D, KV_HEADS * HEAD_DIM), 3.0, 18.0, ((1, 8), (2, 4)), jnp.float32),
        "moment_output": normal_values(keys[11], (HEADS * HEAD_DIM, D), 3.0, 18.0, ((0, 4), (1, 8)), jnp.float32),
        "moment_gateup": normal_values(keys[12], (2, D, FF), 3.0, 18.0, ((1, 8), (2, 4)), jnp.float32),
        "moment_down": normal_values(keys[13], (FF, D), 3.0, 18.0, ((0, 4), (1, 8)), jnp.float32),
        "moment_gains": normal_values(keys[14], (4, D), 3.0, 18.0, ((1, 8),), jnp.float32),
        "square_query": jnp.clip(jnp.exp(math.log(3000.0) - 5.7037825 * jax.random.uniform(keys[15], (D, HEADS * HEAD_DIM), jnp.float32) ** block_scale(keys[15], (D, HEADS * HEAD_DIM), ((0, 8), (1, 4)), -0.2, 0.2)), 10.0, 3000.0),
        "square_keyval": jnp.clip(jnp.exp(math.log(3000.0) - 5.7037825 * jax.random.uniform(keys[16], (2, D, KV_HEADS * HEAD_DIM), jnp.float32) ** block_scale(keys[16], (2, D, KV_HEADS * HEAD_DIM), ((1, 8), (2, 4)), -0.2, 0.2)), 10.0, 3000.0),
        "square_output": jnp.clip(jnp.exp(math.log(3000.0) - 5.7037825 * jax.random.uniform(keys[17], (HEADS * HEAD_DIM, D), jnp.float32) ** block_scale(keys[17], (HEADS * HEAD_DIM, D), ((0, 4), (1, 8)), -0.2, 0.2)), 10.0, 3000.0),
        "square_gateup": jnp.clip(jnp.exp(math.log(3000.0) - 5.7037825 * jax.random.uniform(keys[18], (2, D, FF), jnp.float32) ** block_scale(keys[18], (2, D, FF), ((1, 8), (2, 4)), -0.2, 0.2)), 10.0, 3000.0),
        "square_down": jnp.clip(jnp.exp(math.log(3000.0) - 5.7037825 * jax.random.uniform(keys[19], (FF, D), jnp.float32) ** block_scale(keys[19], (FF, D), ((0, 4), (1, 8)), -0.2, 0.2)), 10.0, 3000.0),
        "square_gains": jnp.clip(jnp.exp(math.log(3000.0) - 5.7037825 * jax.random.uniform(keys[20], (4, D), jnp.float32) ** block_scale(keys[20], (4, D), ((1, 8),), -0.2, 0.2)), 10.0, 3000.0),
    }


@jax.custom_vjp
def low(v):
    return lax.optimization_barrier(v.astype(jnp.bfloat16)).astype(jnp.float32)

@jax.custom_vjp
def low_back(v):
    return v

def low_keep(v):
    return (low(v), None)

def low_pass(kept, grad):
    return (grad,)

def back_keep(v):
    return (v, None)

def back_low(kept, grad):
    return (low(grad),)
low.defvjp(low_keep, low_pass)
low_back.defvjp(back_keep, back_low)
HIGH = lax.Precision.HIGHEST
norm_eps = 1e-06
cap_value = 50.0
rope_base = 10000.0
learn_rate = 0.1
beta_one = 0.9
beta_two = 0.95
adam_eps = 1e-08
decay_rate = 0.1

def rms_norm(tensor, gain_vec):
    factor = lax.rsqrt(lax.optimization_barrier(jnp.mean(tensor * tensor, axis=-1, keepdims=True)) + norm_eps)
    return tensor * factor * (1.0 + gain_vec)

def rotate(tensor, cosine, sine):
    half_dim = tensor.shape[-1] // 2
    first = tensor[..., :half_dim]
    second = tensor[..., half_dim:]
    return jnp.concatenate([first * cosine - second * sine, second * cosine + first * sine], axis=-1)

def layout(labels):
    length = labels.shape[0]
    places = jnp.arange(length, dtype=jnp.int32)
    same_seq = labels[:, None] == labels[None, :]
    earlier = places[None, :] < places[:, None]
    position = lax.optimization_barrier(jnp.sum((same_seq & earlier).astype(jnp.int32), axis=1))
    allowed = same_seq & (places[None, :] <= places[:, None]) & (places[:, None] - places[None, :] < WINDOW)
    half_dim = HEAD_DIM // 2
    freq = rope_base ** (-2.0 * jnp.arange(half_dim, dtype=jnp.float32) / HEAD_DIM)
    angle = position.astype(jnp.float32)[:, None] * freq[None, :]
    return (allowed, jnp.cos(angle)[:, None, :], jnp.sin(angle)[:, None, :])

def forward(inputs, wq_full, wkv_full, wo_full, wgu_full, wdn_full, gain_all, allowed, cosine, sine):
    length = inputs.shape[0]
    group = HEADS // KV_HEADS
    normed = low(rms_norm(inputs, gain_all[0]))
    qraw = low_back(jnp.dot(normed, wq_full, precision=HIGH)).reshape(length, HEADS, HEAD_DIM)
    queries = low(rotate(qraw, cosine, sine) * HEAD_DIM ** (-0.5)).reshape(length, KV_HEADS, group, HEAD_DIM)
    kraw = low_back(jnp.dot(normed, wkv_full[0], precision=HIGH)).reshape(length, KV_HEADS, HEAD_DIM)
    key_rows = low(rotate(kraw, cosine, sine))
    value_rows = low(low_back(jnp.dot(normed, wkv_full[1], precision=HIGH))).reshape(length, KV_HEADS, HEAD_DIM)
    raw_scores = low_back(jnp.einsum('qkgd,skd->kgqs', queries, key_rows, precision=HIGH))
    capped = cap_value * jnp.tanh(raw_scores / cap_value)
    capped = jnp.where(allowed[None, None], capped, -1e+30)
    probs = low(jax.nn.softmax(capped, axis=-1))
    mixed_out = low(low_back(jnp.einsum('kgqs,skd->qkgd', probs, value_rows, precision=HIGH)))
    mixed_out = mixed_out.reshape(length, HEADS * HEAD_DIM)
    attn_sum = low_back(jnp.dot(mixed_out, wo_full, precision=HIGH))
    residual = inputs + rms_norm(attn_sum, gain_all[1])
    hidden_in = low(rms_norm(residual, gain_all[2]))
    gate_out = low_back(jnp.dot(hidden_in, wgu_full[0], precision=HIGH))
    up_out = low_back(jnp.dot(hidden_in, wgu_full[1], precision=HIGH))
    act_low = low(jax.nn.gelu(gate_out, approximate=True) * up_out)
    ffn_sum = low_back(jnp.dot(act_low, wdn_full, precision=HIGH))
    return residual + rms_norm(ffn_sum, gain_all[3])

def adam_step(master, gradient, moment, square, steps_done):
    new_moment = beta_one * moment + (1.0 - beta_one) * gradient
    new_square = beta_two * square + (1.0 - beta_two) * gradient * gradient
    fix_one = 1.0 - beta_one ** steps_done
    fix_two = 1.0 - beta_two ** steps_done
    stride = new_moment / fix_one / (jnp.sqrt(new_square / fix_two) + adam_eps)
    return (-learn_rate * (stride + decay_rate * master), new_moment, new_square)

def reference(tokens, segments, cotangent, query_weight, keyval_weight, output_weight, gateup_weight, down_weight, norm_gains, moment_query, moment_keyval, moment_output, moment_gateup, moment_down, moment_gains, square_query, square_keyval, square_output, square_gateup, square_down, square_gains):
    masters = (query_weight, keyval_weight, output_weight, gateup_weight, down_weight, norm_gains)
    moments = (moment_query, moment_keyval, moment_output, moment_gateup, moment_down, moment_gains)
    squares = (square_query, square_keyval, square_output, square_gateup, square_down, square_gains)
    weights = tuple((low(master) for master in masters))
    tok_blocks = tokens.reshape(GROUPS, GROUP_TOK, D)
    seg_blocks = segments.reshape(GROUPS, GROUP_TOK)
    cot_blocks = cotangent.reshape(GROUPS, GROUP_TOK, D)

    def one_group(totals, block):
        tok_block, seg_block, cot_block = block
        allowed, cosine, sine = layout(seg_block)

        def run(inputs, wq_full, wkv_full, wo_full, wgu_full, wdn_full, gain_all):
            return forward(inputs, wq_full, wkv_full, wo_full, wgu_full, wdn_full, gain_all, allowed, cosine, sine)
        result, pull = jax.vjp(run, tok_block.astype(jnp.float32), *weights)
        valid = (seg_block >= 0).astype(jnp.float32)[:, None]
        grads = pull(cot_block.astype(jnp.float32) * valid)
        totals = tuple((total + grad for total, grad in zip(totals, grads[1:])))
        return (totals, (result.astype(jnp.bfloat16), grads[0]))
    zeros = tuple((jnp.zeros(weight.shape, jnp.float32) for weight in weights))
    totals, (results, input_grads) = lax.scan(one_group, zeros, (tok_blocks, seg_blocks, cot_blocks))
    steps_done = float(ADAM_STEP)
    updates = [adam_step(master, total, moment, square, steps_done) for master, total, moment, square in zip(masters, totals, moments, squares)]
    block_out = results.reshape(TOKENS, D)
    input_grad = input_grads.reshape(TOKENS, D)
    return (block_out, input_grad, totals[0], totals[1], totals[2], totals[3], totals[4], totals[5], updates[0][0], updates[1][0], updates[2][0], updates[3][0], updates[4][0], updates[5][0], updates[0][1], updates[1][1], updates[2][1], updates[3][1], updates[4][1], updates[5][1], updates[0][2], updates[1][2], updates[2][2], updates[3][2], updates[4][2], updates[5][2])
```

```python
import jax
import jax.numpy as jnp
from jax import lax
from jax.sharding import PartitionSpec as P

HEADS = 8
KV_HEADS = 4
HEAD_DIM = 256
WINDOW = 4096
ADAM_STEP = 5


norm_eps = 1e-06
cap_value = 50.0
rope_base = 10000.0
learn_rate = 0.1
beta_one = 0.9
beta_two = 0.95
adam_eps = 1e-08
decay_rate = 0.1


def rms_norm(tensor, gain_vec):
    factor = lax.rsqrt(jnp.mean(tensor * tensor, axis=-1, keepdims=True) + norm_eps)
    return tensor * factor * (1.0 + gain_vec)


def rotate(tensor, cosine, sine):
    half_dim = tensor.shape[-1] // 2
    first = tensor[..., :half_dim]
    second = tensor[..., half_dim:]
    return jnp.concatenate(
        [first * cosine - second * sine, second * cosine + first * sine], axis=-1
    )


def layout(labels):
    length = labels.shape[0]
    places = jnp.arange(length, dtype=jnp.int32)
    same_seq = labels[:, None] == labels[None, :]
    earlier = places[None, :] < places[:, None]
    position = jnp.sum((same_seq & earlier).astype(jnp.int32), axis=1)
    allowed = (
        same_seq
        & (places[None, :] <= places[:, None])
        & (places[:, None] - places[None, :] < WINDOW)
    )
    half_dim = HEAD_DIM // 2
    freq = rope_base ** (-2.0 * jnp.arange(half_dim, dtype=jnp.float32) / HEAD_DIM)
    angle = position.astype(jnp.float32)[:, None] * freq[None, :]
    return (allowed, jnp.cos(angle)[:, None, :], jnp.sin(angle)[:, None, :])


def scores(queries, key_rows, allowed):
    raw_scores = jnp.einsum("qkgd,skd->kgqs", queries, key_rows, preferred_element_type=jnp.float32)
    squashed = jnp.tanh(raw_scores / cap_value)
    capped = jnp.where(allowed[None, None], cap_value * squashed, -1e30)
    return (squashed, capped)


def norm_back(tensor, gain_vec, grad_in):
    unused, pull = jax.vjp(rms_norm, tensor, gain_vec)
    return pull(grad_in)


def rotate_back(grad_in, cosine, sine, shape_like):
    unused, pull = jax.vjp(lambda tensor: rotate(tensor, cosine, sine), shape_like)
    return pull(grad_in)[0]


def adam_step(master, gradient, moment, square, steps_done):
    new_moment = beta_one * moment + (1.0 - beta_one) * gradient
    new_square = beta_two * square + (1.0 - beta_two) * gradient * gradient
    fix_one = 1.0 - beta_one**steps_done
    fix_two = 1.0 - beta_two**steps_done
    stride = new_moment / fix_one / (jnp.sqrt(new_square / fix_two) + adam_eps)
    return (-learn_rate * (stride + decay_rate * master), new_moment, new_square)


def ring_pairs(extent):
    outer = extent // 2
    return [
        (2 * place + side, 2 * ((place + 1) % outer) + side)
        for place in range(outer)
        for side in range(2)
    ]


def swap_pairs(extent, stride):
    return [(place, place ^ stride) for place in range(extent)]


def rows_at(tensor, index, count):
    return lax.dynamic_slice_in_dim(tensor, index * count, count, 0)


def gather_rows(own, extent):
    if extent % 2:
        return lax.all_gather(own, "dp", axis=0, tiled=True)
    outer = extent // 2
    index = lax.axis_index("dp")
    place, side = index // 2, index % 2
    count = own.shape[0]
    ring, swap = ring_pairs(extent), swap_pairs(extent, 1)
    full = jnp.zeros((extent * count,) + own.shape[1:], own.dtype)
    held = own
    for step in range(outer):
        if step:
            held = lax.ppermute(held, "dp", ring)
        other = lax.ppermute(held, "dp", swap)
        source = 2 * lax.rem(place - step + outer, outer)
        full = lax.dynamic_update_slice_in_dim(full, held, (source + side) * count, 0)
        full = lax.dynamic_update_slice_in_dim(full, other, (source + 1 - side) * count, 0)
    return full


def scatter_rows(partial, extent):
    if extent % 2:
        return lax.psum_scatter(
            partial.astype(jnp.float32), "dp", scatter_dimension=0, tiled=True
        )
    outer = extent // 2
    index = lax.axis_index("dp")
    place, side = index // 2, index % 2
    count = partial.shape[0] // extent
    ring, swap = ring_pairs(extent), swap_pairs(extent, 1)
    total = None
    for hops in range(outer - 1, -1, -1):
        target = 2 * lax.rem(place + hops, outer)
        other = lax.ppermute(rows_at(partial, target + 1 - side, count), "dp", swap)
        both = rows_at(partial, target + side, count).astype(jnp.float32) + other.astype(jnp.float32)
        if total is not None:
            both = both + lax.ppermute(total, "dp", ring).astype(jnp.float32)
        total = both.astype(partial.dtype) if hops else both
    return total


def sum_heads(partial, extent):
    if extent != 4:
        return lax.psum(partial, "mp")
    half = partial.shape[0] // 2
    side = lax.rem(lax.axis_index("mp"), 2)
    given = rows_at(partial, 1 - side, half).astype(jnp.bfloat16)
    kept = rows_at(partial, side, half)
    kept = kept + lax.ppermute(given, "mp", swap_pairs(4, 1)).astype(jnp.float32)
    kept = kept.astype(jnp.bfloat16)
    far = lax.ppermute(kept, "mp", swap_pairs(4, 2))
    mine = (kept.astype(jnp.float32) + far.astype(jnp.float32)).astype(jnp.bfloat16)
    theirs = lax.ppermute(mine, "mp", swap_pairs(4, 1))
    first = jnp.where(side == 0, mine, theirs)
    second = jnp.where(side == 0, theirs, mine)
    return jnp.concatenate([first, second], axis=0).astype(jnp.float32)


def shards(
    tokens,
    segments,
    cotangent,
    query_weight,
    keyval_weight,
    output_weight,
    gateup_weight,
    down_weight,
    norm_gains,
    moment_query,
    moment_keyval,
    moment_output,
    moment_gateup,
    moment_down,
    moment_gains,
    square_query,
    square_keyval,
    square_output,
    square_gateup,
    square_down,
    square_gains,
):
    masters = (query_weight, keyval_weight, output_weight, gateup_weight, down_weight, norm_gains)
    low = jnp.bfloat16
    groups, parts = lax.axis_size("dp"), lax.axis_size("mp")
    gain_low = gather_rows(norm_gains.astype(low).T, groups).T
    mixer = jnp.concatenate(
        [
            query_weight.astype(low),
            keyval_weight[0].astype(low),
            keyval_weight[1].astype(low),
            output_weight.astype(low).T,
        ],
        axis=1,
    )
    mixer = gather_rows(mixer, groups)
    width_q, width_kv = query_weight.shape[1], keyval_weight.shape[2]
    wqkv_local = mixer[:, : width_q + 2 * width_kv]
    wo_turned = mixer[:, width_q + 2 * width_kv :]
    wg_local = gather_rows(gateup_weight[0].astype(low), groups)
    wu_local = gather_rows(gateup_weight[1].astype(low), groups)
    wdn_turned = gather_rows(down_weight.astype(low).T, groups)
    gain_all = gain_low.astype(jnp.float32)
    length = tokens.shape[0]
    group = HEADS // KV_HEADS
    kv_local = width_kv // HEAD_DIM
    heads_local = kv_local * group
    qscale = HEAD_DIM ** (-0.5)
    allowed, cosine, sine = layout(segments)
    valid = (segments >= 0).astype(jnp.float32)[:, None]
    inputs = tokens.astype(jnp.float32)
    normed = rms_norm(inputs, gain_all[0])
    normed_low = normed.astype(jnp.bfloat16)
    mixer_raw = jnp.dot(normed_low, wqkv_local, preferred_element_type=jnp.float32)
    qraw = mixer_raw[:, :width_q].reshape(length, heads_local, HEAD_DIM)
    queries = (
        (rotate(qraw, cosine, sine) * qscale)
        .astype(jnp.bfloat16)
        .reshape(length, kv_local, group, HEAD_DIM)
    )
    kraw = mixer_raw[:, width_q : width_q + width_kv].reshape(length, kv_local, HEAD_DIM)
    key_rows = rotate(kraw, cosine, sine).astype(jnp.bfloat16)
    value_rows = (
        mixer_raw[:, width_q + width_kv :]
        .astype(jnp.bfloat16)
        .reshape(length, kv_local, HEAD_DIM)
    )
    squashed, capped = scores(queries, key_rows, allowed)
    row_top = jnp.max(capped, axis=-1, keepdims=True)
    log_total = row_top + jnp.log(jnp.sum(jnp.exp(capped - row_top), axis=-1, keepdims=True))
    probs_low = jnp.exp(capped - log_total).astype(jnp.bfloat16)
    mixed_low = jnp.einsum(
        "kgqs,skd->qkgd", probs_low, value_rows, preferred_element_type=jnp.float32
    ).astype(jnp.bfloat16)
    mixed_low = mixed_low.reshape(length, heads_local * HEAD_DIM)
    attn_part = jnp.einsum("te,de->td", mixed_low, wo_turned, preferred_element_type=jnp.float32)
    attn_sum = sum_heads(attn_part, parts)
    residual = inputs + rms_norm(attn_sum, gain_all[1])
    hidden_in = rms_norm(residual, gain_all[2]).astype(jnp.bfloat16)
    gate_out = jnp.dot(hidden_in, wg_local, preferred_element_type=jnp.float32)
    up_out = jnp.dot(hidden_in, wu_local, preferred_element_type=jnp.float32)
    act_low = (jax.nn.gelu(gate_out, approximate=True) * up_out).astype(jnp.bfloat16)
    ffn_part = jnp.einsum("tf,df->td", act_low, wdn_turned, preferred_element_type=jnp.float32)
    ffn_sum = sum_heads(ffn_part, parts)
    block_out = (residual + rms_norm(ffn_sum, gain_all[3])).astype(jnp.bfloat16)
    grad_out = cotangent.astype(jnp.float32) * valid
    grad_ffn, grad_gain3 = norm_back(ffn_sum, gain_all[3], grad_out)
    grad_ffn_low = grad_ffn.astype(jnp.bfloat16)
    grad_wdn = jnp.einsum("td,tf->df", grad_ffn_low, act_low, preferred_element_type=jnp.float32).astype(low)
    grad_act = jnp.einsum("td,df->tf", grad_ffn_low, wdn_turned, preferred_element_type=jnp.float32)
    unused, pull_act = jax.vjp(
        lambda gate_in, up_in: jax.nn.gelu(gate_in, approximate=True) * up_in, gate_out, up_out
    )
    grad_gate, grad_up = pull_act(grad_act)
    grad_gate = grad_gate.astype(jnp.bfloat16)
    grad_up = grad_up.astype(jnp.bfloat16)
    grad_wg = jnp.einsum("td,tf->df", hidden_in, grad_gate, preferred_element_type=jnp.float32).astype(low)
    grad_wu = jnp.einsum("td,tf->df", hidden_in, grad_up, preferred_element_type=jnp.float32).astype(low)
    hidden_part = jnp.einsum(
        "tf,df->td", grad_gate, wg_local, preferred_element_type=jnp.float32
    )
    hidden_part = hidden_part + jnp.einsum(
        "tf,df->td", grad_up, wu_local, preferred_element_type=jnp.float32
    )
    grad_hidden = sum_heads(hidden_part, parts)
    grad_resid_n, grad_gain2 = norm_back(residual, gain_all[2], grad_hidden)
    grad_resid = grad_out + grad_resid_n
    grad_attn, grad_gain1 = norm_back(attn_sum, gain_all[1], grad_resid)
    grad_attn_low = grad_attn.astype(jnp.bfloat16)
    grad_wo = jnp.einsum("td,te->de", grad_attn_low, mixed_low, preferred_element_type=jnp.float32).astype(low)
    grad_mixed = jnp.einsum(
        "td,de->te", grad_attn_low, wo_turned, preferred_element_type=jnp.float32
    )
    grad_mixed = grad_mixed.astype(jnp.bfloat16).reshape(length, kv_local, group, HEAD_DIM)
    squashed, capped = scores(queries, key_rows, allowed)
    probs = jnp.exp(capped - log_total)
    probs_low = probs.astype(jnp.bfloat16)
    grad_probs = jnp.einsum(
        "qkgd,skd->kgqs", grad_mixed, value_rows, preferred_element_type=jnp.float32
    )
    grad_value = jnp.einsum(
        "kgqs,qkgd->skd", probs_low, grad_mixed, preferred_element_type=jnp.float32
    )
    grad_value = grad_value.astype(jnp.bfloat16).reshape(length, kv_local * HEAD_DIM)
    grad_capped = probs * (grad_probs - jnp.sum(probs * grad_probs, axis=-1, keepdims=True))
    grad_scores = (grad_capped * (1.0 - squashed * squashed)).astype(jnp.bfloat16)
    grad_query = jnp.einsum(
        "kgqs,skd->qkgd", grad_scores, key_rows, preferred_element_type=jnp.float32
    )
    grad_query = grad_query.reshape(length, heads_local, HEAD_DIM) * qscale
    grad_qraw = (
        rotate_back(grad_query, cosine, sine, qraw)
        .astype(jnp.bfloat16)
        .reshape(length, heads_local * HEAD_DIM)
    )
    grad_key = jnp.einsum(
        "kgqs,qkgd->skd", grad_scores, queries, preferred_element_type=jnp.float32
    )
    grad_kraw = (
        rotate_back(grad_key, cosine, sine, kraw)
        .astype(jnp.bfloat16)
        .reshape(length, kv_local * HEAD_DIM)
    )
    grad_mixer_raw = jnp.concatenate([grad_qraw, grad_kraw, grad_value], axis=1)
    grad_wqkv = jnp.einsum("td,te->de", normed_low, grad_mixer_raw, preferred_element_type=jnp.float32).astype(low)
    normed_part = jnp.einsum(
        "te,de->td", grad_mixer_raw, wqkv_local, preferred_element_type=jnp.float32
    )
    grad_normed = sum_heads(normed_part, parts)
    grad_inputs_n, grad_gain0 = norm_back(inputs, gain_all[0], grad_normed)
    input_grad = grad_resid + grad_inputs_n
    grad_gains = jnp.stack([grad_gain0, grad_gain1, grad_gain2, grad_gain3])
    sum_wdn = scatter_rows(grad_wdn, groups).T
    sum_wgu = jnp.stack([scatter_rows(grad_wg, groups), scatter_rows(grad_wu, groups)])
    sum_wo = scatter_rows(grad_wo, groups).T
    sum_wqkv = scatter_rows(grad_wqkv, groups)
    sum_wq = sum_wqkv[:, :width_q]
    sum_wkv = jnp.stack([sum_wqkv[:, width_q : width_q + width_kv], sum_wqkv[:, width_q + width_kv :]])
    sum_gains = scatter_rows(grad_gains.T, groups).T
    totals = (sum_wq, sum_wkv, sum_wo, sum_wgu, sum_wdn, sum_gains)
    moments = (moment_query, moment_keyval, moment_output, moment_gateup, moment_down, moment_gains)
    squares = (square_query, square_keyval, square_output, square_gateup, square_down, square_gains)
    steps_done = float(ADAM_STEP)
    updates = [
        adam_step(master, total, moment, square, steps_done)
        for master, total, moment, square in zip(masters, totals, moments, squares)
    ]
    return (
        block_out,
        input_grad,
        totals[0],
        totals[1],
        totals[2],
        totals[3],
        totals[4],
        totals[5],
        updates[0][0],
        updates[1][0],
        updates[2][0],
        updates[3][0],
        updates[4][0],
        updates[5][0],
        updates[0][1],
        updates[1][1],
        updates[2][1],
        updates[3][1],
        updates[4][1],
        updates[5][1],
        updates[0][2],
        updates[1][2],
        updates[2][2],
        updates[3][2],
        updates[4][2],
        updates[5][2],
    )


def solution(mesh):
    return jax.shard_map(
        shards,
        mesh=mesh,
        in_specs=(
            P("dp", None),
            P("dp"),
            P("dp", None),
            P("dp", "mp"),
            P(None, "dp", "mp"),
            P("mp", "dp"),
            P(None, "dp", "mp"),
            P("mp", "dp"),
            P(None, "dp"),
            P("dp", "mp"),
            P(None, "dp", "mp"),
            P("mp", "dp"),
            P(None, "dp", "mp"),
            P("mp", "dp"),
            P(None, "dp"),
            P("dp", "mp"),
            P(None, "dp", "mp"),
            P("mp", "dp"),
            P(None, "dp", "mp"),
            P("mp", "dp"),
            P(None, "dp"),
        ),
        out_specs=(
            P("dp", None),
            P("dp", None),
            P("dp", "mp"),
            P(None, "dp", "mp"),
            P("mp", "dp"),
            P(None, "dp", "mp"),
            P("mp", "dp"),
            P(None, "dp"),
            P("dp", "mp"),
            P(None, "dp", "mp"),
            P("mp", "dp"),
            P(None, "dp", "mp"),
            P("mp", "dp"),
            P(None, "dp"),
            P("dp", "mp"),
            P(None, "dp", "mp"),
            P("mp", "dp"),
            P(None, "dp", "mp"),
            P("mp", "dp"),
            P(None, "dp"),
            P("dp", "mp"),
            P(None, "dp", "mp"),
            P("mp", "dp"),
            P(None, "dp", "mp"),
            P("mp", "dp"),
            P(None, "dp"),
        ),
        check_vma=False,
    )
```

```python
from functools import partial

import jax
import jax.numpy as jnp
from jax import lax
from jax.experimental import pallas as pl
from jax.experimental.layout import Layout, with_layout_constraint
from jax.experimental.pallas import tpu as pltpu
from jax.sharding import PartitionSpec as P

HEADS = 8
KV_HEADS = 4
HEAD_DIM = 256
WINDOW = 4096
ADAM_STEP = 5


norm_eps = 1e-06
cap_value = 50.0
rope_base = 10000.0
learn_rate = 0.1
beta_one = 0.9
beta_two = 0.95
adam_eps = 1e-08
decay_rate = 0.1


low = jnp.bfloat16
wide = jnp.float32


def tie(tensor, *others):
    return lax.optimization_barrier((tensor,) + others)[0]


def plain(tensor):
    return with_layout_constraint(tensor, Layout(tuple(range(tensor.ndim))))


def ring_pairs(extent, hops=1):
    outer = extent // 2
    return [
        (2 * place + side, 2 * ((place + hops) % outer) + side)
        for place in range(outer)
        for side in range(2)
    ]


def swap_pairs(extent, stride):
    return [(place, place ^ stride) for place in range(extent)]


def rows_at(tensor, index, count):
    return lax.dynamic_slice_in_dim(tensor, index * count, count, 0)


def add(first, second, kind=low):
    return (first.astype(wide) + second.astype(wide)).astype(kind)


BLOCK = 64


def by_rows(body, side, rows, whole, outs, sums):
    length = rows[0].shape[0]

    def blocked(width):
        return pl.BlockSpec((BLOCK, width), lambda i: (i, 0))

    def kept(shape):
        return pl.BlockSpec(shape, lambda i: (0, 0))

    return pl.pallas_call(
        body,
        grid=(length // BLOCK,),
        in_specs=[pl.BlockSpec(memory_space=pltpu.SMEM)]
        + [blocked(t.shape[1]) for t in rows]
        + [kept(t.shape) for t in whole],
        out_specs=[blocked(width) for width, kind in outs] + [kept((1, width)) for width in sums],
        out_shape=[jax.ShapeDtypeStruct((length, width), kind) for width, kind in outs]
        + [jax.ShapeDtypeStruct((1, width), wide) for width in sums],
        compiler_params=pltpu.CompilerParams(vmem_limit_bytes=48 * 1024 * 1024),
    )(side, *rows, *whole)


def factor_of(value):
    return lax.rsqrt(jnp.mean(value * value, axis=-1, keepdims=True) + norm_eps)


def back_of(value, factor, gain, grad):
    scaled = grad * (1.0 + gain)
    shared = factor * factor * jnp.mean(scaled * value, axis=-1, keepdims=True)
    return factor * (scaled - shared * value), grad * (value * factor)


def add_up(ref, value):
    @pl.when(pl.program_id(0) == 0)
    def start():
        ref[...] = jnp.zeros_like(ref)

    ref[...] += jnp.sum(value, axis=0, keepdims=True)


def pieces_of(value, groups):
    count = value.shape[1] // groups
    return [value[:, k * count : (k + 1) * count] for k in range(groups)]


def turn(value, side, groups):
    cut = pieces_of(value, groups)
    even, odd = jnp.concatenate(cut[0::2], axis=1), jnp.concatenate(cut[1::2], axis=1)
    first, second = jnp.where(side == 0, even, odd), jnp.where(side == 0, odd, even)
    return jnp.concatenate([first, second], axis=1)


def straighten(value, side, groups):
    half = value.shape[1] // 2
    own, peer = value[:, :half], value[:, half:]
    even, odd = jnp.where(side == 0, own, peer), jnp.where(side == 0, peer, own)
    woven = zip(pieces_of(even, groups // 2), pieces_of(odd, groups // 2))
    return jnp.concatenate([cut for pair in woven for cut in pair], axis=1)


def start_body(groups, side, tokens, cotangent, valid, inputs, grad_out):
    inputs[...] = turn(tokens[...].astype(wide), side[0], groups).astype(low)
    grad_out[...] = turn(cotangent[...].astype(wide) * valid[...], side[0], groups).astype(low)


def normed_body(side, inputs, gains, normed):
    value = inputs[...].astype(wide)
    normed[...] = (value * factor_of(value) * (1.0 + gains[0:1])).astype(low)


def residual_of(inputs, attn, gains):
    value, mixed = inputs[...].astype(wide), attn[...].astype(wide)
    factor = factor_of(mixed)
    return value + mixed * factor * (1.0 + gains[1:2]), mixed, factor


def hidden_body(side, inputs, attn, gains, hidden):
    residual = residual_of(inputs, attn, gains)[0]
    hidden[...] = (residual * factor_of(residual) * (1.0 + gains[2:3])).astype(low)


def ffn_of(own, peer):
    return jnp.concatenate([own[...].astype(wide), peer[...].astype(wide)], axis=1)


def ffn_back_body(side, own, peer, grad_out, gains, grad_own, grad_peer, grad_gain):
    ffn = ffn_of(own, peer)
    grad, term = back_of(ffn, factor_of(ffn), gains[3:4], grad_out[...].astype(wide))
    half = ffn.shape[1] // 2
    grad_own[...] = grad[:, :half].astype(low)
    grad_peer[...] = grad[:, half:].astype(low)
    add_up(grad_gain, term)


def out_body(groups, side, inputs, attn, own, peer, gains, out):
    ffn = ffn_of(own, peer)
    value = residual_of(inputs, attn, gains)[0] + ffn * factor_of(ffn) * (1.0 + gains[3:4])
    out[...] = straighten(value, side[0], groups).astype(low)


def attn_back_body(side, inputs, attn, grad_hidden, grad_out, gains, grad_resid, grad_attn, gain1, gain2):
    residual, mixed, factor = residual_of(inputs, attn, gains)
    grad, term2 = back_of(residual, factor_of(residual), gains[2:3], grad_hidden[...].astype(wide))
    grad = grad + grad_out[...].astype(wide)
    grad_resid[...] = grad
    back, term1 = back_of(mixed, factor, gains[1:2], grad)
    grad_attn[...] = back.astype(low)
    add_up(gain1, term1)
    add_up(gain2, term2)


def in_back_body(groups, side, inputs, grad_normed, grad_resid, gains, input_grad, gain0):
    value = inputs[...].astype(wide)
    grad, term = back_of(value, factor_of(value), gains[0:1], grad_normed[...].astype(wide))
    input_grad[...] = straighten(grad_resid[...] + grad, side[0], groups)
    add_up(gain0, term)


def rotate(tensor, cosine, sine):
    half_dim = tensor.shape[-1] // 2
    first = tensor[..., :half_dim]
    second = tensor[..., half_dim:]
    return jnp.concatenate(
        [first * cosine - second * sine, second * cosine + first * sine], axis=-1
    )


def layout(labels):
    length = labels.shape[0]
    places = jnp.arange(length, dtype=jnp.int32)
    same_seq = labels[:, None] == labels[None, :]
    earlier = places[None, :] < places[:, None]
    position = jnp.sum((same_seq & earlier).astype(jnp.int32), axis=1)
    allowed = (
        same_seq
        & (places[None, :] <= places[:, None])
        & (places[:, None] - places[None, :] < WINDOW)
    )
    half_dim = HEAD_DIM // 2
    freq = rope_base ** (-2.0 * jnp.arange(half_dim, dtype=jnp.float32) / HEAD_DIM)
    angle = position.astype(jnp.float32)[:, None] * freq[None, :]
    return (allowed, jnp.cos(angle)[:, None, :], jnp.sin(angle)[:, None, :])


def scores(queries, key_rows, allowed):
    raw_scores = jnp.einsum("qkgd,skd->kgqs", queries, key_rows, preferred_element_type=jnp.float32)
    squashed = jnp.tanh(raw_scores / cap_value)
    capped = jnp.where(allowed[None, None], cap_value * squashed, -1e30)
    return (squashed, capped)


def rotate_back(grad_in, cosine, sine, shape_like):
    unused, pull = jax.vjp(lambda tensor: rotate(tensor, cosine, sine), shape_like)
    return pull(grad_in)[0]


def adam_step(master, gradient, moment, square, steps_done):
    new_moment = beta_one * moment + (1.0 - beta_one) * gradient
    new_square = beta_two * square + (1.0 - beta_two) * gradient * gradient
    fix_one = 1.0 - beta_one**steps_done
    fix_two = 1.0 - beta_two**steps_done
    stride = new_moment / fix_one / (jnp.sqrt(new_square / fix_two) + adam_eps)
    return (-learn_rate * (stride + decay_rate * master), new_moment, new_square)


def shards(
    tokens,
    segments,
    cotangent,
    query_weight,
    keyval_weight,
    output_weight,
    gateup_weight,
    down_weight,
    norm_gains,
    moment_query,
    moment_keyval,
    moment_output,
    moment_gateup,
    moment_down,
    moment_gains,
    square_query,
    square_keyval,
    square_output,
    square_gateup,
    square_down,
    square_gains,
):
    groups, parts = lax.axis_size("dp"), lax.axis_size("mp")
    outer = groups // 2
    index = lax.axis_index("dp")
    place = index // 2
    side = lax.rem(index, 2).astype(jnp.int32).reshape(1)
    length, features = tokens.shape
    half = features // 2
    count = features // groups
    group = HEADS // KV_HEADS
    width_q, width_kv = query_weight.shape[1], keyval_weight.shape[2]
    width_qkv = width_q + 2 * width_kv
    width_mixer = width_qkv + output_weight.shape[0]
    width_ff = down_weight.shape[0]
    kv_local = width_kv // HEAD_DIM
    heads_local = kv_local * group
    qscale = HEAD_DIM ** (-0.5)
    core = lax.rem(lax.axis_index("mp"), 2)
    paired = outer == 4 and parts == 4

    def dot(pattern, first, second):
        return jnp.einsum(pattern, first, second, preferred_element_type=wide)

    def around(tensor):
        return lax.ppermute(tensor, "dp", ring_pairs(groups))

    def swap(tensor):
        return lax.ppermute(tensor, "dp", swap_pairs(groups, 1))

    def near(tensor):
        return lax.ppermute(tensor, "mp", swap_pairs(parts, 1))

    def far(tensor):
        return lax.ppermute(tensor, "mp", swap_pairs(parts, 2))

    def apart(partial_sum):
        rows = length // 2
        return rows_at(partial_sum, 1 - core, rows), rows_at(partial_sum, core, rows)

    def together(mine, theirs):
        first = jnp.where(core == 0, mine, theirs)
        second = jnp.where(core == 0, theirs, mine)
        return jnp.concatenate([first, second], axis=0)

    allowed, cosine, sine = layout(segments)
    valid = (segments >= 0).astype(wide)[:, None]

    def projections(inputs, weights, gains):
        (normed_low,) = by_rows(normed_body, side, [inputs], [gains], [(features, low)], [])
        mixer_raw = dot("td,de->te", normed_low, weights[:, :width_qkv])
        qraw = mixer_raw[:, :width_q].reshape(length, heads_local, HEAD_DIM)
        kraw = mixer_raw[:, width_q : width_q + width_kv].reshape(length, kv_local, HEAD_DIM)
        queries = (
            (rotate(qraw, cosine, sine) * qscale).astype(low).reshape(length, kv_local, group, HEAD_DIM)
        )
        key_rows = rotate(kraw, cosine, sine).astype(low)
        value_rows = mixer_raw[:, width_q + width_kv :].astype(low).reshape(length, kv_local, HEAD_DIM)
        return normed_low, queries, key_rows, value_rows

    def attention(projected, weights):
        unused, queries, key_rows, value_rows = projected
        squashed, capped = scores(queries, key_rows, allowed)
        row_top = jnp.max(capped, axis=-1, keepdims=True)
        log_total = row_top + jnp.log(jnp.sum(jnp.exp(capped - row_top), axis=-1, keepdims=True))
        probs = jnp.exp(capped - log_total)
        probs_low = probs.astype(low)
        mixed_low = dot("kgqs,skd->qkgd", probs_low, value_rows).astype(low)
        mixed_low = mixed_low.reshape(length, heads_local * HEAD_DIM)
        attn_part = dot("te,de->td", mixed_low, weights[:, width_qkv:]).astype(low)
        return attn_part, projected + (squashed, probs, probs_low, mixed_low)

    def attention_back(grad_attn, weights, saved):
        normed_low, queries, key_rows, value_rows, squashed, probs, probs_low, mixed_low = saved
        grad_mixed = dot("td,de->te", grad_attn, weights[:, width_qkv:]).astype(low)
        grad_mixed = grad_mixed.reshape(length, kv_local, group, HEAD_DIM)
        grad_probs = dot("qkgd,skd->kgqs", grad_mixed, value_rows)
        grad_value = dot("kgqs,qkgd->skd", probs_low, grad_mixed)
        grad_value = grad_value.astype(low).reshape(length, kv_local * HEAD_DIM)
        grad_capped = probs * (grad_probs - jnp.sum(probs * grad_probs, axis=-1, keepdims=True))
        grad_scores = (grad_capped * (1.0 - squashed * squashed)).astype(low)
        grad_query = dot("kgqs,skd->qkgd", grad_scores, key_rows)
        grad_query = grad_query.reshape(length, heads_local, HEAD_DIM) * qscale
        shape_q = jnp.zeros((length, heads_local, HEAD_DIM), wide)
        grad_qraw = rotate_back(grad_query, cosine, sine, shape_q).astype(low)
        grad_key = dot("kgqs,qkgd->skd", grad_scores, queries)
        shape_k = jnp.zeros((length, kv_local, HEAD_DIM), wide)
        grad_kraw = rotate_back(grad_key, cosine, sine, shape_k).astype(low)
        flat = [t.reshape(length, -1) for t in (grad_qraw, grad_kraw, grad_value)]
        return plain(jnp.concatenate(flat, axis=1))

    def gated(gate_in, up_in):
        return jax.nn.gelu(gate_in, approximate=True) * up_in

    def weight_grad(first, second):
        return plain(dot("td,te->de", first, second).astype(low))

    def ffn_back(ffn_own, ffn_peer, grad_out, gains):
        return by_rows(
            ffn_back_body, side, [ffn_own, ffn_peer, grad_out], [gains], [(half, low)] * 2, [features]
        )

    def layer_out(inputs, attn_sum, ffn_own, ffn_peer, gains):
        rows = [inputs, attn_sum, ffn_own, ffn_peer]
        return by_rows(partial(out_body, groups), side, rows, [gains], [(features, low)], [])[0]

    def attn_back(inputs, attn_sum, grad_hidden, grad_out, gains):
        rows = [inputs, attn_sum, grad_hidden, grad_out]
        outs = [(features, wide), (features, low)]
        return by_rows(attn_back_body, side, rows, [gains], outs, [features] * 2)

    def in_back(inputs, grad_normed, grad_resid, gains):
        rows = [inputs, grad_normed, grad_resid]
        return by_rows(partial(in_back_body, groups), side, rows, [gains], [(features, wide)], [features])

    steps_done = float(ADAM_STEP)

    def updated(master, total, moment, square):
        return (total,) + adam_step(master, total, moment, square, steps_done)

    def update_gate_up(sums):
        return updated(gateup_weight, jnp.stack(sums), moment_gateup, square_gateup)

    def update_down(total):
        return updated(down_weight.T, total, moment_down.T, square_down.T)

    def update_mixer(total):
        total = plain(total)
        sum_k, sum_v = total[:, width_q : width_q + width_kv], total[:, width_q + width_kv : width_qkv]
        return (
            updated(query_weight, total[:, :width_q], moment_query, square_query),
            updated(keyval_weight, jnp.stack([sum_k, sum_v]), moment_keyval, square_keyval),
            updated(output_weight.T, total[:, width_qkv:], moment_output.T, square_output.T),
        )

    gain_row = norm_gains.astype(low).reshape(1, 4 * count)
    mixer = jnp.concatenate(
        [
            query_weight.astype(low),
            keyval_weight[0].astype(low),
            keyval_weight[1].astype(low),
            output_weight.astype(low).T,
        ],
        axis=1,
    )
    mixer = jnp.concatenate([mixer, jnp.pad(gain_row, ((0, 15), (0, width_mixer - 4 * count)))], axis=0)
    mixer = plain(mixer)

    def source(step):
        return lax.rem(place - step + outer, outer)

    def put(full, piece, step, offset=0):
        return lax.dynamic_update_slice_in_dim(full, piece, source(step) * count + offset, 0)

    def gains_of(held, peer):
        gain_low = jnp.zeros((2, outer, 4, count), low)
        for at, pieces in enumerate((held, peer)):
            for step, piece in enumerate(pieces):
                gain_piece = piece[count, : 4 * count].reshape(1, 1, 4, count)
                gain_low = lax.dynamic_update_slice(gain_low, gain_piece, (at, source(step), 0, 0))
        return jnp.moveaxis(gain_low.reshape(groups, 4, count), 1, 0).reshape(4, features).astype(wide)

    def start(tokens_in, cotangent_in):
        return by_rows(
            partial(start_body, groups), side, [tokens_in, cotangent_in, valid], [], [(features, low)] * 2, []
        )

    clock = [jnp.broadcast_to(valid[:8], (8, 128))]

    def sync(values):
        values, clock[0] = lax.optimization_barrier((values, clock[0]))
        return values

    always = index < groups

    def whole(work, *values):
        shapes = jax.eval_shape(work, *values)

        def blank(*unused):
            return jax.tree.map(lambda t: jnp.zeros(t.shape, t.dtype), shapes)

        return lax.cond(always, work, blank, *values)

    def behind(*values):
        values, clock[0] = lax.optimization_barrier((values, clock[0] * 0.5))
        return values

    gate, up = plain(gateup_weight[0].astype(low)), plain(gateup_weight[1].astype(low))
    down = plain(down_weight.astype(low).T)

    def down_part(act_low, weights):
        return dot("tf,df->td", act_low, weights).astype(low)

    def act_back(grad_own, grad_peer, gate_out, up_out, wd_own, wd_peer):
        grad_act = dot("td,df->tf", grad_own, wd_own) + dot("td,df->tf", grad_peer, wd_peer)
        unused, pull_act = jax.vjp(gated, gate_out, up_out)
        return tuple(grad.astype(low) for grad in pull_act(grad_act))

    def hidden_back(grad_gate, grad_up, wg, wu):
        return (dot("tf,df->td", grad_gate, wg) + dot("tf,df->td", grad_up, wu)).astype(low)

    def results(block_out, input_grad, new_mixer, new_gate_up, new_down, sum_gains):
        new_query, new_keyval, new_output = new_mixer
        new_gains = updated(norm_gains, sum_gains, moment_gains, square_gains)
        turned_back = [tuple(t.T for t in group_of) for group_of in (new_output, new_down)]
        new = (new_query, new_keyval, turned_back[0], new_gate_up, turned_back[1], new_gains)
        return (block_out, input_grad) + tuple(new[at][kind] for kind in range(4) for at in range(6))

    def simple():
        def gathered(own):
            rows = lax.all_gather(own, "dp", axis=0, tiled=True).reshape(outer, 2, -1, own.shape[1])
            return jnp.moveaxis(jnp.where(side == 0, rows, rows[:, ::-1]), 1, 0)

        def whole_rows(own):
            return gathered(own).reshape(features, own.shape[1])

        def scattered(rows):
            rows = rows.astype(wide).reshape(2, outer, count, rows.shape[1])
            rows = jnp.moveaxis(jnp.where(side == 0, rows, rows[::-1]), 0, 1).reshape(features, -1)
            return lax.psum_scatter(rows, "dp", scatter_dimension=0, tiled=True)

        def over_heads(part):
            return lax.psum(part.astype(wide), "mp").astype(low)

        rows = gathered(mixer)
        full = rows[:, :, :count].reshape(features, width_mixer)
        gains = jnp.moveaxis(rows[:, :, count, : 4 * count].reshape(groups, 4, count), 1, 0)
        gains = gains.reshape(4, features).astype(wide)
        wg, wu, wd = whole_rows(gate), whole_rows(up), whole_rows(down)
        inputs, grad_out = start(tokens, cotangent)
        attn_part, saved = attention(projections(inputs, full, gains), full)
        attn_sum = over_heads(attn_part)
        (hidden_in,) = by_rows(hidden_body, side, [inputs, attn_sum], [gains], [(features, low)], [])
        gate_out, up_out = dot("td,df->tf", hidden_in, wg), dot("td,df->tf", hidden_in, wu)
        act_low = gated(gate_out, up_out).astype(low)
        ffn = over_heads(down_part(act_low, wd))
        own, peer = ffn[:, :half], ffn[:, half:]
        block_out = layer_out(inputs, attn_sum, own, peer, gains)
        grad_own, grad_peer, gain3 = ffn_back(own, peer, grad_out, gains)
        grad_gate, grad_up = act_back(grad_own, grad_peer, gate_out, up_out, wd[:half], wd[half:])
        sum_down = scattered(weight_grad(jnp.concatenate([grad_own, grad_peer], axis=1), act_low))
        sums = [scattered(weight_grad(hidden_in, grad)) for grad in (grad_gate, grad_up)]
        grad_hidden = over_heads(hidden_back(grad_gate, grad_up, wg, wu))
        grad_resid, grad_attn, gain1, gain2 = attn_back(inputs, attn_sum, grad_hidden, grad_out, gains)
        grad_raw = attention_back(grad_attn, full, saved)
        grads = weight_grad(saved[0], grad_raw), weight_grad(grad_attn, saved[-1])
        sum_mixer = scattered(jnp.concatenate(grads, axis=1))
        grad_normed = over_heads(dot("te,de->td", grad_raw, full[:, :width_qkv]))
        input_grad, gain0 = in_back(inputs, grad_normed, grad_resid, gains)
        sum_gains = scattered(jnp.concatenate([gain0, gain1, gain2, gain3], axis=0).T).T
        return results(
            block_out, input_grad, update_mixer(sum_mixer), update_gate_up(sums), update_down(sum_down), sum_gains
        )

    if not paired:
        return simple()
    cut = count // 3 * 2

    m1, n0 = around(mixer), swap(mixer)
    inputs, grad_out = start(tokens, cotangent)
    m1, n0, mixer = sync((m1, n0, mixer))
    m2, n1 = around(m1), swap(m1)
    full = put(put(jnp.zeros((features, width_mixer), low), mixer[:count], 0), n0[:count], 0, half)
    wg, wu = jnp.zeros((features, width_ff), low), jnp.zeros((features, width_ff), low)
    m2, n1, m1, full, gate, up, wg, wu = sync((m2, n1, m1, full, gate, up, wg, wu))
    m3, n2 = around(m2), swap(m2)
    full = put(put(full, m1[:count], 1), n1[:count], 1, half)
    m3, n2, m2, full, gate, up, down = sync((m3, n2, m2, full, gate, up, down))
    g1, n3, down_far = around(gate), swap(m3), swap(down[cut:])
    full = put(put(full, m2[:count], 2), n2[:count], 2, half)
    wg = put(wg, gate, 0)
    wu = put(wu, up, 0)
    n3, m3, g1, down_far, full, gate, up, wg, wu, inputs, grad_out = sync(
        (n3, m3, g1, down_far, full, gate, up, wg, wu, inputs, grad_out)
    )
    u1, g2, h0, v0 = around(up), around(g1), swap(gate), swap(up)

    def attend(inputs, full, m3, n3, gains):
        full = put(put(full, m3[:count], 3), n3[:count], 3, half)
        attn_part, saved = attention(projections(inputs, full, gains), full)
        return apart(attn_part) + (saved, full)

    gains = gains_of((mixer, m1, m2, m3), (n0, n1, n2, n3))
    given, kept, saved, full = whole(attend, inputs, full, m3, n3, gains)
    given, kept, u1, g1, g2, v0, h0, saved, gains = sync((given, kept, u1, g1, g2, v0, h0, saved, gains))
    u2, g3, h1, v1 = around(u1), around(g2), swap(g1), swap(u1)
    kept = add(kept, near(given))
    across = far(kept)
    wg, wu, h0, v0, u1, g1 = behind(wg, wu, h0, v0, u1, g1)
    wg = put(put(wg, g1, 1), h0, 0, half)
    wu = put(put(wu, u1, 1), v0, 0, half)
    u2, g2, g3, h1, v1, across, kept, wg, wu, down = sync((u2, g2, g3, h1, v1, across, kept, wg, wu, down))
    u3, d1, h2, v2 = around(u2), around(down), swap(g2), swap(u2)
    mine = add(kept, across)
    attn_sum = together(mine, near(mine))
    (hidden_in,) = by_rows(hidden_body, side, [inputs, attn_sum], [gains], [(features, low)], [])
    wg = put(put(wg, g2, 2), h1, 1, half)
    wu = put(put(wu, u2, 2), v1, 1, half)
    u3, g3, d1, h2, v2, hidden_in, wg, wu = sync((u3, g3, d1, h2, v2, hidden_in, wg, wu))
    d2, h3, v3 = around(d1), swap(g3), swap(u3)
    wg, wu, h2, v2, u3, g3 = behind(wg, wu, h2, v2, u3, g3)
    wg = put(put(wg, g3, 3), h2, 2, half)
    wu = put(put(wu, u3, 3), v2, 2, half)
    wd_own = put(put(jnp.zeros((half, width_ff), low), down, 0), d1, 1)
    wd_peer = put(jnp.zeros((half, width_ff), low), down_far, 0, cut)
    d3 = around(d2)
    down_cut, d1_cut = down[:cut], d1[:cut]
    d2, d3, h3, v3, wg, wu, wd_own, wd_peer, down_cut, d1_cut, down_far = sync(
        (d2, d3, h3, v3, wg, wu, wd_own, wd_peer, down_cut, d1_cut, down_far)
    )
    f1, e0, e1 = around(down_far), swap(down_cut), swap(d1_cut)
    wg, wu, h3, v3 = behind(wg, wu, h3, v3)
    wg = put(wg, h3, 3, half)
    wu = put(wu, v3, 3, half)
    gate_out = dot("td,df->tf", hidden_in, wg)
    up_out = dot("td,df->tf", hidden_in, wu)
    act_low = gated(gate_out, up_out).astype(low)
    wd_own = put(put(wd_own, d2, 2), d3, 3)
    d2_cut, d3_cut = d2[:cut], d3[:cut]
    f1, e0, e1, act_low, wd_own, d2_cut, d3_cut = sync((f1, e0, e1, act_low, wd_own, d2_cut, d3_cut))
    f2, e2, e3 = around(f1), swap(d2_cut), swap(d3_cut)

    given, kept = apart(whole(down_part, act_low, wd_own))
    kept = add(kept, near(given))
    across = far(kept)
    wd_peer, f1, e0, e1, f2 = behind(wd_peer, f1, e0, e1, f2)
    f3 = around(f2)
    wd_peer = put(put(put(put(wd_peer, f1, 1, cut), f2, 2, cut), e0, 0), e1, 1)
    f3, e2, e3, across, kept, wd_peer = sync((f3, e2, e3, across, kept, wd_peer))
    wd_peer = put(put(put(wd_peer, f3, 3, cut), e2, 2), e3, 3)
    given, kept_peer = apart(down_part(act_low, wd_peer))
    mine = add(kept, across)
    kept_peer = add(kept_peer, near(given))
    ffn_own = together(mine, near(mine))
    across = far(kept_peer)
    mine = add(kept_peer, across)
    ffn_peer = together(mine, near(mine))

    def piece(tensor, hops):
        return rows_at(tensor, lax.rem(place + hops, outer), count)

    def plus(own, arrived, total=None, kind=low):
        both = own.astype(wide) + arrived.astype(wide)
        if total is not None:
            both = both + total.astype(wide)
        return both.astype(kind)

    def pieces(tensor):
        return [piece(tensor, hops) for hops in (3, 2, 1, 0)]

    def both(hops, offset, tensors):
        target = lax.rem(place + hops, outer) * count + offset
        cuts = [lax.dynamic_slice_in_dim(t, target, count, 0) for t in tensors]
        return plain(jnp.concatenate(cuts, axis=1))

    grad_ffn_own, grad_ffn_peer, grad_gain3 = ffn_back(ffn_own, ffn_peer, grad_out, gains)
    sent = pieces(weight_grad(grad_ffn_peer, act_low))
    far_parts = [given[cut:] for given in sent]
    sent = [given[:cut] for given in sent]
    sent, far_parts, grad_ffn_own, grad_ffn_peer = sync((sent, far_parts, grad_ffn_own, grad_ffn_peer))
    def grown(arrived):
        return jnp.pad(arrived, ((0, count - cut), (0, 0)))

    d3, d2, f3 = swap(sent[0]), swap(sent[1]), around(far_parts[0])

    def act_step(grad_own, grad_peer, gate_out, up_out, act_low, wd_own, wd_peer):
        back_of_act = act_back(grad_own, grad_peer, gate_out, up_out, wd_own, wd_peer)
        return back_of_act + (weight_grad(grad_own, act_low),)

    grad_gate, grad_up, wd_grad = whole(
        act_step, grad_ffn_own, grad_ffn_peer, gate_out, up_out, act_low, wd_own, wd_peer
    )
    d3, d2, f3, grad_gate, grad_up, wd_grad, sent[2:], far_parts[1:] = sync(
        (d3, d2, f3, grad_gate, grad_up, wd_grad, sent[2:], far_parts[1:])
    )
    d1, d0, f2 = swap(sent[2]), swap(sent[3]), around(add(far_parts[1], f3))
    came = around(plus(piece(wd_grad, 3), grown(d3)))

    def hidden_step(grad_gate, grad_up, hidden_in, wg, wu):
        given_kept = apart(hidden_back(grad_gate, grad_up, wg, wu))
        return given_kept + (pieces(weight_grad(hidden_in[:, half:], grad_gate)),)

    given, kept, gate_sent = whole(hidden_step, grad_gate, grad_up, hidden_in, wg, wu)
    d1, d0, f2, came, given, kept, gate_sent, grad_gate, grad_up = sync(
        (d1, d0, f2, came, given, kept, gate_sent, grad_gate, grad_up)
    )
    h3, theirs = swap(gate_sent[0]), near(given)
    came = around(plus(piece(wd_grad, 2), grown(d2), came))

    def rest_of_grads(grad_gate, grad_up, hidden_in):
        up_sent = pieces(weight_grad(hidden_in[:, half:], grad_up))
        wg_grad = weight_grad(hidden_in[:, :half], grad_gate)
        return up_sent, wg_grad, weight_grad(hidden_in[:, :half], grad_up)

    up_sent, wg_grad, wu_grad = whole(rest_of_grads, grad_gate, grad_up, hidden_in)
    h3, theirs, came, up_sent, wg_grad, wu_grad, gate_sent[1:], kept = sync(
        (h3, theirs, came, up_sent, wg_grad, wu_grad, gate_sent[1:], kept)
    )
    kept = add(kept, theirs)
    across, h2, v3 = far(kept), swap(gate_sent[1]), swap(up_sent[0])
    came = around(plus(piece(wd_grad, 1), grown(d1), came))
    gate_came = around(plus(piece(wg_grad, 3), h3))
    across, h2, v3, came, gate_came, kept, gate_sent[2:], up_sent[1:] = sync(
        (across, h2, v3, came, gate_came, kept, gate_sent[2:], up_sent[1:])
    )
    h1, h0 = swap(gate_sent[2]), swap(gate_sent[3])
    mine = add(kept, across)
    theirs = near(mine)
    gate_came = around(plus(piece(wg_grad, 2), h2, gate_came))
    up_came = around(plus(piece(wu_grad, 3), v3))

    def mixer_back(inputs, attn_sum, mine, theirs, grad_out, gains, full, saved):
        grad_hidden = together(mine, theirs)
        grad_resid, grad_attn, gain1, gain2 = attn_back(inputs, attn_sum, grad_hidden, grad_out, gains)
        grad_raw = attention_back(grad_attn, full, saved)
        given, kept = apart(dot("te,de->td", grad_raw, full[:, :width_qkv]).astype(low))
        return given, kept, grad_resid, grad_attn, gain1, gain2, grad_raw

    given, kept, grad_resid, grad_attn, grad_gain1, grad_gain2, grad_raw = whole(
        mixer_back, inputs, attn_sum, mine, theirs, grad_out, gains, full, saved
    )
    h1, h0, gate_came, up_came, given, kept, grad_resid, grad_attn, grad_raw, up_sent[1:], f2 = sync(
        (h1, h0, gate_came, up_came, given, kept, grad_resid, grad_attn, grad_raw, up_sent[1:], f2)
    )
    v2, v1, theirs = swap(up_sent[1]), swap(up_sent[2]), near(given)
    gate_came = around(plus(piece(wg_grad, 1), h1, gate_came))
    f1 = around(add(far_parts[2], f2))

    def mixer_grads(normed_low, mixed_low, grad_raw, grad_attn):
        grads = weight_grad(normed_low, grad_raw), weight_grad(grad_attn, mixed_low)
        pairs = ((3, 2), (1, 0))
        mixer_sent = [jnp.concatenate([both(hops, half, grads) for hops in pair], axis=0) for pair in pairs]
        return mixer_sent, [both(hops, 0, grads) for hops in (3, 2, 1, 0)]

    mixer_sent, mixer_own = whole(mixer_grads, saved[0], saved[-1], grad_raw, grad_attn)
    v2, v1, f1, theirs, gate_came, mixer_sent, mixer_own, kept, up_sent[3] = sync(
        (v2, v1, f1, theirs, gate_came, mixer_sent, mixer_own, kept, up_sent[3])
    )
    kept = add(kept, theirs)
    across, v0, x32 = far(kept), swap(up_sent[3]), swap(mixer_sent[0])
    up_came = around(plus(piece(wu_grad, 2), v2, up_came))
    up_came = around(plus(piece(wu_grad, 1), v1, up_came))
    v0, x32, up_came, across, kept, mixer_sent[1], inputs, f1 = sync(
        (v0, x32, up_came, across, kept, mixer_sent[1], inputs, f1)
    )
    x10, b_far = swap(mixer_sent[1]), swap(add(far_parts[3], f1))
    mine = add(kept, across)
    theirs = near(mine)
    passed = around(plus(mixer_own[0], x32[:count]))

    def finish(inputs, mine, theirs, grad_resid, attn_sum, ffn_own, ffn_peer, gains):
        block_out = layer_out(inputs, attn_sum, ffn_own, ffn_peer, gains)
        input_grad, gain0 = in_back(inputs, together(mine, theirs), grad_resid, gains)
        return block_out, input_grad, gain0

    block_out, input_grad, grad_gain0 = whole(
        finish, inputs, mine, theirs, grad_resid, attn_sum, ffn_own, ffn_peer, gains
    )
    x10, b_far, passed, block_out, input_grad, grad_gain0, x32 = sync(
        (x10, b_far, passed, block_out, input_grad, grad_gain0, x32)
    )
    passed = around(plus(mixer_own[1], x32[count:], passed))
    grad_gains = jnp.concatenate([grad_gain0, grad_gain1, grad_gain2, grad_gain3], axis=0)
    gain_sum = grad_gains[:, :half] + swap(grad_gains[:, half:])
    gain_sum = gain_sum.reshape(4, outer, count)
    down_total = plus(piece(wd_grad, 0), jnp.concatenate([d0, b_far], axis=0), came, wide)
    new_down = update_down(behind(down_total)[0])
    sum_gate = plus(piece(wg_grad, 0), h0, gate_came, wide)
    sum_up = plus(piece(wu_grad, 0), v0, up_came, wide)
    new_gate_up = update_gate_up([sum_gate, sum_up])
    passed, gain_sum, new_down, new_gate_up = sync((passed, gain_sum, new_down, new_gate_up))
    passed = around(plus(mixer_own[2], x10[:count], passed))
    sum_gains = lax.dynamic_index_in_dim(gain_sum, place, 1, False)
    for hops in (1, 2, 3):
        given = lax.dynamic_index_in_dim(gain_sum, lax.rem(place + hops, outer), 1, False)
        sum_gains = sum_gains + lax.ppermute(given, "dp", ring_pairs(groups, hops))
    new_mixer = update_mixer(plus(mixer_own[3], x10[count:], passed, wide))
    return results(block_out, input_grad, new_mixer, new_gate_up, new_down, sum_gains)


def solution(mesh):
    return jax.shard_map(
        shards,
        mesh=mesh,
        in_specs=(
            P("dp", None),
            P("dp"),
            P("dp", None),
            P("dp", "mp"),
            P(None, "dp", "mp"),
            P("mp", "dp"),
            P(None, "dp", "mp"),
            P("mp", "dp"),
            P(None, "dp"),
            P("dp", "mp"),
            P(None, "dp", "mp"),
            P("mp", "dp"),
            P(None, "dp", "mp"),
            P("mp", "dp"),
            P(None, "dp"),
            P("dp", "mp"),
            P(None, "dp", "mp"),
            P("mp", "dp"),
            P(None, "dp", "mp"),
            P("mp", "dp"),
            P(None, "dp"),
        ),
        out_specs=(
            P("dp", None),
            P("dp", None),
            P("dp", "mp"),
            P(None, "dp", "mp"),
            P("mp", "dp"),
            P(None, "dp", "mp"),
            P("mp", "dp"),
            P(None, "dp"),
            P("dp", "mp"),
            P(None, "dp", "mp"),
            P("mp", "dp"),
            P(None, "dp", "mp"),
            P("mp", "dp"),
            P(None, "dp"),
            P("dp", "mp"),
            P(None, "dp", "mp"),
            P("mp", "dp"),
            P(None, "dp", "mp"),
            P("mp", "dp"),
            P(None, "dp"),
            P("dp", "mp"),
            P(None, "dp", "mp"),
            P("mp", "dp"),
            P(None, "dp", "mp"),
            P("mp", "dp"),
            P(None, "dp"),
        ),
        check_vma=False,
    )
```

```python
from functools import partial

import jax
import jax.numpy as jnp
from jax import lax
from jax.experimental import pallas as pl
from jax.experimental.layout import Layout, with_layout_constraint
from jax.experimental.pallas import tpu as pltpu
from jax.sharding import PartitionSpec as P

HEADS = 8
KV_HEADS = 4
HEAD_DIM = 256
WINDOW = 4096
ADAM_STEP = 5


norm_eps = 1e-06
cap_value = 50.0
rope_base = 10000.0
learn_rate = 0.1
beta_one = 0.9
beta_two = 0.95
adam_eps = 1e-08
decay_rate = 0.1


low = jnp.bfloat16
wide = jnp.float32


def tie(tensor, *others):
    return lax.optimization_barrier((tensor,) + others)[0]


def plain(tensor):
    return with_layout_constraint(tensor, Layout(tuple(range(tensor.ndim))))


def ring_pairs(extent, hops=1):
    outer = extent // 2
    return [
        (2 * place + side, 2 * ((place + hops) % outer) + side)
        for place in range(outer)
        for side in range(2)
    ]


def swap_pairs(extent, stride):
    return [(place, place ^ stride) for place in range(extent)]


def rows_at(tensor, index, count):
    return lax.dynamic_slice_in_dim(tensor, index * count, count, 0)


def add(first, second, kind=low):
    return (first.astype(wide) + second.astype(wide)).astype(kind)


BLOCK = 128


def by_rows(body, side, rows, whole, outs, sums):
    length = rows[0].shape[0]

    def blocked(width):
        return pl.BlockSpec((BLOCK, width), lambda i: (i, 0))

    def kept(shape):
        return pl.BlockSpec(shape, lambda i: (0, 0))

    return pl.pallas_call(
        body,
        grid=(length // BLOCK,),
        in_specs=[pl.BlockSpec(memory_space=pltpu.SMEM)]
        + [blocked(t.shape[1]) for t in rows]
        + [kept(t.shape) for t in whole],
        out_specs=[blocked(width) for width, kind in outs] + [kept((1, width)) for width in sums],
        out_shape=[jax.ShapeDtypeStruct((length, width), kind) for width, kind in outs]
        + [jax.ShapeDtypeStruct((1, width), wide) for width in sums],
        compiler_params=pltpu.CompilerParams(vmem_limit_bytes=48 * 1024 * 1024),
    )(side, *rows, *whole)


def factor_of(value):
    return lax.rsqrt(jnp.mean(value * value, axis=-1, keepdims=True) + norm_eps)


def back_of(value, factor, gain, grad):
    scaled = grad * (1.0 + gain)
    shared = factor * factor * jnp.mean(scaled * value, axis=-1, keepdims=True)
    return factor * (scaled - shared * value), grad * (value * factor)


def add_up(ref, value):
    @pl.when(pl.program_id(0) == 0)
    def start():
        ref[...] = jnp.zeros_like(ref)

    ref[...] += jnp.sum(value, axis=0, keepdims=True)


def pieces_of(value, groups):
    count = value.shape[1] // groups
    return [value[:, k * count : (k + 1) * count] for k in range(groups)]


def turn(value, side, groups):
    cut = pieces_of(value, groups)
    even, odd = jnp.concatenate(cut[0::2], axis=1), jnp.concatenate(cut[1::2], axis=1)
    first, second = jnp.where(side == 0, even, odd), jnp.where(side == 0, odd, even)
    return jnp.concatenate([first, second], axis=1)


def straighten(value, side, groups):
    half = value.shape[1] // 2
    own, peer = value[:, :half], value[:, half:]
    even, odd = jnp.where(side == 0, own, peer), jnp.where(side == 0, peer, own)
    woven = zip(pieces_of(even, groups // 2), pieces_of(odd, groups // 2))
    return jnp.concatenate([cut for pair in woven for cut in pair], axis=1)


def start_body(groups, side, tokens, cotangent, valid, inputs, grad_out):
    inputs[...] = turn(tokens[...].astype(wide), side[0], groups).astype(low)
    grad_out[...] = turn(cotangent[...].astype(wide) * valid[...], side[0], groups).astype(low)


def normed_body(side, inputs, gains, normed):
    value = inputs[...].astype(wide)
    normed[...] = (value * factor_of(value) * (1.0 + gains[0:1])).astype(low)


def residual_of(inputs, attn, gains):
    value, mixed = inputs[...].astype(wide), attn[...].astype(wide)
    factor = factor_of(mixed)
    return value + mixed * factor * (1.0 + gains[1:2]), mixed, factor


def hidden_body(side, inputs, attn, gains, hidden):
    residual = residual_of(inputs, attn, gains)[0]
    hidden[...] = (residual * factor_of(residual) * (1.0 + gains[2:3])).astype(low)


def ffn_of(own, peer):
    return jnp.concatenate([own[...].astype(wide), peer[...].astype(wide)], axis=1)


def ffn_back_body(side, own, peer, grad_out, gains, grad_own, grad_peer, grad_gain):
    ffn = ffn_of(own, peer)
    grad, term = back_of(ffn, factor_of(ffn), gains[3:4], grad_out[...].astype(wide))
    half = ffn.shape[1] // 2
    grad_own[...] = grad[:, :half].astype(low)
    grad_peer[...] = grad[:, half:].astype(low)
    add_up(grad_gain, term)


def out_body(groups, side, inputs, attn, own, peer, gains, out):
    ffn = ffn_of(own, peer)
    value = residual_of(inputs, attn, gains)[0] + ffn * factor_of(ffn) * (1.0 + gains[3:4])
    out[...] = straighten(value, side[0], groups).astype(low)


def attn_back_body(side, inputs, attn, grad_hidden, grad_out, gains, grad_resid, grad_attn, gain1, gain2):
    residual, mixed, factor = residual_of(inputs, attn, gains)
    grad, term2 = back_of(residual, factor_of(residual), gains[2:3], grad_hidden[...].astype(wide))
    grad = grad + grad_out[...].astype(wide)
    grad_resid[...] = grad
    back, term1 = back_of(mixed, factor, gains[1:2], grad)
    grad_attn[...] = back.astype(low)
    add_up(gain1, term1)
    add_up(gain2, term2)


def in_back_body(groups, side, inputs, grad_normed, grad_resid, gains, input_grad, gain0):
    value = inputs[...].astype(wide)
    grad, term = back_of(value, factor_of(value), gains[0:1], grad_normed[...].astype(wide))
    input_grad[...] = straighten(grad_resid[...] + grad, side[0], groups)
    add_up(gain0, term)


def rotate(tensor, cosine, sine):
    half_dim = tensor.shape[-1] // 2
    first = tensor[..., :half_dim]
    second = tensor[..., half_dim:]
    return jnp.concatenate(
        [first * cosine - second * sine, second * cosine + first * sine], axis=-1
    )


def layout(labels):
    length = labels.shape[0]
    places = jnp.arange(length, dtype=jnp.int32)
    same_seq = labels[:, None] == labels[None, :]
    earlier = places[None, :] < places[:, None]
    position = jnp.sum((same_seq & earlier).astype(jnp.int32), axis=1)
    allowed = (
        same_seq
        & (places[None, :] <= places[:, None])
        & (places[:, None] - places[None, :] < WINDOW)
    )
    half_dim = HEAD_DIM // 2
    freq = rope_base ** (-2.0 * jnp.arange(half_dim, dtype=jnp.float32) / HEAD_DIM)
    angle = position.astype(jnp.float32)[:, None] * freq[None, :]
    return (allowed, jnp.cos(angle)[:, None, :], jnp.sin(angle)[:, None, :])


def scores(queries, key_rows, allowed):
    raw_scores = jnp.einsum("qkgd,skd->kgqs", queries, key_rows, preferred_element_type=jnp.float32)
    squashed = jnp.tanh(raw_scores / cap_value)
    capped = jnp.where(allowed[None, None], cap_value * squashed, -1e30)
    return (squashed, capped)


def rotate_back(grad_in, cosine, sine, shape_like):
    unused, pull = jax.vjp(lambda tensor: rotate(tensor, cosine, sine), shape_like)
    return pull(grad_in)[0]


def adam_step(master, gradient, moment, square, steps_done):
    new_moment = beta_one * moment + (1.0 - beta_one) * gradient
    new_square = beta_two * square + (1.0 - beta_two) * gradient * gradient
    fix_one = 1.0 - beta_one**steps_done
    fix_two = 1.0 - beta_two**steps_done
    stride = new_moment / fix_one / (jnp.sqrt(new_square / fix_two) + adam_eps)
    return (-learn_rate * (stride + decay_rate * master), new_moment, new_square)


def shards(
    tokens,
    segments,
    cotangent,
    query_weight,
    keyval_weight,
    output_weight,
    gateup_weight,
    down_weight,
    norm_gains,
    moment_query,
    moment_keyval,
    moment_output,
    moment_gateup,
    moment_down,
    moment_gains,
    square_query,
    square_keyval,
    square_output,
    square_gateup,
    square_down,
    square_gains,
):
    groups, parts = lax.axis_size("dp"), lax.axis_size("mp")
    outer = groups // 2
    index = lax.axis_index("dp")
    place = index // 2
    side = lax.rem(index, 2).astype(jnp.int32).reshape(1)
    length, features = tokens.shape
    half = features // 2
    count = features // groups
    group = HEADS // KV_HEADS
    width_q, width_kv = query_weight.shape[1], keyval_weight.shape[2]
    width_qkv = width_q + 2 * width_kv
    width_mixer = width_qkv + output_weight.shape[0]
    width_ff = down_weight.shape[0]
    kv_local = width_kv // HEAD_DIM
    heads_local = kv_local * group
    qscale = HEAD_DIM ** (-0.5)
    core = lax.rem(lax.axis_index("mp"), 2)
    paired = outer == 4 and parts == 4

    def dot(pattern, first, second):
        return jnp.einsum(pattern, first, second, preferred_element_type=wide)

    def around(tensor, hops=1):
        return lax.ppermute(tensor, "dp", ring_pairs(groups, hops))

    def swap(tensor):
        return lax.ppermute(tensor, "dp", swap_pairs(groups, 1))

    def near(tensor):
        return lax.ppermute(tensor, "mp", swap_pairs(parts, 1))

    def far(tensor):
        return lax.ppermute(tensor, "mp", swap_pairs(parts, 2))

    def apart(partial_sum):
        rows = length // 2
        return rows_at(partial_sum, 1 - core, rows), rows_at(partial_sum, core, rows)

    def together(mine, theirs):
        first = jnp.where(core == 0, mine, theirs)
        second = jnp.where(core == 0, theirs, mine)
        return jnp.concatenate([first, second], axis=0)

    allowed, cosine, sine = layout(segments)
    valid = (segments >= 0).astype(wide)[:, None]

    def projections(inputs, weights, gains):
        (normed_low,) = by_rows(normed_body, side, [inputs], [gains], [(features, low)], [])
        mixer_raw = dot("td,de->te", normed_low, weights[:, :width_qkv])
        qraw = mixer_raw[:, :width_q].reshape(length, heads_local, HEAD_DIM)
        kraw = mixer_raw[:, width_q : width_q + width_kv].reshape(length, kv_local, HEAD_DIM)
        queries = (
            (rotate(qraw, cosine, sine) * qscale).astype(low).reshape(length, kv_local, group, HEAD_DIM)
        )
        key_rows = rotate(kraw, cosine, sine).astype(low)
        value_rows = mixer_raw[:, width_q + width_kv :].astype(low).reshape(length, kv_local, HEAD_DIM)
        return normed_low, queries, key_rows, value_rows

    def attention(projected, weights):
        unused, queries, key_rows, value_rows = projected
        squashed, capped = scores(queries, key_rows, allowed)
        row_top = jnp.max(capped, axis=-1, keepdims=True)
        log_total = row_top + jnp.log(jnp.sum(jnp.exp(capped - row_top), axis=-1, keepdims=True))
        probs = jnp.exp(capped - log_total)
        probs_low = probs.astype(low)
        mixed_low = dot("kgqs,skd->qkgd", probs_low, value_rows).astype(low)
        mixed_low = mixed_low.reshape(length, heads_local * HEAD_DIM)
        attn_part = dot("te,de->td", mixed_low, weights[:, width_qkv:]).astype(low)
        return attn_part, projected + (squashed, probs, probs_low, mixed_low)

    def attention_back(grad_attn, weights, saved):
        normed_low, queries, key_rows, value_rows, squashed, probs, probs_low, mixed_low = saved
        grad_mixed = dot("td,de->te", grad_attn, weights[:, width_qkv:]).astype(low)
        grad_mixed = grad_mixed.reshape(length, kv_local, group, HEAD_DIM)
        grad_probs = dot("qkgd,skd->kgqs", grad_mixed, value_rows)
        grad_value = dot("kgqs,qkgd->skd", probs_low, grad_mixed)
        grad_value = grad_value.astype(low).reshape(length, kv_local * HEAD_DIM)
        grad_capped = probs * (grad_probs - jnp.sum(probs * grad_probs, axis=-1, keepdims=True))
        grad_scores = (grad_capped * (1.0 - squashed * squashed)).astype(low)
        grad_query = dot("kgqs,skd->qkgd", grad_scores, key_rows)
        grad_query = grad_query.reshape(length, heads_local, HEAD_DIM) * qscale
        shape_q = jnp.zeros((length, heads_local, HEAD_DIM), wide)
        grad_qraw = rotate_back(grad_query, cosine, sine, shape_q).astype(low)
        grad_key = dot("kgqs,qkgd->skd", grad_scores, queries)
        shape_k = jnp.zeros((length, kv_local, HEAD_DIM), wide)
        grad_kraw = rotate_back(grad_key, cosine, sine, shape_k).astype(low)
        flat = [t.reshape(length, -1) for t in (grad_qraw, grad_kraw, grad_value)]
        return plain(jnp.concatenate(flat, axis=1))

    def gated(gate_in, up_in):
        return jax.nn.gelu(gate_in, approximate=True) * up_in

    def weight_grad(first, second):
        return plain(dot("td,te->de", first, second).astype(low))

    def ffn_back(ffn_own, ffn_peer, grad_out, gains):
        return by_rows(
            ffn_back_body, side, [ffn_own, ffn_peer, grad_out], [gains], [(half, low)] * 2, [features]
        )

    def layer_out(inputs, attn_sum, ffn_own, ffn_peer, gains):
        rows = [inputs, attn_sum, ffn_own, ffn_peer]
        return by_rows(partial(out_body, groups), side, rows, [gains], [(features, low)], [])[0]

    def attn_back(inputs, attn_sum, grad_hidden, grad_out, gains):
        rows = [inputs, attn_sum, grad_hidden, grad_out]
        outs = [(features, wide), (features, low)]
        return by_rows(attn_back_body, side, rows, [gains], outs, [features] * 2)

    def in_back(inputs, grad_normed, grad_resid, gains):
        rows = [inputs, grad_normed, grad_resid]
        return by_rows(partial(in_back_body, groups), side, rows, [gains], [(features, wide)], [features])

    steps_done = float(ADAM_STEP)

    def updated(master, total, moment, square):
        return (total,) + adam_step(master, total, moment, square, steps_done)

    def update_gate_up(sums):
        return updated(gateup_weight, jnp.stack(sums), moment_gateup, square_gateup)

    def update_down(total):
        return updated(down_weight.T, total, moment_down.T, square_down.T)

    def update_mixer(total):
        total = plain(total)
        sum_k, sum_v = total[:, width_q : width_q + width_kv], total[:, width_q + width_kv : width_qkv]
        return (
            updated(query_weight, total[:, :width_q], moment_query, square_query),
            updated(keyval_weight, jnp.stack([sum_k, sum_v]), moment_keyval, square_keyval),
            updated(output_weight.T, total[:, width_qkv:], moment_output.T, square_output.T),
        )

    gain_row = norm_gains.astype(low).reshape(1, 4 * count)
    mixer = jnp.concatenate(
        [
            query_weight.astype(low),
            keyval_weight[0].astype(low),
            keyval_weight[1].astype(low),
            output_weight.astype(low).T,
        ],
        axis=1,
    )
    mixer = jnp.concatenate([mixer, jnp.pad(gain_row, ((0, 15), (0, width_mixer - 4 * count)))], axis=0)
    mixer = plain(mixer)

    def source(step):
        return lax.rem(place - step + outer, outer)

    def put(full, piece, step, offset=0):
        return lax.dynamic_update_slice_in_dim(full, piece, source(step) * count + offset, 0)

    def gains_of(held, peer):
        gain_low = jnp.zeros((2, outer, 4, count), low)
        for at, pieces in enumerate((held, peer)):
            for step, piece in enumerate(pieces):
                gain_piece = piece[count, : 4 * count].reshape(1, 1, 4, count)
                gain_low = lax.dynamic_update_slice(gain_low, gain_piece, (at, source(step), 0, 0))
        return jnp.moveaxis(gain_low.reshape(groups, 4, count), 1, 0).reshape(4, features).astype(wide)

    def start(tokens_in, cotangent_in):
        return by_rows(
            partial(start_body, groups), side, [tokens_in, cotangent_in, valid], [], [(features, low)] * 2, []
        )

    clock = [jnp.broadcast_to(valid[:8], (8, 128))]

    def sync(values):
        values, clock[0] = lax.optimization_barrier((values, clock[0]))
        return values

    always = index < groups

    def whole(work, *values):
        shapes = jax.eval_shape(work, *values)

        def blank(*unused):
            return jax.tree.map(lambda t: jnp.zeros(t.shape, t.dtype), shapes)

        return lax.cond(always, work, blank, *values)

    def behind(*values):
        values, clock[0] = lax.optimization_barrier((values, clock[0] * 0.5))
        return values

    gate, up = plain(gateup_weight[0].astype(low)), plain(gateup_weight[1].astype(low))
    down = plain(down_weight.astype(low).T)

    def down_part(act_low, weights):
        return dot("tf,df->td", act_low, weights).astype(low)

    def act_back(grad_own, grad_peer, gate_out, up_out, wd_own, wd_peer):
        grad_act = dot("td,df->tf", grad_own, wd_own) + dot("td,df->tf", grad_peer, wd_peer)
        unused, pull_act = jax.vjp(gated, gate_out, up_out)
        return tuple(grad.astype(low) for grad in pull_act(grad_act))

    def hidden_back(grad_gate, grad_up, wg, wu):
        return (dot("tf,df->td", grad_gate, wg) + dot("tf,df->td", grad_up, wu)).astype(low)

    def results(block_out, input_grad, new_mixer, new_gate_up, new_down, sum_gains):
        new_query, new_keyval, new_output = new_mixer
        new_gains = updated(norm_gains, sum_gains, moment_gains, square_gains)
        turned_back = [tuple(t.T for t in group_of) for group_of in (new_output, new_down)]
        new = (new_query, new_keyval, turned_back[0], new_gate_up, turned_back[1], new_gains)
        return (block_out, input_grad) + tuple(new[at][kind] for kind in range(4) for at in range(6))

    def simple():
        def gathered(own):
            rows = lax.all_gather(own, "dp", axis=0, tiled=True).reshape(outer, 2, -1, own.shape[1])
            return jnp.moveaxis(jnp.where(side == 0, rows, rows[:, ::-1]), 1, 0)

        def whole_rows(own):
            return gathered(own).reshape(features, own.shape[1])

        def scattered(rows):
            rows = rows.astype(wide).reshape(2, outer, count, rows.shape[1])
            rows = jnp.moveaxis(jnp.where(side == 0, rows, rows[::-1]), 0, 1).reshape(features, -1)
            return lax.psum_scatter(rows, "dp", scatter_dimension=0, tiled=True)

        def over_heads(part):
            return lax.psum(part.astype(wide), "mp").astype(low)

        rows = gathered(mixer)
        full = rows[:, :, :count].reshape(features, width_mixer)
        gains = jnp.moveaxis(rows[:, :, count, : 4 * count].reshape(groups, 4, count), 1, 0)
        gains = gains.reshape(4, features).astype(wide)
        wg, wu, wd = whole_rows(gate), whole_rows(up), whole_rows(down)
        inputs, grad_out = start(tokens, cotangent)
        attn_part, saved = attention(projections(inputs, full, gains), full)
        attn_sum = over_heads(attn_part)
        (hidden_in,) = by_rows(hidden_body, side, [inputs, attn_sum], [gains], [(features, low)], [])
        gate_out, up_out = dot("td,df->tf", hidden_in, wg), dot("td,df->tf", hidden_in, wu)
        act_low = gated(gate_out, up_out).astype(low)
        ffn = over_heads(down_part(act_low, wd))
        own, peer = ffn[:, :half], ffn[:, half:]
        block_out = layer_out(inputs, attn_sum, own, peer, gains)
        grad_own, grad_peer, gain3 = ffn_back(own, peer, grad_out, gains)
        grad_gate, grad_up = act_back(grad_own, grad_peer, gate_out, up_out, wd[:half], wd[half:])
        sum_down = scattered(weight_grad(jnp.concatenate([grad_own, grad_peer], axis=1), act_low))
        sums = [scattered(weight_grad(hidden_in, grad)) for grad in (grad_gate, grad_up)]
        grad_hidden = over_heads(hidden_back(grad_gate, grad_up, wg, wu))
        grad_resid, grad_attn, gain1, gain2 = attn_back(inputs, attn_sum, grad_hidden, grad_out, gains)
        grad_raw = attention_back(grad_attn, full, saved)
        grads = weight_grad(saved[0], grad_raw), weight_grad(grad_attn, saved[-1])
        sum_mixer = scattered(jnp.concatenate(grads, axis=1))
        grad_normed = over_heads(dot("te,de->td", grad_raw, full[:, :width_qkv]))
        input_grad, gain0 = in_back(inputs, grad_normed, grad_resid, gains)
        sum_gains = scattered(jnp.concatenate([gain0, gain1, gain2, gain3], axis=0).T).T
        return results(
            block_out, input_grad, update_mixer(sum_mixer), update_gate_up(sums), update_down(sum_down), sum_gains
        )

    if not paired:
        return simple()
    cut = count // 2

    m1, n0 = around(mixer), swap(mixer)
    inputs, grad_out = start(tokens, cotangent)
    m1, n0, mixer = sync((m1, n0, mixer))
    m2, n1 = around(m1), swap(m1)
    full = put(put(jnp.zeros((features, width_mixer), low), mixer[:count], 0), n0[:count], 0, half)
    wg, wu = jnp.zeros((features, width_ff), low), jnp.zeros((features, width_ff), low)
    m2, n1, m1, full, gate, up, wg, wu, allowed, cosine, sine = sync(
        (m2, n1, m1, full, gate, up, wg, wu, allowed, cosine, sine)
    )
    m3, n2 = around(m2), swap(m2)
    full = put(put(full, m1[:count], 1), n1[:count], 1, half)
    m3, n2, m2, full, gate, up, down = sync((m3, n2, m2, full, gate, up, down))
    g1, n3, down_far = around(gate), swap(m3), swap(down[cut:])
    full = put(put(full, m2[:count], 2), n2[:count], 2, half)
    wg = put(wg, gate, 0)
    wu = put(wu, up, 0)
    n3, m3, g1, down_far, full, gate, up, wg, wu, inputs, grad_out = sync(
        (n3, m3, g1, down_far, full, gate, up, wg, wu, inputs, grad_out)
    )
    u1, g2, h0, v0 = around(up), around(g1), swap(gate), swap(up)

    def attend(inputs, full, m3, n3, gains):
        full = put(put(full, m3[:count], 3), n3[:count], 3, half)
        attn_part, saved = attention(projections(inputs, full, gains), full)
        return apart(attn_part) + (saved, full)

    gains = gains_of((mixer, m1, m2, m3), (n0, n1, n2, n3))
    given, kept, saved, full = whole(attend, inputs, full, m3, n3, gains)
    given, kept, u1, g1, g2, v0, h0, saved, gains = sync((given, kept, u1, g1, g2, v0, h0, saved, gains))
    u2, g3, h1, v1 = around(u1), around(g2), swap(g1), swap(u1)
    kept = add(kept, near(given))
    across = far(kept)
    wg, wu, h0, v0, u1, g1 = behind(wg, wu, h0, v0, u1, g1)
    wg = put(put(wg, g1, 1), h0, 0, half)
    wu = put(put(wu, u1, 1), v0, 0, half)
    u2, g2, g3, h1, v1, across, kept, wg, wu, down = sync((u2, g2, g3, h1, v1, across, kept, wg, wu, down))
    u3, d1, h2, v2 = around(u2), around(down), swap(g2), swap(u2)
    mine = add(kept, across)
    attn_sum = together(mine, near(mine))
    (hidden_in,) = by_rows(hidden_body, side, [inputs, attn_sum], [gains], [(features, low)], [])
    wg = put(put(wg, g2, 2), h1, 1, half)
    wu = put(put(wu, u2, 2), v1, 1, half)
    u3, g3, d1, h2, v2, hidden_in, wg, wu = sync((u3, g3, d1, h2, v2, hidden_in, wg, wu))
    d2, h3 = around(d1), swap(g3)
    v3 = swap(tie(u3, h3))
    wg, wu, h2, v2, u3, g3 = behind(wg, wu, h2, v2, u3, g3)
    wg = put(put(wg, g3, 3), h2, 2, half)
    wu = put(put(wu, u3, 3), v2, 2, half)
    wd_own = put(put(jnp.zeros((half, width_ff), low), down, 0), d1, 1)
    wd_peer = put(jnp.zeros((half, width_ff), low), down_far, 0, cut)
    d3 = around(d2)
    wg = put(wg, h3, 3, half)
    gate_out = dot("td,df->tf", hidden_in, wg)
    down_cut, d1_cut = down[:cut], d1[:cut]
    d2, d3, v3, wg, gate_out, wu, wd_own, wd_peer, down_cut, d1_cut, down_far = sync(
        (d2, d3, v3, wg, gate_out, wu, wd_own, wd_peer, down_cut, d1_cut, down_far)
    )
    f1, e0, e1 = around(down_far), swap(down_cut), swap(d1_cut)
    wu, v3 = behind(wu, v3)
    wu = put(wu, v3, 3, half)
    up_out = dot("td,df->tf", hidden_in, wu)
    act_low = gated(gate_out, up_out).astype(low)
    wd_own = put(put(wd_own, d2, 2), d3, 3)
    d2_cut, d3_cut = d2[:cut], d3[:cut]
    given, kept = apart(down_part(act_low, wd_own))
    f1, e0, e1, act_low, given, kept, d2_cut, d3_cut = sync((f1, e0, e1, act_low, given, kept, d2_cut, d3_cut))
    f2, e2, e3 = around(f1), swap(d2_cut), swap(d3_cut)
    kept = add(kept, near(given))
    across = far(kept)
    wd_peer, f1, e0, e1 = behind(wd_peer, f1, e0, e1)
    f3 = around(tie(f2, kept))
    wd_peer = put(put(put(put(wd_peer, f1, 1, cut), f2, 2, cut), e0, 0), e1, 1)
    f3, e2, e3, across, kept, wd_peer = sync((f3, e2, e3, across, kept, wd_peer))
    wd_peer = put(put(put(wd_peer, f3, 3, cut), e2, 2), e3, 3)
    given, kept_peer = apart(down_part(act_low, wd_peer))
    mine = add(kept, across)
    kept_peer = add(kept_peer, near(given))
    ffn_own = together(mine, near(mine))
    across = far(kept_peer)
    mine = add(kept_peer, across)
    ffn_peer = together(mine, near(mine))

    def piece(tensor, hops):
        return rows_at(tensor, lax.rem(place + hops, outer), count)

    def plus(own, arrived, total=None, kind=low):
        both = own.astype(wide) + arrived.astype(wide)
        if total is not None:
            both = both + total.astype(wide)
        return both.astype(kind)

    def pieces(tensor):
        return [piece(tensor, hops) for hops in (3, 2, 1, 0)]

    def rows_of(tensor, offset, rows):
        starts = [lax.rem(place + hops, outer) * count + offset for hops in (3, 2, 1, 0)]
        return [lax.dynamic_slice_in_dim(tensor, first, rows, 0) for first in starts]

    def both(hops, offset, tensors):
        target = lax.rem(place + hops, outer) * count + offset
        cuts = [lax.dynamic_slice_in_dim(t, target, count, 0) for t in tensors]
        return plain(jnp.concatenate(cuts, axis=1))

    grad_ffn_own, grad_ffn_peer, grad_gain3 = ffn_back(ffn_own, ffn_peer, grad_out, gains)
    wd_grad = weight_grad(grad_ffn_peer, act_low)
    cut = count * 7 // 18 // 16 * 16
    sent, far_parts = jnp.concatenate(rows_of(wd_grad, 0, cut), axis=0), rows_of(wd_grad, cut, count - cut)
    sent, far_parts, grad_ffn_own, grad_ffn_peer = sync((sent, far_parts, grad_ffn_own, grad_ffn_peer))

    arrived, f3 = swap(sent), around(far_parts[0])

    def act_step(grad_own, grad_peer, gate_out, up_out, act_low, hidden_in, wd_own, wd_peer):
        grad_gate, grad_up = act_back(grad_own, grad_peer, gate_out, up_out, wd_own, wd_peer)
        gate_sent = pieces(weight_grad(hidden_in[:, half:], grad_gate))
        return grad_gate, grad_up, weight_grad(grad_own, act_low), gate_sent

    grad_gate, grad_up, wd_grad, gate_sent = whole(
        act_step, grad_ffn_own, grad_ffn_peer, gate_out, up_out, act_low, hidden_in, wd_own, wd_peer
    )
    arrived, f3, grad_gate, grad_up, wd_grad, gate_sent, far_parts = sync(
        (arrived, f3, grad_gate, grad_up, wd_grad, gate_sent, far_parts)
    )

    def grown(at):
        return jnp.pad(arrived[at * cut : (at + 1) * cut], ((0, count - cut), (0, 0)))

    h3 = swap(gate_sent[0])
    came = around(plus(piece(wd_grad, 3), grown(0)))
    f2 = around(add(far_parts[1], f3))

    def hidden_step(grad_gate, grad_up, wg, wu):
        return apart(hidden_back(grad_gate, grad_up, wg, wu))

    given, kept = whole(hidden_step, grad_gate, grad_up, wg, wu)
    h3, came, f2, given, kept, gate_sent, grad_gate, grad_up = sync(
        (h3, came, f2, given, kept, gate_sent, grad_gate, grad_up)
    )
    h2, theirs = swap(gate_sent[1]), near(given)
    came = around(plus(piece(wd_grad, 2), grown(1), came))
    f1 = around(add(far_parts[2], f2))

    def rest_of_grads(grad_gate, grad_up, hidden_in, gate_sent):
        up_sent = pieces(weight_grad(hidden_in[:, half:], grad_up))
        wg_grad = weight_grad(hidden_in[:, :half], grad_gate)
        mixed_sent = [jnp.concatenate(pair, axis=0) for pair in zip(gate_sent[2:], up_sent[:2])]
        return mixed_sent, up_sent[2:], wg_grad, weight_grad(hidden_in[:, :half], grad_up)

    mixed_sent, up_sent, wg_grad, wu_grad = whole(rest_of_grads, grad_gate, grad_up, hidden_in, gate_sent)
    h2, theirs, came, f1, mixed_sent, up_sent, wg_grad, wu_grad, kept = sync(
        (h2, theirs, came, f1, mixed_sent, up_sent, wg_grad, wu_grad, kept)
    )
    pair = swap(mixed_sent[0])
    kept = add(kept, theirs)
    across = far(kept)
    came = around(plus(piece(wd_grad, 1), grown(2), came))
    gate_came = around(plus(piece(wg_grad, 3), h3))
    across, pair, came, gate_came, kept, mixed_sent[1], up_sent = sync(
        (across, pair, came, gate_came, kept, mixed_sent[1], up_sent)
    )
    h1, v3 = pair[:count], pair[count:]
    pair = swap(mixed_sent[1])
    mine = add(kept, across)
    theirs = near(mine)
    gate_came = around(plus(piece(wg_grad, 2), h2, gate_came))
    up_came = around(plus(piece(wu_grad, 3), v3))

    def mixer_back(inputs, attn_sum, mine, theirs, grad_out, gains, full, saved):
        grad_hidden = together(mine, theirs)
        grad_resid, grad_attn, gain1, gain2 = attn_back(inputs, attn_sum, grad_hidden, grad_out, gains)
        grad_raw = attention_back(grad_attn, full, saved)
        given, kept = apart(dot("te,de->td", grad_raw, full[:, :width_qkv]).astype(low))
        return given, kept, grad_resid, grad_attn, gain1, gain2, grad_raw

    given, kept, grad_resid, grad_attn, grad_gain1, grad_gain2, grad_raw = whole(
        mixer_back, inputs, attn_sum, mine, theirs, grad_out, gains, full, saved
    )
    pair, gate_came, up_came, given, kept, grad_resid, grad_attn, grad_raw, up_sent = sync(
        (pair, gate_came, up_came, given, kept, grad_resid, grad_attn, grad_raw, up_sent)
    )
    h0, v2 = pair[:count], pair[count:]
    v1, theirs = swap(up_sent[0]), near(given)
    gate_came = around(plus(piece(wg_grad, 1), h1, gate_came))

    def mixer_grads(normed_low, mixed_low, grad_raw, grad_attn):
        grads = weight_grad(normed_low, grad_raw), weight_grad(grad_attn, mixed_low)
        pairs = ((3, 2), (1, 0))
        mixer_sent = [jnp.concatenate([both(hops, half, grads) for hops in pair], axis=0) for pair in pairs]
        return mixer_sent, [both(hops, 0, grads) for hops in (3, 2, 1, 0)]

    mixer_sent, mixer_own = whole(mixer_grads, saved[0], saved[-1], grad_raw, grad_attn)
    v1, theirs, gate_came, mixer_sent, mixer_own, kept, up_sent = sync(
        (v1, theirs, gate_came, mixer_sent, mixer_own, kept, up_sent)
    )
    v0, x32 = swap(up_sent[1]), swap(mixer_sent[0])
    kept = add(kept, theirs)
    across = far(kept)
    up_came = around(plus(piece(wu_grad, 2), v2, up_came))
    gate_late = tie(gate_came, up_came)
    sum_gate = plus(piece(wg_grad, 0), h0, gate_late, wide)
    up_came = around(plus(piece(wu_grad, 1), v1, up_came))
    v0, x32, up_came, across, kept, mixer_sent[1], inputs, f1, sum_gate = sync(
        (v0, x32, up_came, across, kept, mixer_sent[1], inputs, f1, sum_gate)
    )
    x10, b_far = swap(mixer_sent[1]), swap(add(far_parts[3], f1))
    m3 = around(plus(mixer_own[0], x32[:count]), 3)
    m2 = around(plus(mixer_own[1], x32[count:]), 2)
    mine = add(kept, across)
    theirs = near(mine)

    def finish(inputs, mine, theirs, grad_resid, attn_sum, ffn_own, ffn_peer, gains):
        block_out = layer_out(inputs, attn_sum, ffn_own, ffn_peer, gains)
        input_grad, gain0 = in_back(inputs, together(mine, theirs), grad_resid, gains)
        return block_out, input_grad, gain0

    block_out, input_grad, grad_gain0 = whole(
        finish, inputs, mine, theirs, grad_resid, attn_sum, ffn_own, ffn_peer, gains
    )
    x10, b_far, m3, m2, block_out, input_grad, grad_gain0 = sync(
        (x10, b_far, m3, m2, block_out, input_grad, grad_gain0)
    )
    m1 = around(plus(mixer_own[2], x10[:count]))
    grad_gains = jnp.concatenate([grad_gain0, grad_gain1, grad_gain2, grad_gain3], axis=0)
    gain_sum = grad_gains[:, :half] + swap(grad_gains[:, half:])
    gain_sum = gain_sum.reshape(4, outer, count)
    down_total = plus(piece(wd_grad, 0), jnp.concatenate([arrived[3 * cut :], b_far], axis=0), came, wide)
    new_down = update_down(behind(down_total)[0])
    sum_up = plus(piece(wu_grad, 0), v0, up_came, wide)
    new_gate_up = update_gate_up([sum_gate, sum_up])
    sum_gains = lax.dynamic_index_in_dim(gain_sum, place, 1, False)
    for hops in (1, 2, 3):
        given = lax.dynamic_index_in_dim(gain_sum, lax.rem(place + hops, outer), 1, False)
        sum_gains = sum_gains + around(given, hops)
    m1, sum_gains, new_down, new_gate_up = sync((m1, sum_gains, new_down, new_gate_up))
    sum_mixer = plus(mixer_own[3], x10[count:], m1, wide) + m2.astype(wide) + m3.astype(wide)
    return results(block_out, input_grad, update_mixer(sum_mixer), new_gate_up, new_down, sum_gains)


def solution(mesh):
    return jax.shard_map(
        shards,
        mesh=mesh,
        in_specs=(
            P("dp", None),
            P("dp"),
            P("dp", None),
            P("dp", "mp"),
            P(None, "dp", "mp"),
            P("mp", "dp"),
            P(None, "dp", "mp"),
            P("mp", "dp"),
            P(None, "dp"),
            P("dp", "mp"),
            P(None, "dp", "mp"),
            P("mp", "dp"),
            P(None, "dp", "mp"),
            P("mp", "dp"),
            P(None, "dp"),
            P("dp", "mp"),
            P(None, "dp", "mp"),
            P("mp", "dp"),
            P(None, "dp", "mp"),
            P("mp", "dp"),
            P(None, "dp"),
        ),
        out_specs=(
            P("dp", None),
            P("dp", None),
            P("dp", "mp"),
            P(None, "dp", "mp"),
            P("mp", "dp"),
            P(None, "dp", "mp"),
            P("mp", "dp"),
            P(None, "dp"),
            P("dp", "mp"),
            P(None, "dp", "mp"),
            P("mp", "dp"),
            P(None, "dp", "mp"),
            P("mp", "dp"),
            P(None, "dp"),
            P("dp", "mp"),
            P(None, "dp", "mp"),
            P("mp", "dp"),
            P(None, "dp", "mp"),
            P("mp", "dp"),
            P(None, "dp"),
            P("dp", "mp"),
            P(None, "dp", "mp"),
            P("mp", "dp"),
            P(None, "dp", "mp"),
            P("mp", "dp"),
            P(None, "dp"),
        ),
        check_vma=False,
    )
```

```python
from functools import partial

import jax
import jax.numpy as jnp
from jax import lax
from jax.experimental import pallas as pl
from jax.experimental.layout import Layout, with_layout_constraint
from jax.experimental.pallas import tpu as pltpu
from jax.sharding import PartitionSpec as P

HEADS = 8
KV_HEADS = 4
HEAD_DIM = 256
WINDOW = 4096
ADAM_STEP = 5


norm_eps = 1e-06
cap_value = 50.0
rope_base = 10000.0
learn_rate = 0.1
beta_one = 0.9
beta_two = 0.95
adam_eps = 1e-08
decay_rate = 0.1


low = jnp.bfloat16
wide = jnp.float32


def tie(tensor, *others):
    return lax.optimization_barrier((tensor,) + others)[0]


def plain(tensor):
    return with_layout_constraint(tensor, Layout(tuple(range(tensor.ndim))))


def ring_pairs(extent, hops=1):
    outer = extent // 2
    return [
        (2 * place + side, 2 * ((place + hops) % outer) + side)
        for place in range(outer)
        for side in range(2)
    ]


def swap_pairs(extent, stride):
    return [(place, place ^ stride) for place in range(extent)]


def rows_at(tensor, index, count):
    return lax.dynamic_slice_in_dim(tensor, index * count, count, 0)


def add(first, second, kind=low):
    return (first.astype(wide) + second.astype(wide)).astype(kind)


BLOCK = 128


def by_rows(body, side, rows, whole, outs, sums):
    length = rows[0].shape[0]

    def blocked(width):
        return pl.BlockSpec((BLOCK, width), lambda i: (i, 0))

    def kept(shape):
        return pl.BlockSpec(shape, lambda i: (0, 0))

    return pl.pallas_call(
        body,
        grid=(length // BLOCK,),
        in_specs=[pl.BlockSpec(memory_space=pltpu.SMEM)]
        + [blocked(t.shape[1]) for t in rows]
        + [kept(t.shape) for t in whole],
        out_specs=[blocked(width) for width, kind in outs] + [kept((1, width)) for width in sums],
        out_shape=[jax.ShapeDtypeStruct((length, width), kind) for width, kind in outs]
        + [jax.ShapeDtypeStruct((1, width), wide) for width in sums],
        compiler_params=pltpu.CompilerParams(vmem_limit_bytes=48 * 1024 * 1024),
    )(side, *rows, *whole)


def factor_of(value):
    return lax.rsqrt(jnp.mean(value * value, axis=-1, keepdims=True) + norm_eps)


def back_of(value, factor, gain, grad):
    scaled = grad * (1.0 + gain)
    shared = factor * factor * jnp.mean(scaled * value, axis=-1, keepdims=True)
    return factor * (scaled - shared * value), grad * (value * factor)


def add_up(ref, value):
    @pl.when(pl.program_id(0) == 0)
    def start():
        ref[...] = jnp.zeros_like(ref)

    ref[...] += jnp.sum(value, axis=0, keepdims=True)


def pieces_of(value, groups):
    count = value.shape[1] // groups
    return [value[:, k * count : (k + 1) * count] for k in range(groups)]


def turn(value, side, groups):
    cut = pieces_of(value, groups)
    even, odd = jnp.concatenate(cut[0::2], axis=1), jnp.concatenate(cut[1::2], axis=1)
    first, second = jnp.where(side == 0, even, odd), jnp.where(side == 0, odd, even)
    return jnp.concatenate([first, second], axis=1)


def straighten(value, side, groups):
    half = value.shape[1] // 2
    own, peer = value[:, :half], value[:, half:]
    even, odd = jnp.where(side == 0, own, peer), jnp.where(side == 0, peer, own)
    woven = zip(pieces_of(even, groups // 2), pieces_of(odd, groups // 2))
    return jnp.concatenate([cut for pair in woven for cut in pair], axis=1)


def start_body(groups, side, tokens, cotangent, valid, inputs, grad_out):
    inputs[...] = turn(tokens[...].astype(wide), side[0], groups).astype(low)
    grad_out[...] = turn(cotangent[...].astype(wide) * valid[...], side[0], groups).astype(low)


def normed_body(side, inputs, gains, normed):
    value = inputs[...].astype(wide)
    normed[...] = (value * factor_of(value) * (1.0 + gains[0:1])).astype(low)


def residual_of(inputs, attn, gains):
    value, mixed = inputs[...].astype(wide), attn[...].astype(wide)
    factor = factor_of(mixed)
    return value + mixed * factor * (1.0 + gains[1:2]), mixed, factor


def hidden_body(side, inputs, attn, gains, hidden):
    residual = residual_of(inputs, attn, gains)[0]
    hidden[...] = (residual * factor_of(residual) * (1.0 + gains[2:3])).astype(low)


def ffn_of(groups, ordered, place, own, first, last):
    own, first, last = (part[...].astype(wide) for part in (own, first, last))
    if ordered:
        return jnp.concatenate([own, first, last], axis=1)
    outer = groups // 2
    by_step = pieces_of(first, outer // 2) + pieces_of(last, outer // 2)
    peer = []
    for at in range(outer):
        block = by_step[(outer - 1 - at) % outer]
        for spot in range(outer - 1):
            block = jnp.where(place == spot, by_step[(spot - at) % outer], block)
        peer.append(block)
    return jnp.concatenate([own] + peer, axis=1)


def ffn_back_body(groups, ordered, spot, own, first, last, grad_out, gains, grad_own, grad_peer, grad_gain):
    ffn = ffn_of(groups, ordered, spot[1], own, first, last)
    grad, term = back_of(ffn, factor_of(ffn), gains[3:4], grad_out[...].astype(wide))
    half = ffn.shape[1] // 2
    grad_own[...] = grad[:, :half].astype(low)
    grad_peer[...] = grad[:, half:].astype(low)
    add_up(grad_gain, term)


def out_body(groups, ordered, spot, inputs, attn, own, first, last, gains, out):
    ffn = ffn_of(groups, ordered, spot[1], own, first, last)
    value = residual_of(inputs, attn, gains)[0] + ffn * factor_of(ffn) * (1.0 + gains[3:4])
    out[...] = straighten(value, spot[0], groups).astype(low)


def attn_back_body(side, inputs, attn, grad_hidden, grad_out, gains, grad_resid, grad_attn, gain1, gain2):
    residual, mixed, factor = residual_of(inputs, attn, gains)
    grad, term2 = back_of(residual, factor_of(residual), gains[2:3], grad_hidden[...].astype(wide))
    grad = grad + grad_out[...].astype(wide)
    grad_resid[...] = grad
    back, term1 = back_of(mixed, factor, gains[1:2], grad)
    grad_attn[...] = back.astype(low)
    add_up(gain1, term1)
    add_up(gain2, term2)


def in_back_body(groups, side, inputs, grad_normed, grad_resid, gains, input_grad, gain0):
    value = inputs[...].astype(wide)
    grad, term = back_of(value, factor_of(value), gains[0:1], grad_normed[...].astype(wide))
    input_grad[...] = straighten(grad_resid[...] + grad, side[0], groups)
    add_up(gain0, term)


def rotate(tensor, cosine, sine):
    half_dim = tensor.shape[-1] // 2
    first = tensor[..., :half_dim]
    second = tensor[..., half_dim:]
    return jnp.concatenate(
        [first * cosine - second * sine, second * cosine + first * sine], axis=-1
    )


def layout(labels):
    length = labels.shape[0]
    places = jnp.arange(length, dtype=jnp.int32)
    same_seq = labels[:, None] == labels[None, :]
    earlier = places[None, :] < places[:, None]
    position = jnp.sum((same_seq & earlier).astype(jnp.int32), axis=1)
    allowed = (
        same_seq
        & (places[None, :] <= places[:, None])
        & (places[:, None] - places[None, :] < WINDOW)
    )
    half_dim = HEAD_DIM // 2
    freq = rope_base ** (-2.0 * jnp.arange(half_dim, dtype=jnp.float32) / HEAD_DIM)
    angle = position.astype(jnp.float32)[:, None] * freq[None, :]
    return (allowed, jnp.cos(angle)[:, None, :], jnp.sin(angle)[:, None, :])


def scores(queries, key_rows, allowed):
    raw_scores = jnp.einsum("qkgd,skd->kgqs", queries, key_rows, preferred_element_type=jnp.float32)
    squashed = jnp.tanh(raw_scores / cap_value)
    capped = jnp.where(allowed[None, None], cap_value * squashed, -1e30)
    return (squashed, capped)


def rotate_back(grad_in, cosine, sine, shape_like):
    unused, pull = jax.vjp(lambda tensor: rotate(tensor, cosine, sine), shape_like)
    return pull(grad_in)[0]


def adam_step(master, gradient, moment, square, steps_done):
    new_moment = beta_one * moment + (1.0 - beta_one) * gradient
    new_square = beta_two * square + (1.0 - beta_two) * gradient * gradient
    fix_one = 1.0 - beta_one**steps_done
    fix_two = 1.0 - beta_two**steps_done
    stride = new_moment / fix_one / (jnp.sqrt(new_square / fix_two) + adam_eps)
    return (-learn_rate * (stride + decay_rate * master), new_moment, new_square)


def shards(
    tokens,
    segments,
    cotangent,
    query_weight,
    keyval_weight,
    output_weight,
    gateup_weight,
    down_weight,
    norm_gains,
    moment_query,
    moment_keyval,
    moment_output,
    moment_gateup,
    moment_down,
    moment_gains,
    square_query,
    square_keyval,
    square_output,
    square_gateup,
    square_down,
    square_gains,
):
    groups, parts = lax.axis_size("dp"), lax.axis_size("mp")
    outer = groups // 2
    index = lax.axis_index("dp")
    place = index // 2
    side = lax.rem(index, 2)
    spot = jnp.stack([side, place]).astype(jnp.int32)
    length, features = tokens.shape
    half = features // 2
    count = features // groups
    group = HEADS // KV_HEADS
    width_q, width_kv = query_weight.shape[1], keyval_weight.shape[2]
    width_qkv = width_q + 2 * width_kv
    width_mixer = width_qkv + output_weight.shape[0]
    width_ff = down_weight.shape[0]
    kv_local = width_kv // HEAD_DIM
    heads_local = kv_local * group
    qscale = HEAD_DIM ** (-0.5)
    core = lax.rem(lax.axis_index("mp"), 2)
    paired = outer == 4 and parts == 4

    def dot(pattern, first, second):
        return jnp.einsum(pattern, first, second, preferred_element_type=wide)

    def around(tensor, hops=1):
        return lax.ppermute(tensor, "dp", ring_pairs(groups, hops))

    def swap(tensor):
        return lax.ppermute(tensor, "dp", swap_pairs(groups, 1))

    def near(tensor):
        return lax.ppermute(tensor, "mp", swap_pairs(parts, 1))

    def far(tensor):
        return lax.ppermute(tensor, "mp", swap_pairs(parts, 2))

    def apart(partial_sum):
        rows = length // 2
        return rows_at(partial_sum, 1 - core, rows), rows_at(partial_sum, core, rows)

    def together(mine, theirs):
        first = jnp.where(core == 0, mine, theirs)
        second = jnp.where(core == 0, theirs, mine)
        return jnp.concatenate([first, second], axis=0)

    allowed, cosine, sine = layout(segments)
    valid = (segments >= 0).astype(wide)[:, None]

    def projections(inputs, weights, gains):
        (normed_low,) = by_rows(normed_body, spot, [inputs], [gains], [(features, low)], [])
        mixer_raw = dot("td,de->te", normed_low, weights[:, :width_qkv])
        qraw = mixer_raw[:, :width_q].reshape(length, heads_local, HEAD_DIM)
        kraw = mixer_raw[:, width_q : width_q + width_kv].reshape(length, kv_local, HEAD_DIM)
        queries = (
            (rotate(qraw, cosine, sine) * qscale).astype(low).reshape(length, kv_local, group, HEAD_DIM)
        )
        key_rows = rotate(kraw, cosine, sine).astype(low)
        value_rows = mixer_raw[:, width_q + width_kv :].astype(low).reshape(length, kv_local, HEAD_DIM)
        return normed_low, queries, key_rows, value_rows

    def attention(projected, weights):
        unused, queries, key_rows, value_rows = projected
        squashed, capped = scores(queries, key_rows, allowed)
        row_top = jnp.max(capped, axis=-1, keepdims=True)
        log_total = row_top + jnp.log(jnp.sum(jnp.exp(capped - row_top), axis=-1, keepdims=True))
        probs = jnp.exp(capped - log_total)
        probs_low = probs.astype(low)
        mixed_low = dot("kgqs,skd->qkgd", probs_low, value_rows).astype(low)
        mixed_low = mixed_low.reshape(length, heads_local * HEAD_DIM)
        attn_part = dot("te,de->td", mixed_low, weights[:, width_qkv:]).astype(low)
        return attn_part, projected + (squashed, probs, probs_low, mixed_low)

    def attention_back(grad_attn, weights, saved):
        normed_low, queries, key_rows, value_rows, squashed, probs, probs_low, mixed_low = saved
        grad_mixed = dot("td,de->te", grad_attn, weights[:, width_qkv:]).astype(low)
        grad_mixed = grad_mixed.reshape(length, kv_local, group, HEAD_DIM)
        grad_probs = dot("qkgd,skd->kgqs", grad_mixed, value_rows)
        grad_value = dot("kgqs,qkgd->skd", probs_low, grad_mixed)
        grad_value = grad_value.astype(low).reshape(length, kv_local * HEAD_DIM)
        grad_capped = probs * (grad_probs - jnp.sum(probs * grad_probs, axis=-1, keepdims=True))
        grad_scores = (grad_capped * (1.0 - squashed * squashed)).astype(low)
        grad_query = dot("kgqs,skd->qkgd", grad_scores, key_rows)
        grad_query = grad_query.reshape(length, heads_local, HEAD_DIM) * qscale
        shape_q = jnp.zeros((length, heads_local, HEAD_DIM), wide)
        grad_qraw = rotate_back(grad_query, cosine, sine, shape_q).astype(low)
        grad_key = dot("kgqs,qkgd->skd", grad_scores, queries)
        shape_k = jnp.zeros((length, kv_local, HEAD_DIM), wide)
        grad_kraw = rotate_back(grad_key, cosine, sine, shape_k).astype(low)
        flat = [t.reshape(length, -1) for t in (grad_qraw, grad_kraw, grad_value)]
        return plain(jnp.concatenate(flat, axis=1))

    def gated(gate_in, up_in):
        return jax.nn.gelu(gate_in, approximate=True) * up_in

    def weight_grad(first, second):
        return plain(dot("td,te->de", first, second).astype(low))

    def ffn_back(ffn_parts, grad_out, gains, ordered):
        body = partial(ffn_back_body, groups, ordered)
        return by_rows(body, spot, [*ffn_parts, grad_out], [gains], [(half, low)] * 2, [features])

    def layer_out(inputs, attn_sum, ffn_parts, gains, ordered):
        rows = [inputs, attn_sum, *ffn_parts]
        return by_rows(partial(out_body, groups, ordered), spot, rows, [gains], [(features, low)], [])[0]

    def attn_back(inputs, attn_sum, grad_hidden, grad_out, gains):
        rows = [inputs, attn_sum, grad_hidden, grad_out]
        outs = [(features, wide), (features, low)]
        return by_rows(attn_back_body, spot, rows, [gains], outs, [features] * 2)

    def in_back(inputs, grad_normed, grad_resid, gains):
        rows = [inputs, grad_normed, grad_resid]
        return by_rows(partial(in_back_body, groups), spot, rows, [gains], [(features, wide)], [features])

    steps_done = float(ADAM_STEP)

    def updated(master, total, moment, square):
        return (total,) + adam_step(master, total, moment, square, steps_done)

    def update_gate_up(sums):
        return updated(gateup_weight, jnp.stack(sums), moment_gateup, square_gateup)

    def update_down(total):
        return updated(down_weight.T, total, moment_down.T, square_down.T)

    def update_mixer(total):
        total = plain(total)
        sum_k, sum_v = total[:, width_q : width_q + width_kv], total[:, width_q + width_kv : width_qkv]
        return (
            updated(query_weight, total[:, :width_q], moment_query, square_query),
            updated(keyval_weight, jnp.stack([sum_k, sum_v]), moment_keyval, square_keyval),
            updated(output_weight.T, total[:, width_qkv:], moment_output.T, square_output.T),
        )

    gain_row = norm_gains.astype(low).reshape(1, 4 * count)
    mixer = jnp.concatenate(
        [
            query_weight.astype(low),
            keyval_weight[0].astype(low),
            keyval_weight[1].astype(low),
            output_weight.astype(low).T,
        ],
        axis=1,
    )
    mixer = jnp.concatenate([mixer, jnp.pad(gain_row, ((0, 15), (0, width_mixer - 4 * count)))], axis=0)
    mixer = plain(mixer)

    def source(step):
        return lax.rem(place - step + outer, outer)

    def put(full, piece, step, offset=0):
        return lax.dynamic_update_slice_in_dim(full, piece, source(step) * count + offset, 0)

    def gains_of(held, peer):
        gain_low = jnp.zeros((2, outer, 4, count), low)
        for at, pieces in enumerate((held, peer)):
            for step, piece in enumerate(pieces):
                gain_piece = piece[count, : 4 * count].reshape(1, 1, 4, count)
                gain_low = lax.dynamic_update_slice(gain_low, gain_piece, (at, source(step), 0, 0))
        return jnp.moveaxis(gain_low.reshape(groups, 4, count), 1, 0).reshape(4, features).astype(wide)

    def start(tokens_in, cotangent_in):
        return by_rows(
            partial(start_body, groups), spot, [tokens_in, cotangent_in, valid], [], [(features, low)] * 2, []
        )

    clock = [jnp.broadcast_to(valid[:8], (8, 128))]

    def sync(values):
        values, clock[0] = lax.optimization_barrier((values, clock[0]))
        return values

    always = index < groups

    def whole(work, *values):
        shapes = jax.eval_shape(work, *values)

        def blank(*unused):
            return jax.tree.map(lambda t: jnp.zeros(t.shape, t.dtype), shapes)

        return lax.cond(always, work, blank, *values)

    def behind(*values):
        values, clock[0] = lax.optimization_barrier((values, clock[0] * 0.5))
        return values

    gate, up = plain(gateup_weight[0].astype(low)), plain(gateup_weight[1].astype(low))
    down = plain(down_weight.astype(low).T)

    def down_part(act_low, weights):
        return dot("tf,df->td", act_low, weights).astype(low)

    def act_back(grad_own, grad_peer, gate_out, up_out, wd_own, wd_peer):
        grad_act = dot("td,df->tf", grad_own, wd_own) + dot("td,df->tf", grad_peer, wd_peer)
        unused, pull_act = jax.vjp(gated, gate_out, up_out)
        return tuple(grad.astype(low) for grad in pull_act(grad_act))

    def hidden_back(grad_gate, grad_up, wg, wu):
        return (dot("tf,df->td", grad_gate, wg) + dot("tf,df->td", grad_up, wu)).astype(low)

    def results(block_out, input_grad, new_mixer, new_gate_up, new_down, sum_gains):
        new_query, new_keyval, new_output = new_mixer
        new_gains = updated(norm_gains, sum_gains, moment_gains, square_gains)
        turned_back = [tuple(t.T for t in group_of) for group_of in (new_output, new_down)]
        new = (new_query, new_keyval, turned_back[0], new_gate_up, turned_back[1], new_gains)
        return (block_out, input_grad) + tuple(new[at][kind] for kind in range(4) for at in range(6))

    def simple():
        def gathered(own):
            rows = lax.all_gather(own, "dp", axis=0, tiled=True).reshape(outer, 2, -1, own.shape[1])
            return jnp.moveaxis(jnp.where(side == 0, rows, rows[:, ::-1]), 1, 0)

        def whole_rows(own):
            return gathered(own).reshape(features, own.shape[1])

        def scattered(rows):
            rows = rows.astype(wide).reshape(2, outer, count, rows.shape[1])
            rows = jnp.moveaxis(jnp.where(side == 0, rows, rows[::-1]), 0, 1).reshape(features, -1)
            return lax.psum_scatter(rows, "dp", scatter_dimension=0, tiled=True)

        def over_heads(part):
            return lax.psum(part.astype(wide), "mp").astype(low)

        rows = gathered(mixer)
        full = rows[:, :, :count].reshape(features, width_mixer)
        gains = jnp.moveaxis(rows[:, :, count, : 4 * count].reshape(groups, 4, count), 1, 0)
        gains = gains.reshape(4, features).astype(wide)
        wg, wu, wd = whole_rows(gate), whole_rows(up), whole_rows(down)
        inputs, grad_out = start(tokens, cotangent)
        attn_part, saved = attention(projections(inputs, full, gains), full)
        attn_sum = over_heads(attn_part)
        (hidden_in,) = by_rows(hidden_body, spot, [inputs, attn_sum], [gains], [(features, low)], [])
        gate_out, up_out = dot("td,df->tf", hidden_in, wg), dot("td,df->tf", hidden_in, wu)
        act_low = gated(gate_out, up_out).astype(low)
        ffn = over_heads(down_part(act_low, wd))
        ffn_parts = ffn[:, :half], ffn[:, half : half + half // 2], ffn[:, half + half // 2 :]
        block_out = layer_out(inputs, attn_sum, ffn_parts, gains, True)
        grad_own, grad_peer, gain3 = ffn_back(ffn_parts, grad_out, gains, True)
        grad_gate, grad_up = act_back(grad_own, grad_peer, gate_out, up_out, wd[:half], wd[half:])
        sum_down = scattered(weight_grad(jnp.concatenate([grad_own, grad_peer], axis=1), act_low))
        sums = [scattered(weight_grad(hidden_in, grad)) for grad in (grad_gate, grad_up)]
        grad_hidden = over_heads(hidden_back(grad_gate, grad_up, wg, wu))
        grad_resid, grad_attn, gain1, gain2 = attn_back(inputs, attn_sum, grad_hidden, grad_out, gains)
        grad_raw = attention_back(grad_attn, full, saved)
        grads = weight_grad(saved[0], grad_raw), weight_grad(grad_attn, saved[-1])
        sum_mixer = scattered(jnp.concatenate(grads, axis=1))
        grad_normed = over_heads(dot("te,de->td", grad_raw, full[:, :width_qkv]))
        input_grad, gain0 = in_back(inputs, grad_normed, grad_resid, gains)
        sum_gains = scattered(jnp.concatenate([gain0, gain1, gain2, gain3], axis=0).T).T
        return results(
            block_out, input_grad, update_mixer(sum_mixer), update_gate_up(sums), update_down(sum_down), sum_gains
        )

    if not paired:
        return simple()
    cut = count // 2

    m1, n0 = around(mixer), swap(mixer)
    inputs, grad_out = start(tokens, cotangent)
    m1, n0, mixer = sync((m1, n0, mixer))
    m2, n1 = around(m1), swap(m1)
    full = put(put(jnp.zeros((features, width_mixer), low), mixer[:count], 0), n0[:count], 0, half)
    wg, wu = jnp.zeros((features, width_ff), low), jnp.zeros((features, width_ff), low)
    m2, n1, m1, full, gate, up, wg, wu, allowed, cosine, sine = sync(
        (m2, n1, m1, full, gate, up, wg, wu, allowed, cosine, sine)
    )
    m3, n2 = around(m2), swap(m2)
    full = put(put(full, m1[:count], 1), n1[:count], 1, half)
    m3, n2, m2, full, gate, up, down = sync((m3, n2, m2, full, gate, up, down))
    g1, n3, down_far = around(gate), swap(m3), swap(down[cut:])
    full = put(put(full, m2[:count], 2), n2[:count], 2, half)
    wg = put(wg, gate, 0)
    wu = put(wu, up, 0)
    n3, m3, g1, down_far, full, gate, up, wg, wu, inputs, grad_out = sync(
        (n3, m3, g1, down_far, full, gate, up, wg, wu, inputs, grad_out)
    )
    u1, g2, h0, v0 = around(up), around(g1), swap(gate), swap(up)

    def attend(inputs, full, m3, n3, gains):
        full = put(put(full, m3[:count], 3), n3[:count], 3, half)
        attn_part, saved = attention(projections(inputs, full, gains), full)
        return apart(attn_part) + (saved, full)

    gains = gains_of((mixer, m1, m2, m3), (n0, n1, n2, n3))
    given, kept, saved, full = whole(attend, inputs, full, m3, n3, gains)
    given, kept, u1, g1, g2, v0, h0, saved, gains = sync((given, kept, u1, g1, g2, v0, h0, saved, gains))
    u2, g3, h1, v1 = around(u1), around(g2), swap(g1), swap(u1)
    kept = add(kept, near(given))
    across = far(kept)
    wg, wu, h0, v0, u1, g1 = behind(wg, wu, h0, v0, u1, g1)
    wg = put(put(wg, g1, 1), h0, 0, half)
    wu = put(put(wu, u1, 1), v0, 0, half)
    u2, g2, g3, h1, v1, across, kept, wg, wu, down = sync((u2, g2, g3, h1, v1, across, kept, wg, wu, down))
    u3, d1, h2, v2 = around(u2), around(down), swap(g2), swap(u2)
    mine = add(kept, across)
    attn_sum = together(mine, near(mine))
    (hidden_in,) = by_rows(hidden_body, spot, [inputs, attn_sum], [gains], [(features, low)], [])
    wg = put(put(wg, g2, 2), h1, 1, half)
    wu = put(put(wu, u2, 2), v1, 1, half)
    u3, g3, d1, h2, v2, hidden_in, wg, wu = sync((u3, g3, d1, h2, v2, hidden_in, wg, wu))
    d2, h3 = around(d1), swap(g3)
    v3 = swap(tie(u3, h3))
    wg, wu, h2, v2, u3, g3 = behind(wg, wu, h2, v2, u3, g3)
    wg = put(put(wg, g3, 3), h2, 2, half)
    wu = put(put(wu, u3, 3), v2, 2, half)
    wd_own = put(put(jnp.zeros((half, width_ff), low), down, 0), d1, 1)
    wd_peer = jnp.zeros((half, width_ff), low)
    d3 = around(d2)
    wg = put(wg, h3, 3, half)
    gate_out = dot("td,df->tf", hidden_in, wg)
    down_cut, d1_cut = down[:cut], d1[:cut]
    d2, d3, v3, wg, gate_out, wu, wd_own, wd_peer, down_cut, d1_cut, down_far = sync(
        (d2, d3, v3, wg, gate_out, wu, wd_own, wd_peer, down_cut, d1_cut, down_far)
    )
    f1, e0, e1 = around(down_far), swap(down_cut), swap(d1_cut)
    wu, v3 = behind(wu, v3)
    wu = put(wu, v3, 3, half)
    up_out = dot("td,df->tf", hidden_in, wu)
    act_low = gated(gate_out, up_out).astype(low)
    wd_own = put(put(wd_own, d2, 2), d3, 3)
    d2_cut, d3_cut = d2[:cut], d3[:cut]
    given, kept = apart(down_part(act_low, wd_own))
    f1, e0, e1, act_low, given, kept, d2_cut, d3_cut, wd_peer = sync(
        (f1, e0, e1, act_low, given, kept, d2_cut, d3_cut, wd_peer)
    )
    f2, e2, e3 = around(f1), swap(d2_cut), swap(d3_cut)
    kept = add(kept, near(given))
    across = far(kept)
    f3 = around(tie(f2, kept))
    first_rows = jnp.concatenate([e0, down_far, e1, f1], axis=0)
    given, kept_first = apart(down_part(act_low, first_rows))
    kept_first = add(kept_first, near(given))
    across_first = far(tie(kept_first, kept))
    wd_peer = put(put(put(put(wd_peer, e0, 0), down_far, 0, cut), e1, 1), f1, 1, cut)
    f2, f3, e2, e3, across, kept, across_first, kept_first, wd_peer = sync(
        (f2, f3, e2, e3, across, kept, across_first, kept_first, wd_peer)
    )
    last_rows = jnp.concatenate([e2, f2, e3, f3], axis=0)
    given, kept_last = apart(down_part(act_low, last_rows))
    kept_last = add(kept_last, near(given))
    across_last = far(kept_last)
    ffn_parts = []
    for held, came in ((kept, across), (kept_first, across_first), (kept_last, across_last)):
        mine = add(held, came)
        ffn_parts.append(together(mine, near(mine)))
    wd_peer = put(put(put(put(wd_peer, e2, 2), f2, 2, cut), e3, 3), f3, 3, cut)

    def piece(tensor, hops):
        return rows_at(tensor, lax.rem(place + hops, outer), count)

    def plus(own, arrived, total=None, kind=low):
        both = own.astype(wide) + arrived.astype(wide)
        if total is not None:
            both = both + total.astype(wide)
        return both.astype(kind)

    def pieces(tensor):
        return [piece(tensor, hops) for hops in (3, 2, 1, 0)]

    def rows_of(tensor, offset, rows):
        starts = [lax.rem(place + hops, outer) * count + offset for hops in (3, 2, 1, 0)]
        return [lax.dynamic_slice_in_dim(tensor, first, rows, 0) for first in starts]

    def both(hops, offset, tensors):
        target = lax.rem(place + hops, outer) * count + offset
        cuts = [lax.dynamic_slice_in_dim(t, target, count, 0) for t in tensors]
        return plain(jnp.concatenate(cuts, axis=1))

    grad_ffn_own, grad_ffn_peer, grad_gain3 = ffn_back(ffn_parts, grad_out, gains, False)
    wd_grad = weight_grad(grad_ffn_peer, act_low)
    cut = count * 7 // 18 // 16 * 16
    sent, far_parts = jnp.concatenate(rows_of(wd_grad, 0, cut), axis=0), rows_of(wd_grad, cut, count - cut)
    sent, far_parts, grad_ffn_own, grad_ffn_peer, wd_peer = sync(
        (sent, far_parts, grad_ffn_own, grad_ffn_peer, wd_peer)
    )

    arrived, f3 = swap(sent), around(far_parts[0])

    def act_step(grad_own, grad_peer, gate_out, up_out, act_low, hidden_in, wd_own, wd_peer):
        grad_gate, grad_up = act_back(grad_own, grad_peer, gate_out, up_out, wd_own, wd_peer)
        gate_sent = pieces(weight_grad(hidden_in[:, half:], grad_gate))
        return grad_gate, grad_up, weight_grad(grad_own, act_low), gate_sent

    grad_gate, grad_up, wd_grad, gate_sent = whole(
        act_step, grad_ffn_own, grad_ffn_peer, gate_out, up_out, act_low, hidden_in, wd_own, wd_peer
    )
    arrived, f3, grad_gate, grad_up, wd_grad, gate_sent, far_parts = sync(
        (arrived, f3, grad_gate, grad_up, wd_grad, gate_sent, far_parts)
    )

    def grown(at):
        return jnp.pad(arrived[at * cut : (at + 1) * cut], ((0, count - cut), (0, 0)))

    h3 = swap(gate_sent[0])
    came = around(plus(piece(wd_grad, 3), grown(0)))
    f2 = around(add(far_parts[1], f3))

    def hidden_step(grad_gate, grad_up, wg, wu):
        return apart(hidden_back(grad_gate, grad_up, wg, wu))

    given, kept = whole(hidden_step, grad_gate, grad_up, wg, wu)
    h3, came, f2, given, kept, gate_sent, grad_gate, grad_up = sync(
        (h3, came, f2, given, kept, gate_sent, grad_gate, grad_up)
    )
    h2, theirs = swap(gate_sent[1]), near(given)
    came = around(plus(piece(wd_grad, 2), grown(1), came))

    def rest_of_grads(grad_gate, grad_up, hidden_in, gate_sent, h3):
        up_sent = pieces(weight_grad(hidden_in[:, half:], grad_up))
        wg_grad = weight_grad(hidden_in[:, :half], grad_gate)
        mixed_sent = [jnp.concatenate(pair, axis=0) for pair in zip(gate_sent[2:], up_sent[:2])]
        gate_first = plus(piece(wg_grad, 3), h3)
        return mixed_sent, up_sent[2:], wg_grad, weight_grad(hidden_in[:, :half], grad_up), gate_first

    mixed_sent, up_sent, wg_grad, wu_grad, gate_first = whole(
        rest_of_grads, grad_gate, grad_up, hidden_in, gate_sent, h3
    )
    h2, theirs, came, mixed_sent, up_sent, wg_grad, wu_grad, kept, gate_first = sync(
        (h2, theirs, came, mixed_sent, up_sent, wg_grad, wu_grad, kept, gate_first)
    )
    pair = swap(mixed_sent[0])
    kept = add(kept, theirs)
    across = far(kept)
    came = around(plus(piece(wd_grad, 1), grown(2), came))
    gate_came = around(gate_first)
    across, pair, came, gate_came, kept, mixed_sent[1], up_sent, f2 = sync(
        (across, pair, came, gate_came, kept, mixed_sent[1], up_sent, f2)
    )
    h1, v3 = pair[:count], pair[count:]
    pair = swap(mixed_sent[1])
    mine = add(kept, across)
    theirs = near(mine)
    gate_came = around(plus(piece(wg_grad, 2), h2, gate_came))
    up_came = around(plus(piece(wu_grad, 3), v3))
    f1 = around(add(far_parts[2], f2))

    def mixer_back(inputs, attn_sum, mine, theirs, grad_out, gains, full, saved):
        grad_hidden = together(mine, theirs)
        grad_resid, grad_attn, gain1, gain2 = attn_back(inputs, attn_sum, grad_hidden, grad_out, gains)
        grad_raw = attention_back(grad_attn, full, saved)
        given, kept = apart(dot("te,de->td", grad_raw, full[:, :width_qkv]).astype(low))
        return given, kept, grad_resid, grad_attn, gain1, gain2, grad_raw

    given, kept, grad_resid, grad_attn, grad_gain1, grad_gain2, grad_raw = whole(
        mixer_back, inputs, attn_sum, mine, theirs, grad_out, gains, full, saved
    )
    pair, gate_came, up_came, f1, given, kept, grad_resid, grad_attn, grad_raw, up_sent = sync(
        (pair, gate_came, up_came, f1, given, kept, grad_resid, grad_attn, grad_raw, up_sent)
    )
    h0, v2 = pair[:count], pair[count:]
    v1, theirs = swap(up_sent[0]), near(given)
    gate_came = around(plus(piece(wg_grad, 1), h1, gate_came))

    def mixer_grads(normed_low, mixed_low, grad_raw, grad_attn):
        grads = weight_grad(normed_low, grad_raw), weight_grad(grad_attn, mixed_low)
        pairs = ((3, 2), (1, 0))
        mixer_sent = [jnp.concatenate([both(hops, half, grads) for hops in pair], axis=0) for pair in pairs]
        return mixer_sent, [both(hops, 0, grads) for hops in (3, 2, 1, 0)]

    mixer_sent, mixer_own = whole(mixer_grads, saved[0], saved[-1], grad_raw, grad_attn)
    v1, theirs, gate_came, mixer_sent, mixer_own, kept, up_sent = sync(
        (v1, theirs, gate_came, mixer_sent, mixer_own, kept, up_sent)
    )
    v0, x32 = swap(up_sent[1]), swap(mixer_sent[0])
    kept = add(kept, theirs)
    across = far(kept)
    up_came = around(plus(piece(wu_grad, 2), v2, up_came))
    gate_late = tie(gate_came, up_came)
    sum_gate = plus(piece(wg_grad, 0), h0, gate_late, wide)
    up_came = around(plus(piece(wu_grad, 1), v1, up_came))
    v0, x32, up_came, across, kept, mixer_sent[1], inputs, f1, sum_gate = sync(
        (v0, x32, up_came, across, kept, mixer_sent[1], inputs, f1, sum_gate)
    )
    x10, b_far = swap(mixer_sent[1]), swap(add(far_parts[3], f1))
    m3 = around(plus(mixer_own[0], x32[:count]), 3)
    m2 = around(plus(mixer_own[1], x32[count:]), 2)
    mine = add(kept, across)
    theirs = near(mine)

    def finish(inputs, mine, theirs, grad_resid, attn_sum, ffn_parts, gains):
        block_out = layer_out(inputs, attn_sum, ffn_parts, gains, False)
        input_grad, gain0 = in_back(inputs, together(mine, theirs), grad_resid, gains)
        return block_out, input_grad, gain0

    block_out, input_grad, grad_gain0 = whole(
        finish, inputs, mine, theirs, grad_resid, attn_sum, ffn_parts, gains
    )
    x10, b_far, m3, m2, block_out, input_grad, grad_gain0 = sync(
        (x10, b_far, m3, m2, block_out, input_grad, grad_gain0)
    )
    mixed = plus(mixer_own[2], x10[:count])
    m1 = around(mixed)
    came = tie(came, mixed)
    grad_gains = jnp.concatenate([grad_gain0, grad_gain1, grad_gain2, grad_gain3], axis=0)
    gain_sum = grad_gains[:, :half] + swap(grad_gains[:, half:])
    gain_sum = gain_sum.reshape(4, outer, count)
    down_total = plus(piece(wd_grad, 0), jnp.concatenate([arrived[3 * cut :], b_far], axis=0), came, wide)
    new_down = update_down(behind(down_total)[0])
    sum_up = plus(piece(wu_grad, 0), v0, up_came, wide)
    new_gate_up = update_gate_up([sum_gate, sum_up])
    sum_gains = lax.dynamic_index_in_dim(gain_sum, place, 1, False)
    for hops in (1, 2, 3):
        given = lax.dynamic_index_in_dim(gain_sum, lax.rem(place + hops, outer), 1, False)
        sum_gains = sum_gains + around(given, hops)
    m1, sum_gains, new_down, new_gate_up = sync((m1, sum_gains, new_down, new_gate_up))
    sum_mixer = plus(mixer_own[3], x10[count:], m1, wide) + m2.astype(wide) + m3.astype(wide)
    return results(block_out, input_grad, update_mixer(sum_mixer), new_gate_up, new_down, sum_gains)


def solution(mesh):
    return jax.shard_map(
        shards,
        mesh=mesh,
        in_specs=(
            P("dp", None),
            P("dp"),
            P("dp", None),
            P("dp", "mp"),
            P(None, "dp", "mp"),
            P("mp", "dp"),
            P(None, "dp", "mp"),
            P("mp", "dp"),
            P(None, "dp"),
            P("dp", "mp"),
            P(None, "dp", "mp"),
            P("mp", "dp"),
            P(None, "dp", "mp"),
            P("mp", "dp"),
            P(None, "dp"),
            P("dp", "mp"),
            P(None, "dp", "mp"),
            P("mp", "dp"),
            P(None, "dp", "mp"),
            P("mp", "dp"),
            P(None, "dp"),
        ),
        out_specs=(
            P("dp", None),
            P("dp", None),
            P("dp", "mp"),
            P(None, "dp", "mp"),
            P("mp", "dp"),
            P(None, "dp", "mp"),
            P("mp", "dp"),
            P(None, "dp"),
            P("dp", "mp"),
            P(None, "dp", "mp"),
            P("mp", "dp"),
            P(None, "dp", "mp"),
            P("mp", "dp"),
            P(None, "dp"),
            P("dp", "mp"),
            P(None, "dp", "mp"),
            P("mp", "dp"),
            P(None, "dp", "mp"),
            P("mp", "dp"),
            P(None, "dp"),
            P("dp", "mp"),
            P(None, "dp", "mp"),
            P("mp", "dp"),
            P(None, "dp", "mp"),
            P("mp", "dp"),
            P(None, "dp"),
        ),
        check_vma=False,
    )
```

```python
from functools import partial

import jax
import jax.numpy as jnp
from jax import lax
from jax.experimental import pallas as pl
from jax.experimental.layout import Layout, with_layout_constraint
from jax.experimental.pallas import tpu as pltpu
from jax.sharding import PartitionSpec as P

HEADS = 8
KV_HEADS = 4
HEAD_DIM = 256
WINDOW = 4096
ADAM_STEP = 5


norm_eps = 1e-06
cap_value = 50.0
rope_base = 10000.0
learn_rate = 0.1
beta_one = 0.9
beta_two = 0.95
adam_eps = 1e-08
decay_rate = 0.1


low = jnp.bfloat16
wide = jnp.float32


def tie(tensor, *others):
    return lax.optimization_barrier((tensor,) + others)[0]


def plain(tensor):
    return with_layout_constraint(tensor, Layout(tuple(range(tensor.ndim))))


def ring_pairs(extent, hops=1):
    outer = extent // 2
    return [
        (2 * place + side, 2 * ((place + hops) % outer) + side)
        for place in range(outer)
        for side in range(2)
    ]


def swap_pairs(extent, stride):
    return [(place, place ^ stride) for place in range(extent)]


def rows_at(tensor, index, count):
    return lax.dynamic_slice_in_dim(tensor, index * count, count, 0)


def add(first, second, kind=low):
    return (first.astype(wide) + second.astype(wide)).astype(kind)


BLOCK = 224


def by_rows(body, side, rows, whole, outs, sums):
    length = rows[0].shape[0]

    def blocked(width):
        return pl.BlockSpec((BLOCK, width), lambda i: (i, 0))

    def kept(shape):
        return pl.BlockSpec(shape, lambda i: (0, 0))

    return pl.pallas_call(
        body,
        grid=(length // BLOCK,),
        in_specs=[pl.BlockSpec(memory_space=pltpu.SMEM)]
        + [blocked(t.shape[1]) for t in rows]
        + [kept(t.shape) for t in whole],
        out_specs=[blocked(width) for width, kind in outs] + [kept((1, width)) for width in sums],
        out_shape=[jax.ShapeDtypeStruct((length, width), kind) for width, kind in outs]
        + [jax.ShapeDtypeStruct((1, width), wide) for width in sums],
        compiler_params=pltpu.CompilerParams(vmem_limit_bytes=48 * 1024 * 1024),
    )(side, *rows, *whole)


def factor_of(value):
    return lax.rsqrt(jnp.mean(value * value, axis=-1, keepdims=True) + norm_eps)


def back_of(value, factor, gain, grad):
    scaled = grad * (1.0 + gain)
    shared = factor * factor * jnp.mean(scaled * value, axis=-1, keepdims=True)
    return factor * (scaled - shared * value), grad * (value * factor)


def add_up(ref, value):
    @pl.when(pl.program_id(0) == 0)
    def start():
        ref[...] = jnp.zeros_like(ref)

    ref[...] += jnp.sum(value, axis=0, keepdims=True)


def pieces_of(value, groups):
    count = value.shape[1] // groups
    return [value[:, k * count : (k + 1) * count] for k in range(groups)]


def turn(value, side, groups):
    cut = pieces_of(value, groups)
    even, odd = jnp.concatenate(cut[0::2], axis=1), jnp.concatenate(cut[1::2], axis=1)
    first, second = jnp.where(side == 0, even, odd), jnp.where(side == 0, odd, even)
    return jnp.concatenate([first, second], axis=1)


def straighten(value, side, groups):
    half = value.shape[1] // 2
    own, peer = value[:, :half], value[:, half:]
    even, odd = jnp.where(side == 0, own, peer), jnp.where(side == 0, peer, own)
    woven = zip(pieces_of(even, groups // 2), pieces_of(odd, groups // 2))
    return jnp.concatenate([cut for pair in woven for cut in pair], axis=1)


def start_body(groups, side, tokens, cotangent, valid, inputs, grad_out):
    inputs[...] = turn(tokens[...].astype(wide), side[0], groups).astype(low)
    grad_out[...] = turn(cotangent[...].astype(wide) * valid[...], side[0], groups).astype(low)


def normed_body(side, inputs, gains, normed):
    value = inputs[...].astype(wide)
    normed[...] = (value * factor_of(value) * (1.0 + gains[0:1])).astype(low)


def residual_of(inputs, attn, gains):
    value, mixed = inputs[...].astype(wide), attn[...].astype(wide)
    factor = factor_of(mixed)
    return value + mixed * factor * (1.0 + gains[1:2]), mixed, factor


def hidden_body(side, inputs, attn, gains, hidden):
    residual = residual_of(inputs, attn, gains)[0]
    hidden[...] = (residual * factor_of(residual) * (1.0 + gains[2:3])).astype(low)


def ffn_of(groups, ordered, place, own, first, last):
    own, first, last = (part[...].astype(wide) for part in (own, first, last))
    if ordered:
        return jnp.concatenate([own, first, last], axis=1)
    outer = groups // 2
    by_step = pieces_of(first, outer // 2) + pieces_of(last, outer // 2)
    peer = []
    for at in range(outer):
        block = by_step[(outer - 1 - at) % outer]
        for spot in range(outer - 1):
            block = jnp.where(place == spot, by_step[(spot - at) % outer], block)
        peer.append(block)
    return jnp.concatenate([own] + peer, axis=1)


def ffn_back_body(groups, ordered, spot, own, first, last, grad_out, gains, grad_own, grad_peer, grad_gain):
    ffn = ffn_of(groups, ordered, spot[1], own, first, last)
    grad, term = back_of(ffn, factor_of(ffn), gains[3:4], grad_out[...].astype(wide))
    half = ffn.shape[1] // 2
    grad_own[...] = grad[:, :half].astype(low)
    grad_peer[...] = grad[:, half:].astype(low)
    add_up(grad_gain, term)


def out_body(groups, ordered, spot, inputs, attn, own, first, last, gains, out):
    ffn = ffn_of(groups, ordered, spot[1], own, first, last)
    value = residual_of(inputs, attn, gains)[0] + ffn * factor_of(ffn) * (1.0 + gains[3:4])
    out[...] = straighten(value, spot[0], groups).astype(low)


def attn_back_body(side, inputs, attn, grad_hidden, grad_out, gains, grad_resid, grad_attn, gain1, gain2):
    residual, mixed, factor = residual_of(inputs, attn, gains)
    grad, term2 = back_of(residual, factor_of(residual), gains[2:3], grad_hidden[...].astype(wide))
    grad = grad + grad_out[...].astype(wide)
    grad_resid[...] = grad
    back, term1 = back_of(mixed, factor, gains[1:2], grad)
    grad_attn[...] = back.astype(low)
    add_up(gain1, term1)
    add_up(gain2, term2)


def in_back_body(groups, side, inputs, grad_normed, grad_resid, gains, input_grad, gain0):
    value = inputs[...].astype(wide)
    grad, term = back_of(value, factor_of(value), gains[0:1], grad_normed[...].astype(wide))
    input_grad[...] = straighten(grad_resid[...] + grad, side[0], groups)
    add_up(gain0, term)


def rotate(tensor, cosine, sine):
    half_dim = tensor.shape[-1] // 2
    first = tensor[..., :half_dim]
    second = tensor[..., half_dim:]
    return jnp.concatenate(
        [first * cosine - second * sine, second * cosine + first * sine], axis=-1
    )


def layout(labels):
    length = labels.shape[0]
    places = jnp.arange(length, dtype=jnp.int32)
    same_seq = labels[:, None] == labels[None, :]
    earlier = places[None, :] < places[:, None]
    position = jnp.sum((same_seq & earlier).astype(jnp.int32), axis=1)
    allowed = (
        same_seq
        & (places[None, :] <= places[:, None])
        & (places[:, None] - places[None, :] < WINDOW)
    )
    half_dim = HEAD_DIM // 2
    freq = rope_base ** (-2.0 * jnp.arange(half_dim, dtype=jnp.float32) / HEAD_DIM)
    angle = position.astype(jnp.float32)[:, None] * freq[None, :]
    return (allowed, jnp.cos(angle)[:, None, :], jnp.sin(angle)[:, None, :])


def scores(queries, key_rows, allowed):
    raw_scores = jnp.einsum("qkgd,skd->kgqs", queries, key_rows, preferred_element_type=jnp.float32)
    squashed = jnp.tanh(raw_scores / cap_value)
    capped = jnp.where(allowed[None, None], cap_value * squashed, -1e30)
    return (squashed, capped)


def rotate_back(grad_in, cosine, sine, shape_like):
    unused, pull = jax.vjp(lambda tensor: rotate(tensor, cosine, sine), shape_like)
    return pull(grad_in)[0]


def adam_step(master, gradient, moment, square, steps_done):
    new_moment = beta_one * moment + (1.0 - beta_one) * gradient
    new_square = beta_two * square + (1.0 - beta_two) * gradient * gradient
    fix_one = 1.0 - beta_one**steps_done
    fix_two = 1.0 - beta_two**steps_done
    stride = new_moment / fix_one / (jnp.sqrt(new_square / fix_two) + adam_eps)
    return (-learn_rate * (stride + decay_rate * master), new_moment, new_square)


def shards(
    tokens,
    segments,
    cotangent,
    query_weight,
    keyval_weight,
    output_weight,
    gateup_weight,
    down_weight,
    norm_gains,
    moment_query,
    moment_keyval,
    moment_output,
    moment_gateup,
    moment_down,
    moment_gains,
    square_query,
    square_keyval,
    square_output,
    square_gateup,
    square_down,
    square_gains,
):
    groups, parts = lax.axis_size("dp"), lax.axis_size("mp")
    outer = groups // 2
    index = lax.axis_index("dp")
    place = index // 2
    side = lax.rem(index, 2)
    spot = jnp.stack([side, place]).astype(jnp.int32)
    length, features = tokens.shape
    half = features // 2
    count = features // groups
    group = HEADS // KV_HEADS
    width_q, width_kv = query_weight.shape[1], keyval_weight.shape[2]
    width_qkv = width_q + 2 * width_kv
    width_mixer = width_qkv + output_weight.shape[0]
    width_ff = down_weight.shape[0]
    kv_local = width_kv // HEAD_DIM
    heads_local = kv_local * group
    qscale = HEAD_DIM ** (-0.5)
    core = lax.rem(lax.axis_index("mp"), 2)
    paired = outer == 4 and parts == 4

    def dot(pattern, first, second):
        return jnp.einsum(pattern, first, second, preferred_element_type=wide)

    def around(tensor, hops=1):
        return lax.ppermute(tensor, "dp", ring_pairs(groups, hops))

    def swap(tensor):
        return lax.ppermute(tensor, "dp", swap_pairs(groups, 1))

    def near(tensor):
        return lax.ppermute(tensor, "mp", swap_pairs(parts, 1))

    def far(tensor):
        return lax.ppermute(tensor, "mp", swap_pairs(parts, 2))

    def apart(partial_sum):
        rows = length // 2
        return rows_at(partial_sum, 1 - core, rows), rows_at(partial_sum, core, rows)

    def together(mine, theirs):
        first = jnp.where(core == 0, mine, theirs)
        second = jnp.where(core == 0, theirs, mine)
        return jnp.concatenate([first, second], axis=0)

    allowed, cosine, sine = layout(segments)
    valid = (segments >= 0).astype(wide)[:, None]

    def projections(inputs, weights, gains):
        (normed_low,) = by_rows(normed_body, spot, [inputs], [gains], [(features, low)], [])
        mixer_raw = dot("td,de->te", normed_low, weights[:, :width_qkv])
        qraw = mixer_raw[:, :width_q].reshape(length, heads_local, HEAD_DIM)
        kraw = mixer_raw[:, width_q : width_q + width_kv].reshape(length, kv_local, HEAD_DIM)
        queries = (
            (rotate(qraw, cosine, sine) * qscale).astype(low).reshape(length, kv_local, group, HEAD_DIM)
        )
        key_rows = rotate(kraw, cosine, sine).astype(low)
        value_rows = mixer_raw[:, width_q + width_kv :].astype(low).reshape(length, kv_local, HEAD_DIM)
        return normed_low, queries, key_rows, value_rows

    def attention(projected, weights):
        unused, queries, key_rows, value_rows = projected
        squashed, capped = scores(queries, key_rows, allowed)
        row_top = jnp.max(capped, axis=-1, keepdims=True)
        log_total = row_top + jnp.log(jnp.sum(jnp.exp(capped - row_top), axis=-1, keepdims=True))
        probs = jnp.exp(capped - log_total)
        probs_low = probs.astype(low)
        mixed_low = dot("kgqs,skd->qkgd", probs_low, value_rows).astype(low)
        mixed_low = mixed_low.reshape(length, heads_local * HEAD_DIM)
        attn_part = dot("te,de->td", mixed_low, weights[:, width_qkv:]).astype(low)
        return attn_part, projected + (squashed, probs, probs_low, mixed_low)

    def attention_back(grad_attn, weights, saved):
        normed_low, queries, key_rows, value_rows, squashed, probs, probs_low, mixed_low = saved
        grad_mixed = dot("td,de->te", grad_attn, weights[:, width_qkv:]).astype(low)
        grad_mixed = grad_mixed.reshape(length, kv_local, group, HEAD_DIM)
        grad_probs = dot("qkgd,skd->kgqs", grad_mixed, value_rows)
        grad_value = dot("kgqs,qkgd->skd", probs_low, grad_mixed)
        grad_value = grad_value.astype(low).reshape(length, kv_local * HEAD_DIM)
        grad_capped = probs * (grad_probs - jnp.sum(probs * grad_probs, axis=-1, keepdims=True))
        grad_scores = (grad_capped * (1.0 - squashed * squashed)).astype(low)
        grad_query = dot("kgqs,skd->qkgd", grad_scores, key_rows)
        grad_query = grad_query.reshape(length, heads_local, HEAD_DIM) * qscale
        shape_q = jnp.zeros((length, heads_local, HEAD_DIM), wide)
        grad_qraw = rotate_back(grad_query, cosine, sine, shape_q).astype(low)
        grad_key = dot("kgqs,qkgd->skd", grad_scores, queries)
        shape_k = jnp.zeros((length, kv_local, HEAD_DIM), wide)
        grad_kraw = rotate_back(grad_key, cosine, sine, shape_k).astype(low)
        flat = [t.reshape(length, -1) for t in (grad_qraw, grad_kraw, grad_value)]
        return plain(jnp.concatenate(flat, axis=1))

    def gated(gate_in, up_in):
        return jax.nn.gelu(gate_in, approximate=True) * up_in

    def weight_grad(first, second):
        return plain(dot("td,te->de", first, second).astype(low))

    def ffn_back(ffn_parts, grad_out, gains, ordered):
        body = partial(ffn_back_body, groups, ordered)
        return by_rows(body, spot, [*ffn_parts, grad_out], [gains], [(half, low)] * 2, [features])

    def layer_out(inputs, attn_sum, ffn_parts, gains, ordered):
        rows = [inputs, attn_sum, *ffn_parts]
        return by_rows(partial(out_body, groups, ordered), spot, rows, [gains], [(features, low)], [])[0]

    def attn_back(inputs, attn_sum, grad_hidden, grad_out, gains):
        rows = [inputs, attn_sum, grad_hidden, grad_out]
        outs = [(features, wide), (features, low)]
        return by_rows(attn_back_body, spot, rows, [gains], outs, [features] * 2)

    def in_back(inputs, grad_normed, grad_resid, gains):
        rows = [inputs, grad_normed, grad_resid]
        return by_rows(partial(in_back_body, groups), spot, rows, [gains], [(features, wide)], [features])

    steps_done = float(ADAM_STEP)

    def updated(master, total, moment, square):
        return (total,) + adam_step(master, total, moment, square, steps_done)

    def update_gate_up(sums):
        return updated(gateup_weight, jnp.stack(sums), moment_gateup, square_gateup)

    def update_down(total):
        return updated(down_weight.T, total, moment_down.T, square_down.T)

    def update_mixer(total):
        total = plain(total)
        sum_k, sum_v = total[:, width_q : width_q + width_kv], total[:, width_q + width_kv : width_qkv]
        return (
            updated(query_weight, total[:, :width_q], moment_query, square_query),
            updated(keyval_weight, jnp.stack([sum_k, sum_v]), moment_keyval, square_keyval),
            updated(output_weight.T, total[:, width_qkv:], moment_output.T, square_output.T),
        )

    gain_row = norm_gains.astype(low).reshape(1, 4 * count)
    mixer = jnp.concatenate(
        [
            query_weight.astype(low),
            keyval_weight[0].astype(low),
            keyval_weight[1].astype(low),
            output_weight.astype(low).T,
        ],
        axis=1,
    )
    mixer = jnp.concatenate([mixer, jnp.pad(gain_row, ((0, 15), (0, width_mixer - 4 * count)))], axis=0)
    mixer = plain(mixer)

    def source(step):
        return lax.rem(place - step + outer, outer)

    def put(full, piece, step, offset=0):
        return lax.dynamic_update_slice_in_dim(full, piece, source(step) * count + offset, 0)

    def gains_of(held, peer):
        gain_low = jnp.zeros((2, outer, 4, count), low)
        for at, pieces in enumerate((held, peer)):
            for step, piece in enumerate(pieces):
                gain_piece = piece[count, : 4 * count].reshape(1, 1, 4, count)
                gain_low = lax.dynamic_update_slice(gain_low, gain_piece, (at, source(step), 0, 0))
        return jnp.moveaxis(gain_low.reshape(groups, 4, count), 1, 0).reshape(4, features).astype(wide)

    def start(tokens_in, cotangent_in):
        return by_rows(
            partial(start_body, groups), spot, [tokens_in, cotangent_in, valid], [], [(features, low)] * 2, []
        )

    clock = [jnp.broadcast_to(valid[:8], (8, 128))]

    def sync(values):
        values, clock[0] = lax.optimization_barrier((values, clock[0]))
        return values

    always = index < groups

    def whole(work, *values):
        shapes = jax.eval_shape(work, *values)

        def blank(*unused):
            return jax.tree.map(lambda t: jnp.zeros(t.shape, t.dtype), shapes)

        return lax.cond(always, work, blank, *values)

    def behind(*values):
        values, clock[0] = lax.optimization_barrier((values, clock[0] * 0.5))
        return values

    gate, up = plain(gateup_weight[0].astype(low)), plain(gateup_weight[1].astype(low))
    down = plain(down_weight.astype(low).T)

    def down_part(act_low, weights):
        return dot("tf,df->td", act_low, weights).astype(low)

    def act_back(grad_own, grad_peer, gate_out, up_out, wd_own, wd_peer):
        grad_act = dot("td,df->tf", grad_own, wd_own) + dot("td,df->tf", grad_peer, wd_peer)
        unused, pull_act = jax.vjp(gated, gate_out, up_out)
        return tuple(grad.astype(low) for grad in pull_act(grad_act))

    def hidden_back(grad_gate, grad_up, wg, wu):
        return (dot("tf,df->td", grad_gate, wg) + dot("tf,df->td", grad_up, wu)).astype(low)

    def results(block_out, input_grad, new_mixer, new_gate_up, new_down, sum_gains):
        new_query, new_keyval, new_output = new_mixer
        new_gains = updated(norm_gains, sum_gains, moment_gains, square_gains)
        turned_back = [tuple(t.T for t in group_of) for group_of in (new_output, new_down)]
        new = (new_query, new_keyval, turned_back[0], new_gate_up, turned_back[1], new_gains)
        return (block_out, input_grad) + tuple(new[at][kind] for kind in range(4) for at in range(6))

    def simple():
        def gathered(own):
            rows = lax.all_gather(own, "dp", axis=0, tiled=True).reshape(outer, 2, -1, own.shape[1])
            return jnp.moveaxis(jnp.where(side == 0, rows, rows[:, ::-1]), 1, 0)

        def whole_rows(own):
            return gathered(own).reshape(features, own.shape[1])

        def scattered(rows):
            rows = rows.astype(wide).reshape(2, outer, count, rows.shape[1])
            rows = jnp.moveaxis(jnp.where(side == 0, rows, rows[::-1]), 0, 1).reshape(features, -1)
            return lax.psum_scatter(rows, "dp", scatter_dimension=0, tiled=True)

        def over_heads(part):
            return lax.psum(part.astype(wide), "mp").astype(low)

        rows = gathered(mixer)
        full = rows[:, :, :count].reshape(features, width_mixer)
        gains = jnp.moveaxis(rows[:, :, count, : 4 * count].reshape(groups, 4, count), 1, 0)
        gains = gains.reshape(4, features).astype(wide)
        wg, wu, wd = whole_rows(gate), whole_rows(up), whole_rows(down)
        inputs, grad_out = start(tokens, cotangent)
        attn_part, saved = attention(projections(inputs, full, gains), full)
        attn_sum = over_heads(attn_part)
        (hidden_in,) = by_rows(hidden_body, spot, [inputs, attn_sum], [gains], [(features, low)], [])
        gate_out, up_out = dot("td,df->tf", hidden_in, wg), dot("td,df->tf", hidden_in, wu)
        act_low = gated(gate_out, up_out).astype(low)
        ffn = over_heads(down_part(act_low, wd))
        ffn_parts = ffn[:, :half], ffn[:, half : half + half // 2], ffn[:, half + half // 2 :]
        block_out = layer_out(inputs, attn_sum, ffn_parts, gains, True)
        grad_own, grad_peer, gain3 = ffn_back(ffn_parts, grad_out, gains, True)
        grad_gate, grad_up = act_back(grad_own, grad_peer, gate_out, up_out, wd[:half], wd[half:])
        sum_down = scattered(weight_grad(jnp.concatenate([grad_own, grad_peer], axis=1), act_low))
        sums = [scattered(weight_grad(hidden_in, grad)) for grad in (grad_gate, grad_up)]
        grad_hidden = over_heads(hidden_back(grad_gate, grad_up, wg, wu))
        grad_resid, grad_attn, gain1, gain2 = attn_back(inputs, attn_sum, grad_hidden, grad_out, gains)
        grad_raw = attention_back(grad_attn, full, saved)
        grads = weight_grad(saved[0], grad_raw), weight_grad(grad_attn, saved[-1])
        sum_mixer = scattered(jnp.concatenate(grads, axis=1))
        grad_normed = over_heads(dot("te,de->td", grad_raw, full[:, :width_qkv]))
        input_grad, gain0 = in_back(inputs, grad_normed, grad_resid, gains)
        sum_gains = scattered(jnp.concatenate([gain0, gain1, gain2, gain3], axis=0).T).T
        return results(
            block_out, input_grad, update_mixer(sum_mixer), update_gate_up(sums), update_down(sum_down), sum_gains
        )

    if not paired:
        return simple()
    cut = count // 2

    m1, n0 = around(mixer), swap(mixer)
    inputs, grad_out = start(tokens, cotangent)
    m1, n0, mixer = sync((m1, n0, mixer))
    m2, n1 = around(m1), swap(m1)
    full = put(put(jnp.zeros((features, width_mixer), low), mixer[:count], 0), n0[:count], 0, half)
    wg, wu = jnp.zeros((features, width_ff), low), jnp.zeros((features, width_ff), low)
    m2, n1, m1, full, gate, up, wg, wu, allowed, cosine, sine = sync(
        (m2, n1, m1, full, gate, up, wg, wu, allowed, cosine, sine)
    )
    m3, n2 = around(m2), swap(m2)
    full = put(put(full, m1[:count], 1), n1[:count], 1, half)
    m3, n2, m2, full, gate, up, down = sync((m3, n2, m2, full, gate, up, down))
    g1, n3, down_far = around(gate), swap(m3), swap(down[cut:])
    full = put(put(full, m2[:count], 2), n2[:count], 2, half)
    wg = put(wg, gate, 0)
    wu = put(wu, up, 0)
    n3, m3, g1, down_far, full, gate, up, wg, wu, inputs, grad_out = sync(
        (n3, m3, g1, down_far, full, gate, up, wg, wu, inputs, grad_out)
    )
    u1, g2, h0, v0 = around(up), around(g1), swap(gate), swap(up)

    def attend(inputs, full, m3, n3, gains):
        full = put(put(full, m3[:count], 3), n3[:count], 3, half)
        attn_part, saved = attention(projections(inputs, full, gains), full)
        return apart(attn_part) + (saved, full)

    gains = gains_of((mixer, m1, m2, m3), (n0, n1, n2, n3))
    given, kept, saved, full = whole(attend, inputs, full, m3, n3, gains)
    given, kept, u1, g1, g2, v0, h0, saved, gains = sync((given, kept, u1, g1, g2, v0, h0, saved, gains))
    u2, g3, h1, v1 = around(u1), around(g2), swap(g1), swap(u1)
    theirs = near(given)
    wg, wu, h0, v0, u1, g1 = behind(wg, wu, h0, v0, u1, g1)
    wg = put(put(wg, g1, 1), h0, 0, half)
    wu = put(put(wu, u1, 1), v0, 0, half)
    u2, g2, g3, h1, v1, theirs, kept, wg, wu, down = sync((u2, g2, g3, h1, v1, theirs, kept, wg, wu, down))
    u3, d1, h2, v2 = around(u2), around(down), swap(g2), swap(u2)
    kept = add(kept, theirs)
    across = far(kept)
    wg = put(put(wg, g2, 2), h1, 1, half)
    wu = put(put(wu, u2, 2), v1, 1, half)
    u3, g3, d1, h2, v2, across, kept, wg, wu = sync((u3, g3, d1, h2, v2, across, kept, wg, wu))
    d2, h3 = around(d1), swap(g3)
    v3 = swap(tie(u3, h3))
    mine = add(kept, across)
    attn_sum = together(mine, near(mine))
    (hidden_in,) = by_rows(hidden_body, spot, [inputs, attn_sum], [gains], [(features, low)], [])
    wg, wu, h2, v2, u3, g3 = behind(wg, wu, h2, v2, u3, g3)
    wg = put(put(wg, g3, 3), h2, 2, half)
    wu = put(put(wu, u3, 3), v2, 2, half)
    wd_own = put(put(jnp.zeros((half, width_ff), low), down, 0), d1, 1)
    wd_peer = jnp.zeros((half, width_ff), low)
    d3 = around(d2)
    wg = put(wg, h3, 3, half)
    gate_out = dot("td,df->tf", hidden_in, wg)
    down_cut, d1_cut = down[:cut], d1[:cut]
    d2, d3, v3, wg, gate_out, wu, wd_own, wd_peer, down_cut, d1_cut, down_far = sync(
        (d2, d3, v3, wg, gate_out, wu, wd_own, wd_peer, down_cut, d1_cut, down_far)
    )
    f1, e0, e1 = around(down_far), swap(down_cut), swap(d1_cut)
    wu, v3 = behind(wu, v3)
    wu = put(wu, v3, 3, half)
    up_out = dot("td,df->tf", hidden_in, wu)
    act_low = gated(gate_out, up_out).astype(low)
    wd_own = put(put(wd_own, d2, 2), d3, 3)
    d2_cut, d3_cut = d2[:cut], d3[:cut]
    given, kept = apart(down_part(act_low, wd_own))
    f1, e0, e1, act_low, given, kept, d2_cut, d3_cut, wd_peer = sync(
        (f1, e0, e1, act_low, given, kept, d2_cut, d3_cut, wd_peer)
    )
    f2, e2, e3 = around(f1), swap(d2_cut), swap(d3_cut)
    kept = add(kept, near(given))
    across = far(kept)
    f3 = around(tie(f2, kept))
    first_rows = jnp.concatenate([e0, down_far, e1, f1], axis=0)
    given, kept_first = apart(down_part(act_low, first_rows))
    kept_first = add(kept_first, near(given))
    across_first = far(tie(kept_first, kept))
    wd_peer = put(put(put(put(wd_peer, e0, 0), down_far, 0, cut), e1, 1), f1, 1, cut)
    f2, f3, e2, e3, across, kept, across_first, kept_first, wd_peer = sync(
        (f2, f3, e2, e3, across, kept, across_first, kept_first, wd_peer)
    )
    last_rows = jnp.concatenate([e2, f2, e3, f3], axis=0)
    given, kept_last = apart(down_part(act_low, last_rows))
    kept_last = add(kept_last, near(given))
    across_last = far(kept_last)
    ffn_parts = []
    for held, came in ((kept, across), (kept_first, across_first), (kept_last, across_last)):
        mine = add(held, came)
        ffn_parts.append(together(mine, near(mine)))
    wd_peer = put(put(put(put(wd_peer, e2, 2), f2, 2, cut), e3, 3), f3, 3, cut)

    def piece(tensor, hops):
        return rows_at(tensor, lax.rem(place + hops, outer), count)

    def plus(own, arrived, total=None, kind=low):
        both = own.astype(wide) + arrived.astype(wide)
        if total is not None:
            both = both + total.astype(wide)
        return both.astype(kind)

    def pieces(tensor):
        return [piece(tensor, hops) for hops in (3, 2, 1, 0)]

    def rows_of(tensor, offset, rows):
        starts = [lax.rem(place + hops, outer) * count + offset for hops in (3, 2, 1, 0)]
        return [lax.dynamic_slice_in_dim(tensor, first, rows, 0) for first in starts]

    def both(hops, offset, tensors):
        target = lax.rem(place + hops, outer) * count + offset
        cuts = [lax.dynamic_slice_in_dim(t, target, count, 0) for t in tensors]
        return plain(jnp.concatenate(cuts, axis=1))

    grad_ffn_own, grad_ffn_peer, grad_gain3 = ffn_back(ffn_parts, grad_out, gains, False)
    wd_grad = weight_grad(grad_ffn_peer, act_low)
    cut = count * 7 // 18 // 16 * 16
    sent, far_parts = jnp.concatenate(rows_of(wd_grad, 0, cut), axis=0), rows_of(wd_grad, cut, count - cut)
    sent, far_parts, grad_ffn_own, grad_ffn_peer, wd_peer = sync(
        (sent, far_parts, grad_ffn_own, grad_ffn_peer, wd_peer)
    )

    arrived, f3 = swap(sent), around(far_parts[0])

    def act_step(grad_own, grad_peer, gate_out, up_out, act_low, hidden_in, wd_own, wd_peer):
        grad_gate, grad_up = act_back(grad_own, grad_peer, gate_out, up_out, wd_own, wd_peer)
        gate_sent = pieces(weight_grad(hidden_in[:, half:], grad_gate))
        return grad_gate, grad_up, weight_grad(grad_own, act_low), gate_sent

    grad_gate, grad_up, wd_grad, gate_sent = whole(
        act_step, grad_ffn_own, grad_ffn_peer, gate_out, up_out, act_low, hidden_in, wd_own, wd_peer
    )
    arrived, f3, grad_gate, grad_up, wd_grad, gate_sent, far_parts = sync(
        (arrived, f3, grad_gate, grad_up, wd_grad, gate_sent, far_parts)
    )

    def grown(at):
        return jnp.pad(arrived[at * cut : (at + 1) * cut], ((0, count - cut), (0, 0)))

    h3 = swap(gate_sent[0])
    came = around(plus(piece(wd_grad, 3), grown(0)))
    f2 = around(add(far_parts[1], f3))

    def hidden_step(grad_gate, grad_up, wg, wu):
        return apart(hidden_back(grad_gate, grad_up, wg, wu))

    given, kept = whole(hidden_step, grad_gate, grad_up, wg, wu)
    h3, came, f2, given, kept, gate_sent, grad_gate, grad_up = sync(
        (h3, came, f2, given, kept, gate_sent, grad_gate, grad_up)
    )
    h2, theirs = swap(gate_sent[1]), near(given)
    came = around(plus(piece(wd_grad, 2), grown(1), came))

    def rest_of_grads(grad_gate, grad_up, hidden_in, gate_sent, h3, far_part, f2):
        up_sent = pieces(weight_grad(hidden_in[:, half:], grad_up))
        wg_grad = weight_grad(hidden_in[:, :half], grad_gate)
        mixed_sent = [jnp.concatenate(pair, axis=0) for pair in zip(gate_sent[2:], up_sent[:2])]
        firsts = plus(piece(wg_grad, 3), h3), add(far_part, f2)
        return mixed_sent, up_sent[2:], wg_grad, weight_grad(hidden_in[:, :half], grad_up), firsts

    mixed_sent, up_sent, wg_grad, wu_grad, (gate_first, down_first) = whole(
        rest_of_grads, grad_gate, grad_up, hidden_in, gate_sent, h3, far_parts[2], f2
    )
    h2, theirs, came, mixed_sent, up_sent, wg_grad, wu_grad, kept, gate_first = sync(
        (h2, theirs, came, mixed_sent, up_sent, wg_grad, wu_grad, kept, gate_first)
    )
    pair = swap(mixed_sent[0])
    kept = add(kept, theirs)
    across = far(kept)
    came = around(plus(piece(wd_grad, 1), grown(2), came))
    gate_came = around(gate_first)
    across, pair, came, gate_came, kept, mixed_sent[1], up_sent, down_first = sync(
        (across, pair, came, gate_came, kept, mixed_sent[1], up_sent, down_first)
    )
    h1, v3 = pair[:count], pair[count:]
    pair = swap(mixed_sent[1])
    mine = add(kept, across)
    theirs = near(mine)
    gate_came = around(plus(piece(wg_grad, 2), h2, gate_came))
    up_came = around(plus(piece(wu_grad, 3), v3))
    f1 = around(down_first)

    def mixer_back(inputs, attn_sum, mine, theirs, grad_out, gains, full, saved):
        grad_hidden = together(mine, theirs)
        grad_resid, grad_attn, gain1, gain2 = attn_back(inputs, attn_sum, grad_hidden, grad_out, gains)
        grad_raw = attention_back(grad_attn, full, saved)
        given, kept = apart(dot("te,de->td", grad_raw, full[:, :width_qkv]).astype(low))
        return given, kept, grad_resid, grad_attn, gain1, gain2, grad_raw

    given, kept, grad_resid, grad_attn, grad_gain1, grad_gain2, grad_raw = whole(
        mixer_back, inputs, attn_sum, mine, theirs, grad_out, gains, full, saved
    )
    pair, gate_came, up_came, f1, given, kept, grad_resid, grad_attn, grad_raw, up_sent = sync(
        (pair, gate_came, up_came, f1, given, kept, grad_resid, grad_attn, grad_raw, up_sent)
    )
    h0, v2 = pair[:count], pair[count:]
    v1, theirs = swap(up_sent[0]), near(given)
    gate_came = around(plus(piece(wg_grad, 1), h1, gate_came))

    def mixer_grads(normed_low, mixed_low, grad_raw, grad_attn):
        grads = weight_grad(normed_low, grad_raw), weight_grad(grad_attn, mixed_low)
        pairs = ((3, 2), (1, 0))
        mixer_sent = [jnp.concatenate([both(hops, half, grads) for hops in pair], axis=0) for pair in pairs]
        return mixer_sent, [both(hops, 0, grads) for hops in (3, 2, 1, 0)]

    mixer_sent, mixer_own = whole(mixer_grads, saved[0], saved[-1], grad_raw, grad_attn)
    v1, theirs, gate_came, mixer_sent, mixer_own, kept, up_sent = sync(
        (v1, theirs, gate_came, mixer_sent, mixer_own, kept, up_sent)
    )
    v0, x32 = swap(up_sent[1]), swap(mixer_sent[0])
    kept = add(kept, theirs)
    across = far(kept)
    up_came = around(plus(piece(wu_grad, 2), v2, up_came))
    gate_late = tie(gate_came, up_came)
    sum_gate = plus(piece(wg_grad, 0), h0, gate_late, wide)
    up_came = around(plus(piece(wu_grad, 1), v1, up_came))
    v0, x32, up_came, across, kept, mixer_sent[1], inputs, f1, sum_gate = sync(
        (v0, x32, up_came, across, kept, mixer_sent[1], inputs, f1, sum_gate)
    )
    x10, b_far = swap(mixer_sent[1]), swap(add(far_parts[3], f1))
    m3 = around(plus(mixer_own[0], x32[:count]), 3)
    m2 = around(plus(mixer_own[1], x32[count:]), 2)
    mine = add(kept, across)
    theirs = near(mine)

    def finish(inputs, mine, theirs, grad_resid, attn_sum, ffn_parts, gains):
        block_out = layer_out(inputs, attn_sum, ffn_parts, gains, False)
        input_grad, gain0 = in_back(inputs, together(mine, theirs), grad_resid, gains)
        return block_out, input_grad, gain0

    block_out, input_grad, grad_gain0 = whole(
        finish, inputs, mine, theirs, grad_resid, attn_sum, ffn_parts, gains
    )
    x10, b_far, m3, m2, block_out, input_grad, grad_gain0 = sync(
        (x10, b_far, m3, m2, block_out, input_grad, grad_gain0)
    )
    mixed = plus(mixer_own[2], x10[:count])
    m1 = around(mixed)
    came = tie(came, mixed)
    grad_gains = jnp.concatenate([grad_gain0, grad_gain1, grad_gain2, grad_gain3], axis=0)
    gain_sum = grad_gains[:, :half] + swap(grad_gains[:, half:])
    gain_sum = gain_sum.reshape(4, outer, count)
    down_total = plus(piece(wd_grad, 0), jnp.concatenate([arrived[3 * cut :], b_far], axis=0), came, wide)
    new_down = update_down(behind(down_total)[0])
    sum_up = plus(piece(wu_grad, 0), v0, up_came, wide)
    new_gate_up = update_gate_up([sum_gate, sum_up])
    sum_gains = lax.dynamic_index_in_dim(gain_sum, place, 1, False)
    for hops in (1, 2, 3):
        given = lax.dynamic_index_in_dim(gain_sum, lax.rem(place + hops, outer), 1, False)
        sum_gains = sum_gains + around(given, hops)
    m1, sum_gains, new_down, new_gate_up = sync((m1, sum_gains, new_down, new_gate_up))
    sum_mixer = plus(mixer_own[3], x10[count:], m1, wide) + m2.astype(wide) + m3.astype(wide)
    return results(block_out, input_grad, update_mixer(sum_mixer), new_gate_up, new_down, sum_gains)


def solution(mesh):
    return jax.shard_map(
        shards,
        mesh=mesh,
        in_specs=(
            P("dp", None),
            P("dp"),
            P("dp", None),
            P("dp", "mp"),
            P(None, "dp", "mp"),
            P("mp", "dp"),
            P(None, "dp", "mp"),
            P("mp", "dp"),
            P(None, "dp"),
            P("dp", "mp"),
            P(None, "dp", "mp"),
            P("mp", "dp"),
            P(None, "dp", "mp"),
            P("mp", "dp"),
            P(None, "dp"),
            P("dp", "mp"),
            P(None, "dp", "mp"),
            P("mp", "dp"),
            P(None, "dp", "mp"),
            P("mp", "dp"),
            P(None, "dp"),
        ),
        out_specs=(
            P("dp", None),
            P("dp", None),
            P("dp", "mp"),
            P(None, "dp", "mp"),
            P("mp", "dp"),
            P(None, "dp", "mp"),
            P("mp", "dp"),
            P(None, "dp"),
            P("dp", "mp"),
            P(None, "dp", "mp"),
            P("mp", "dp"),
            P(None, "dp", "mp"),
            P("mp", "dp"),
            P(None, "dp"),
            P("dp", "mp"),
            P(None, "dp", "mp"),
            P("mp", "dp"),
            P(None, "dp", "mp"),
            P("mp", "dp"),
            P(None, "dp"),
            P("dp", "mp"),
            P(None, "dp", "mp"),
            P("mp", "dp"),
            P(None, "dp", "mp"),
            P("mp", "dp"),
            P(None, "dp"),
        ),
        check_vma=False,
    )
```

```python
from functools import partial

import jax
import jax.numpy as jnp
from jax import lax
from jax.experimental import pallas as pl
from jax.experimental.layout import Layout, with_layout_constraint
from jax.experimental.pallas import tpu as pltpu
from jax.sharding import PartitionSpec as P

HEADS = 8
KV_HEADS = 4
HEAD_DIM = 256
WINDOW = 4096
ADAM_STEP = 5


norm_eps = 1e-06
cap_value = 50.0
rope_base = 10000.0
learn_rate = 0.1
beta_one = 0.9
beta_two = 0.95
adam_eps = 1e-08
decay_rate = 0.1


low = jnp.bfloat16
wide = jnp.float32


def tie(tensor, *others):
    return lax.optimization_barrier((tensor,) + others)[0]


def plain(tensor):
    return with_layout_constraint(tensor, Layout(tuple(range(tensor.ndim))))


def ring_pairs(extent, hops=1):
    outer = extent // 2
    return [
        (2 * place + side, 2 * ((place + hops) % outer) + side)
        for place in range(outer)
        for side in range(2)
    ]


def swap_pairs(extent, stride):
    return [(place, place ^ stride) for place in range(extent)]


def rows_at(tensor, index, count):
    return lax.dynamic_slice_in_dim(tensor, index * count, count, 0)


def add(first, second, kind=low):
    return (first.astype(wide) + second.astype(wide)).astype(kind)


BLOCK = 224


def by_rows(body, side, rows, whole, outs, sums, block=BLOCK):
    length = rows[0].shape[0]

    def blocked(width):
        return pl.BlockSpec((block, width), lambda i: (i, 0))

    def kept(shape):
        return pl.BlockSpec(shape, lambda i: (0, 0))

    return pl.pallas_call(
        body,
        grid=(length // block,),
        in_specs=[pl.BlockSpec(memory_space=pltpu.SMEM)]
        + [blocked(t.shape[1]) for t in rows]
        + [kept(t.shape) for t in whole],
        out_specs=[blocked(width) for width, kind in outs] + [kept((1, width)) for width in sums],
        out_shape=[jax.ShapeDtypeStruct((length, width), kind) for width, kind in outs]
        + [jax.ShapeDtypeStruct((1, width), wide) for width in sums],
        compiler_params=pltpu.CompilerParams(vmem_limit_bytes=48 * 1024 * 1024),
    )(side, *rows, *whole)


def factor_of(value):
    return lax.rsqrt(jnp.mean(value * value, axis=-1, keepdims=True) + norm_eps)


def back_of(value, factor, gain, grad):
    scaled = grad * (1.0 + gain)
    shared = factor * factor * jnp.mean(scaled * value, axis=-1, keepdims=True)
    return factor * (scaled - shared * value), grad * (value * factor)


def add_up(ref, value):
    @pl.when(pl.program_id(0) == 0)
    def start():
        ref[...] = jnp.zeros_like(ref)

    ref[...] += jnp.sum(value, axis=0, keepdims=True)


def pieces_of(value, groups):
    count = value.shape[1] // groups
    return [value[:, k * count : (k + 1) * count] for k in range(groups)]


def turn(value, side, groups):
    cut = pieces_of(value, groups)
    even, odd = jnp.concatenate(cut[0::2], axis=1), jnp.concatenate(cut[1::2], axis=1)
    first, second = jnp.where(side == 0, even, odd), jnp.where(side == 0, odd, even)
    return jnp.concatenate([first, second], axis=1)


def straighten(value, side, groups):
    half = value.shape[1] // 2
    own, peer = value[:, :half], value[:, half:]
    even, odd = jnp.where(side == 0, own, peer), jnp.where(side == 0, peer, own)
    woven = zip(pieces_of(even, groups // 2), pieces_of(odd, groups // 2))
    return jnp.concatenate([cut for pair in woven for cut in pair], axis=1)


def start_body(groups, side, tokens, cotangent, valid, inputs, grad_out):
    inputs[...] = turn(tokens[...].astype(wide), side[0], groups).astype(low)
    grad_out[...] = turn(cotangent[...].astype(wide) * valid[...], side[0], groups).astype(low)


def normed_body(side, inputs, gains, normed):
    value = inputs[...].astype(wide)
    normed[...] = (value * factor_of(value) * (1.0 + gains[0:1])).astype(low)


def residual_of(inputs, attn, gains):
    value, mixed = inputs[...].astype(wide), attn[...].astype(wide)
    factor = factor_of(mixed)
    return value + mixed * factor * (1.0 + gains[1:2]), mixed, factor


def hidden_body(side, inputs, attn, gains, hidden):
    residual = residual_of(inputs, attn, gains)[0]
    hidden[...] = (residual * factor_of(residual) * (1.0 + gains[2:3])).astype(low)


def ffn_of(groups, ordered, place, own, first, last):
    own, first, last = (part[...].astype(wide) for part in (own, first, last))
    if ordered:
        return jnp.concatenate([own, first, last], axis=1)
    outer = groups // 2
    by_step = pieces_of(first, outer // 2) + pieces_of(last, outer // 2)
    peer = []
    for at in range(outer):
        block = by_step[(outer - 1 - at) % outer]
        for spot in range(outer - 1):
            block = jnp.where(place == spot, by_step[(spot - at) % outer], block)
        peer.append(block)
    return jnp.concatenate([own] + peer, axis=1)


def ffn_back_body(groups, ordered, spot, own, first, last, grad_out, gains, grad_own, grad_peer, grad_gain):
    ffn = ffn_of(groups, ordered, spot[1], own, first, last)
    grad, term = back_of(ffn, factor_of(ffn), gains[3:4], grad_out[...].astype(wide))
    half = ffn.shape[1] // 2
    grad_own[...] = grad[:, :half].astype(low)
    grad_peer[...] = grad[:, half:].astype(low)
    add_up(grad_gain, term)


def out_body(groups, ordered, spot, inputs, attn, own, first, last, gains, out):
    ffn = ffn_of(groups, ordered, spot[1], own, first, last)
    value = residual_of(inputs, attn, gains)[0] + ffn * factor_of(ffn) * (1.0 + gains[3:4])
    out[...] = straighten(value, spot[0], groups).astype(low)


def attn_back_body(side, inputs, attn, grad_hidden, grad_out, gains, grad_resid, grad_attn, gain1, gain2):
    residual, mixed, factor = residual_of(inputs, attn, gains)
    grad, term2 = back_of(residual, factor_of(residual), gains[2:3], grad_hidden[...].astype(wide))
    grad = grad + grad_out[...].astype(wide)
    grad_resid[...] = grad
    back, term1 = back_of(mixed, factor, gains[1:2], grad)
    grad_attn[...] = back.astype(low)
    add_up(gain1, term1)
    add_up(gain2, term2)


def in_back_body(groups, side, inputs, grad_normed, grad_resid, gains, input_grad, gain0):
    value = inputs[...].astype(wide)
    grad, term = back_of(value, factor_of(value), gains[0:1], grad_normed[...].astype(wide))
    input_grad[...] = straighten(grad_resid[...] + grad, side[0], groups)
    add_up(gain0, term)


def rotate(tensor, cosine, sine):
    half_dim = tensor.shape[-1] // 2
    first = tensor[..., :half_dim]
    second = tensor[..., half_dim:]
    return jnp.concatenate(
        [first * cosine - second * sine, second * cosine + first * sine], axis=-1
    )


def layout(labels):
    length = labels.shape[0]
    places = jnp.arange(length, dtype=jnp.int32)
    same_seq = labels[:, None] == labels[None, :]
    earlier = places[None, :] < places[:, None]
    position = jnp.sum((same_seq & earlier).astype(jnp.int32), axis=1)
    allowed = (
        same_seq
        & (places[None, :] <= places[:, None])
        & (places[:, None] - places[None, :] < WINDOW)
    )
    half_dim = HEAD_DIM // 2
    freq = rope_base ** (-2.0 * jnp.arange(half_dim, dtype=jnp.float32) / HEAD_DIM)
    angle = position.astype(jnp.float32)[:, None] * freq[None, :]
    return (allowed, jnp.cos(angle)[:, None, :], jnp.sin(angle)[:, None, :])


def scores(queries, key_rows, allowed):
    raw_scores = jnp.einsum("qkgd,skd->kgqs", queries, key_rows, preferred_element_type=jnp.float32)
    squashed = jnp.tanh(raw_scores / cap_value)
    capped = jnp.where(allowed[None, None], cap_value * squashed, -1e30)
    return (squashed, capped)


def rotate_back(grad_in, cosine, sine, shape_like):
    unused, pull = jax.vjp(lambda tensor: rotate(tensor, cosine, sine), shape_like)
    return pull(grad_in)[0]


def adam_step(master, gradient, moment, square, steps_done):
    new_moment = beta_one * moment + (1.0 - beta_one) * gradient
    new_square = beta_two * square + (1.0 - beta_two) * gradient * gradient
    fix_one = 1.0 - beta_one**steps_done
    fix_two = 1.0 - beta_two**steps_done
    stride = new_moment / fix_one / (jnp.sqrt(new_square / fix_two) + adam_eps)
    return (-learn_rate * (stride + decay_rate * master), new_moment, new_square)


def shards(
    tokens,
    segments,
    cotangent,
    query_weight,
    keyval_weight,
    output_weight,
    gateup_weight,
    down_weight,
    norm_gains,
    moment_query,
    moment_keyval,
    moment_output,
    moment_gateup,
    moment_down,
    moment_gains,
    square_query,
    square_keyval,
    square_output,
    square_gateup,
    square_down,
    square_gains,
):
    groups, parts = lax.axis_size("dp"), lax.axis_size("mp")
    outer = groups // 2
    index = lax.axis_index("dp")
    place = index // 2
    side = lax.rem(index, 2)
    spot = jnp.stack([side, place]).astype(jnp.int32)
    length, features = tokens.shape
    half = features // 2
    count = features // groups
    group = HEADS // KV_HEADS
    width_q, width_kv = query_weight.shape[1], keyval_weight.shape[2]
    width_qkv = width_q + 2 * width_kv
    width_mixer = width_qkv + output_weight.shape[0]
    width_ff = down_weight.shape[0]
    kv_local = width_kv // HEAD_DIM
    heads_local = kv_local * group
    qscale = HEAD_DIM ** (-0.5)
    core = lax.rem(lax.axis_index("mp"), 2)
    paired = outer == 4 and parts == 4

    def dot(pattern, first, second):
        return jnp.einsum(pattern, first, second, preferred_element_type=wide)

    def around(tensor, hops=1):
        return lax.ppermute(tensor, "dp", ring_pairs(groups, hops))

    def swap(tensor):
        return lax.ppermute(tensor, "dp", swap_pairs(groups, 1))

    def near(tensor):
        return lax.ppermute(tensor, "mp", swap_pairs(parts, 1))

    def far(tensor):
        return lax.ppermute(tensor, "mp", swap_pairs(parts, 2))

    def apart(partial_sum):
        rows = length // 2
        return rows_at(partial_sum, 1 - core, rows), rows_at(partial_sum, core, rows)

    def together(mine, theirs):
        first = jnp.where(core == 0, mine, theirs)
        second = jnp.where(core == 0, theirs, mine)
        return jnp.concatenate([first, second], axis=0)

    allowed, cosine, sine = layout(segments)
    valid = (segments >= 0).astype(wide)[:, None]

    def projections(inputs, weights, gains):
        (normed_low,) = by_rows(normed_body, spot, [inputs], [gains], [(features, low)], [])
        mixer_raw = dot("td,de->te", normed_low, weights[:, :width_qkv])
        qraw = mixer_raw[:, :width_q].reshape(length, heads_local, HEAD_DIM)
        kraw = mixer_raw[:, width_q : width_q + width_kv].reshape(length, kv_local, HEAD_DIM)
        queries = (
            (rotate(qraw, cosine, sine) * qscale).astype(low).reshape(length, kv_local, group, HEAD_DIM)
        )
        key_rows = rotate(kraw, cosine, sine).astype(low)
        value_rows = mixer_raw[:, width_q + width_kv :].astype(low).reshape(length, kv_local, HEAD_DIM)
        return normed_low, queries, key_rows, value_rows

    def attention(projected, weights):
        unused, queries, key_rows, value_rows = projected
        squashed, capped = scores(queries, key_rows, allowed)
        row_top = jnp.max(capped, axis=-1, keepdims=True)
        log_total = row_top + jnp.log(jnp.sum(jnp.exp(capped - row_top), axis=-1, keepdims=True))
        probs = jnp.exp(capped - log_total)
        probs_low = probs.astype(low)
        mixed_low = dot("kgqs,skd->qkgd", probs_low, value_rows).astype(low)
        mixed_low = mixed_low.reshape(length, heads_local * HEAD_DIM)
        attn_part = dot("te,de->td", mixed_low, weights[:, width_qkv:]).astype(low)
        return attn_part, projected + (squashed, probs, probs_low, mixed_low)

    def attention_back(grad_attn, weights, saved):
        normed_low, queries, key_rows, value_rows, squashed, probs, probs_low, mixed_low = saved
        grad_mixed = dot("td,de->te", grad_attn, weights[:, width_qkv:]).astype(low)
        grad_mixed = grad_mixed.reshape(length, kv_local, group, HEAD_DIM)
        grad_probs = dot("qkgd,skd->kgqs", grad_mixed, value_rows)
        grad_value = dot("kgqs,qkgd->skd", probs_low, grad_mixed)
        grad_value = grad_value.astype(low).reshape(length, kv_local * HEAD_DIM)
        grad_capped = probs * (grad_probs - jnp.sum(probs * grad_probs, axis=-1, keepdims=True))
        grad_scores = (grad_capped * (1.0 - squashed * squashed)).astype(low)
        grad_query = dot("kgqs,skd->qkgd", grad_scores, key_rows)
        grad_query = grad_query.reshape(length, heads_local, HEAD_DIM) * qscale
        shape_q = jnp.zeros((length, heads_local, HEAD_DIM), wide)
        grad_qraw = rotate_back(grad_query, cosine, sine, shape_q).astype(low)
        grad_key = dot("kgqs,qkgd->skd", grad_scores, queries)
        shape_k = jnp.zeros((length, kv_local, HEAD_DIM), wide)
        grad_kraw = rotate_back(grad_key, cosine, sine, shape_k).astype(low)
        flat = [t.reshape(length, -1) for t in (grad_qraw, grad_kraw, grad_value)]
        return plain(jnp.concatenate(flat, axis=1))

    def gated(gate_in, up_in):
        return jax.nn.gelu(gate_in, approximate=True) * up_in

    def weight_grad(first, second):
        return plain(dot("td,te->de", first, second).astype(low))

    def ffn_back(ffn_parts, grad_out, gains, ordered):
        body = partial(ffn_back_body, groups, ordered)
        return by_rows(body, spot, [*ffn_parts, grad_out], [gains], [(half, low)] * 2, [features])

    def layer_out(inputs, attn_sum, ffn_parts, gains, ordered):
        rows = [inputs, attn_sum, *ffn_parts]
        return by_rows(partial(out_body, groups, ordered), spot, rows, [gains], [(features, low)], [])[0]

    def attn_back(inputs, attn_sum, grad_hidden, grad_out, gains):
        rows = [inputs, attn_sum, grad_hidden, grad_out]
        outs = [(features, wide), (features, low)]
        return by_rows(attn_back_body, spot, rows, [gains], outs, [features] * 2, 128)

    def in_back(inputs, grad_normed, grad_resid, gains):
        rows = [inputs, grad_normed, grad_resid]
        return by_rows(partial(in_back_body, groups), spot, rows, [gains], [(features, wide)], [features])

    steps_done = float(ADAM_STEP)

    def updated(master, total, moment, square):
        return (total,) + adam_step(master, total, moment, square, steps_done)

    def update_gate_up(sums):
        return updated(gateup_weight, jnp.stack(sums), moment_gateup, square_gateup)

    def update_down(total):
        return updated(down_weight.T, total, moment_down.T, square_down.T)

    def update_mixer(total):
        total = plain(total)
        sum_k, sum_v = total[:, width_q : width_q + width_kv], total[:, width_q + width_kv : width_qkv]
        return (
            updated(query_weight, total[:, :width_q], moment_query, square_query),
            updated(keyval_weight, jnp.stack([sum_k, sum_v]), moment_keyval, square_keyval),
            updated(output_weight.T, total[:, width_qkv:], moment_output.T, square_output.T),
        )

    gain_row = norm_gains.astype(low).reshape(1, 4 * count)
    mixer = jnp.concatenate(
        [
            query_weight.astype(low),
            keyval_weight[0].astype(low),
            keyval_weight[1].astype(low),
            output_weight.astype(low).T,
        ],
        axis=1,
    )
    mixer = jnp.concatenate([mixer, jnp.pad(gain_row, ((0, 15), (0, width_mixer - 4 * count)))], axis=0)
    mixer = plain(mixer)

    def source(step):
        return lax.rem(place - step + outer, outer)

    def put(full, piece, step, offset=0):
        return lax.dynamic_update_slice_in_dim(full, piece, source(step) * count + offset, 0)

    def gains_of(held, peer):
        gain_low = jnp.zeros((2, outer, 4, count), low)
        for at, pieces in enumerate((held, peer)):
            for step, piece in enumerate(pieces):
                gain_piece = piece[count, : 4 * count].reshape(1, 1, 4, count)
                gain_low = lax.dynamic_update_slice(gain_low, gain_piece, (at, source(step), 0, 0))
        return jnp.moveaxis(gain_low.reshape(groups, 4, count), 1, 0).reshape(4, features).astype(wide)

    def start(tokens_in, cotangent_in):
        return by_rows(
            partial(start_body, groups), spot, [tokens_in, cotangent_in, valid], [], [(features, low)] * 2, []
        )

    clock = [jnp.broadcast_to(valid[:8], (8, 128))]

    def sync(values):
        values, clock[0] = lax.optimization_barrier((values, clock[0]))
        return values

    always = index < groups

    def whole(work, *values):
        shapes = jax.eval_shape(work, *values)

        def blank(*unused):
            return jax.tree.map(lambda t: jnp.zeros(t.shape, t.dtype), shapes)

        return lax.cond(always, work, blank, *values)

    def behind(*values):
        values, clock[0] = lax.optimization_barrier((values, clock[0] * 0.5))
        return values

    gate, up = plain(gateup_weight[0].astype(low)), plain(gateup_weight[1].astype(low))
    down = plain(down_weight.astype(low).T)

    def down_part(act_low, weights):
        return dot("tf,df->td", act_low, weights).astype(low)

    def act_back(grad_own, grad_peer, gate_out, up_out, wd_own, wd_peer):
        grad_act = dot("td,df->tf", grad_own, wd_own) + dot("td,df->tf", grad_peer, wd_peer)
        unused, pull_act = jax.vjp(gated, gate_out, up_out)
        return tuple(grad.astype(low) for grad in pull_act(grad_act))

    def hidden_back(grad_gate, grad_up, wg, wu):
        return (dot("tf,df->td", grad_gate, wg) + dot("tf,df->td", grad_up, wu)).astype(low)

    def results(block_out, input_grad, new_mixer, new_gate_up, new_down, sum_gains):
        new_query, new_keyval, new_output = new_mixer
        new_gains = updated(norm_gains, sum_gains, moment_gains, square_gains)
        turned_back = [tuple(t.T for t in group_of) for group_of in (new_output, new_down)]
        new = (new_query, new_keyval, turned_back[0], new_gate_up, turned_back[1], new_gains)
        return (block_out, input_grad) + tuple(new[at][kind] for kind in range(4) for at in range(6))

    def simple():
        def gathered(own):
            rows = lax.all_gather(own, "dp", axis=0, tiled=True).reshape(outer, 2, -1, own.shape[1])
            return jnp.moveaxis(jnp.where(side == 0, rows, rows[:, ::-1]), 1, 0)

        def whole_rows(own):
            return gathered(own).reshape(features, own.shape[1])

        def scattered(rows):
            rows = rows.astype(wide).reshape(2, outer, count, rows.shape[1])
            rows = jnp.moveaxis(jnp.where(side == 0, rows, rows[::-1]), 0, 1).reshape(features, -1)
            return lax.psum_scatter(rows, "dp", scatter_dimension=0, tiled=True)

        def over_heads(part):
            return lax.psum(part.astype(wide), "mp").astype(low)

        rows = gathered(mixer)
        full = rows[:, :, :count].reshape(features, width_mixer)
        gains = jnp.moveaxis(rows[:, :, count, : 4 * count].reshape(groups, 4, count), 1, 0)
        gains = gains.reshape(4, features).astype(wide)
        wg, wu, wd = whole_rows(gate), whole_rows(up), whole_rows(down)
        inputs, grad_out = start(tokens, cotangent)
        attn_part, saved = attention(projections(inputs, full, gains), full)
        attn_sum = over_heads(attn_part)
        (hidden_in,) = by_rows(hidden_body, spot, [inputs, attn_sum], [gains], [(features, low)], [])
        gate_out, up_out = dot("td,df->tf", hidden_in, wg), dot("td,df->tf", hidden_in, wu)
        act_low = gated(gate_out, up_out).astype(low)
        ffn = over_heads(down_part(act_low, wd))
        ffn_parts = ffn[:, :half], ffn[:, half : half + half // 2], ffn[:, half + half // 2 :]
        block_out = layer_out(inputs, attn_sum, ffn_parts, gains, True)
        grad_own, grad_peer, gain3 = ffn_back(ffn_parts, grad_out, gains, True)
        grad_gate, grad_up = act_back(grad_own, grad_peer, gate_out, up_out, wd[:half], wd[half:])
        sum_down = scattered(weight_grad(jnp.concatenate([grad_own, grad_peer], axis=1), act_low))
        sums = [scattered(weight_grad(hidden_in, grad)) for grad in (grad_gate, grad_up)]
        grad_hidden = over_heads(hidden_back(grad_gate, grad_up, wg, wu))
        grad_resid, grad_attn, gain1, gain2 = attn_back(inputs, attn_sum, grad_hidden, grad_out, gains)
        grad_raw = attention_back(grad_attn, full, saved)
        grads = weight_grad(saved[0], grad_raw), weight_grad(grad_attn, saved[-1])
        sum_mixer = scattered(jnp.concatenate(grads, axis=1))
        grad_normed = over_heads(dot("te,de->td", grad_raw, full[:, :width_qkv]))
        input_grad, gain0 = in_back(inputs, grad_normed, grad_resid, gains)
        sum_gains = scattered(jnp.concatenate([gain0, gain1, gain2, gain3], axis=0).T).T
        return results(
            block_out, input_grad, update_mixer(sum_mixer), update_gate_up(sums), update_down(sum_down), sum_gains
        )

    if not paired:
        return simple()
    cut = count // 2

    m1, n0 = around(mixer), swap(mixer)
    inputs, grad_out = start(tokens, cotangent)
    m1, n0, mixer = sync((m1, n0, mixer))
    m2, n1 = around(m1), swap(m1)
    full = put(put(jnp.zeros((features, width_mixer), low), mixer[:count], 0), n0[:count], 0, half)
    wg, wu = jnp.zeros((features, width_ff), low), jnp.zeros((features, width_ff), low)
    m2, n1, m1, full, gate, up, wg, wu, allowed, cosine, sine = sync(
        (m2, n1, m1, full, gate, up, wg, wu, allowed, cosine, sine)
    )
    m3, n2 = around(m2), swap(m2)
    full = put(put(full, m1[:count], 1), n1[:count], 1, half)
    m3, n2, m2, full, gate, up, down = sync((m3, n2, m2, full, gate, up, down))
    g1, n3, down_far = around(gate), swap(m3), swap(down[cut:])
    full = put(put(full, m2[:count], 2), n2[:count], 2, half)
    wg = put(wg, gate, 0)
    wu = put(wu, up, 0)
    n3, m3, g1, down_far, full, gate, up, wg, wu, inputs, grad_out = sync(
        (n3, m3, g1, down_far, full, gate, up, wg, wu, inputs, grad_out)
    )
    u1, g2, h0, v0 = around(up), around(g1), swap(gate), swap(up)

    def attend(inputs, full, m3, n3, gains):
        full = put(put(full, m3[:count], 3), n3[:count], 3, half)
        attn_part, saved = attention(projections(inputs, full, gains), full)
        return apart(attn_part) + (saved, full)

    gains = gains_of((mixer, m1, m2, m3), (n0, n1, n2, n3))
    given, kept, saved, full = whole(attend, inputs, full, m3, n3, gains)
    given, kept, u1, g1, g2, v0, h0, saved, gains = sync((given, kept, u1, g1, g2, v0, h0, saved, gains))
    u2, g3, h1, v1 = around(u1), around(g2), swap(g1), swap(u1)
    theirs = near(given)
    wg, wu, h0, v0, u1, g1 = behind(wg, wu, h0, v0, u1, g1)
    wg = put(put(wg, g1, 1), h0, 0, half)
    wu = put(put(wu, u1, 1), v0, 0, half)
    u2, g2, g3, h1, v1, theirs, kept, wg, wu, down = sync((u2, g2, g3, h1, v1, theirs, kept, wg, wu, down))
    u3, d1, h2, v2 = around(u2), around(down), swap(g2), swap(u2)
    kept = add(kept, theirs)
    across = far(kept)
    wg = put(put(wg, g2, 2), h1, 1, half)
    wu = put(put(wu, u2, 2), v1, 1, half)
    u3, g3, d1, h2, v2, across, kept, wg, wu = sync((u3, g3, d1, h2, v2, across, kept, wg, wu))
    d2, h3 = around(d1), swap(g3)
    v3 = swap(tie(u3, h3))
    mine = add(kept, across)
    attn_sum = together(mine, near(mine))
    (hidden_in,) = by_rows(hidden_body, spot, [inputs, attn_sum], [gains], [(features, low)], [])
    wg, wu, h2, v2, u3, g3 = behind(wg, wu, h2, v2, u3, g3)
    wg = put(put(wg, g3, 3), h2, 2, half)
    wu = put(put(wu, u3, 3), v2, 2, half)
    wd_own = put(put(jnp.zeros((half, width_ff), low), down, 0), d1, 1)
    wd_peer = jnp.zeros((half, width_ff), low)
    d3 = around(d2)
    wg = put(wg, h3, 3, half)
    gate_out = dot("td,df->tf", hidden_in, wg)
    down_cut, d1_cut = down[:cut], d1[:cut]
    d2, d3, v3, wg, gate_out, wu, wd_own, wd_peer, down_cut, d1_cut, down_far = sync(
        (d2, d3, v3, wg, gate_out, wu, wd_own, wd_peer, down_cut, d1_cut, down_far)
    )
    f1, e0, e1 = around(down_far), swap(down_cut), swap(d1_cut)
    wu, v3 = behind(wu, v3)
    wu = put(wu, v3, 3, half)
    up_out = dot("td,df->tf", hidden_in, wu)
    act_low = gated(gate_out, up_out).astype(low)
    wd_own = put(put(wd_own, d2, 2), d3, 3)
    d2_cut, d3_cut = d2[:cut], d3[:cut]
    given, kept = apart(down_part(act_low, wd_own))
    f1, e0, e1, act_low, given, kept, d2_cut, d3_cut, wd_peer = sync(
        (f1, e0, e1, act_low, given, kept, d2_cut, d3_cut, wd_peer)
    )
    f2, e2, e3 = around(f1), swap(d2_cut), swap(d3_cut)
    kept = add(kept, near(given))
    across = far(kept)
    f3 = around(tie(f2, kept))
    first_rows = jnp.concatenate([e0, down_far, e1, f1], axis=0)
    given, kept_first = apart(down_part(act_low, first_rows))
    kept_first = add(kept_first, near(given))
    across_first = far(tie(kept_first, kept))
    wd_peer = put(put(put(put(wd_peer, e0, 0), down_far, 0, cut), e1, 1), f1, 1, cut)
    f2, f3, e2, e3, across, kept, across_first, kept_first, wd_peer = sync(
        (f2, f3, e2, e3, across, kept, across_first, kept_first, wd_peer)
    )
    last_rows = jnp.concatenate([e2, f2, e3, f3], axis=0)
    given, kept_last = apart(down_part(act_low, last_rows))
    kept_last = add(kept_last, near(given))
    across_last = far(kept_last)
    ffn_parts = []
    for held, came in ((kept, across), (kept_first, across_first), (kept_last, across_last)):
        mine = add(held, came)
        ffn_parts.append(together(mine, near(mine)))
    wd_peer = put(put(put(put(wd_peer, e2, 2), f2, 2, cut), e3, 3), f3, 3, cut)

    def piece(tensor, hops):
        return rows_at(tensor, lax.rem(place + hops, outer), count)

    def plus(own, arrived, total=None, kind=low):
        both = own.astype(wide) + arrived.astype(wide)
        if total is not None:
            both = both + total.astype(wide)
        return both.astype(kind)

    def pieces(tensor):
        return [piece(tensor, hops) for hops in (3, 2, 1, 0)]

    def rows_of(tensor, offset, rows):
        starts = [lax.rem(place + hops, outer) * count + offset for hops in (3, 2, 1, 0)]
        return [lax.dynamic_slice_in_dim(tensor, first, rows, 0) for first in starts]

    def both(hops, offset, tensors):
        target = lax.rem(place + hops, outer) * count + offset
        cuts = [lax.dynamic_slice_in_dim(t, target, count, 0) for t in tensors]
        return plain(jnp.concatenate(cuts, axis=1))

    grad_ffn_own, grad_ffn_peer, grad_gain3 = ffn_back(ffn_parts, grad_out, gains, False)
    wd_grad = weight_grad(grad_ffn_peer, act_low)
    cut = count * 7 // 18 // 16 * 16
    sent, far_parts = jnp.concatenate(rows_of(wd_grad, 0, cut), axis=0), rows_of(wd_grad, cut, count - cut)
    sent, far_parts, grad_ffn_own, grad_ffn_peer, wd_peer = sync(
        (sent, far_parts, grad_ffn_own, grad_ffn_peer, wd_peer)
    )

    arrived, f3 = swap(sent), around(far_parts[0])

    def act_step(grad_own, grad_peer, gate_out, up_out, act_low, hidden_in, wd_own, wd_peer):
        grad_gate, grad_up = act_back(grad_own, grad_peer, gate_out, up_out, wd_own, wd_peer)
        gate_sent = pieces(weight_grad(hidden_in[:, half:], grad_gate))
        return grad_gate, grad_up, weight_grad(grad_own, act_low), gate_sent

    grad_gate, grad_up, wd_grad, gate_sent = whole(
        act_step, grad_ffn_own, grad_ffn_peer, gate_out, up_out, act_low, hidden_in, wd_own, wd_peer
    )
    arrived, f3, grad_gate, grad_up, wd_grad, gate_sent, far_parts = sync(
        (arrived, f3, grad_gate, grad_up, wd_grad, gate_sent, far_parts)
    )

    def grown(at):
        return jnp.pad(arrived[at * cut : (at + 1) * cut], ((0, count - cut), (0, 0)))

    h3 = swap(gate_sent[0])
    came = around(plus(piece(wd_grad, 3), grown(0)))
    f2 = around(add(far_parts[1], f3))

    def hidden_step(grad_gate, grad_up, wg, wu):
        return apart(hidden_back(grad_gate, grad_up, wg, wu))

    given, kept = whole(hidden_step, grad_gate, grad_up, wg, wu)
    h3, came, f2, given, kept, gate_sent, grad_gate, grad_up = sync(
        (h3, came, f2, given, kept, gate_sent, grad_gate, grad_up)
    )
    h2, theirs = swap(gate_sent[1]), near(given)
    came = around(plus(piece(wd_grad, 2), grown(1), came))

    def rest_of_grads(grad_gate, grad_up, hidden_in, gate_sent, h3, far_part, f2):
        up_sent = pieces(weight_grad(hidden_in[:, half:], grad_up))
        wg_grad = weight_grad(hidden_in[:, :half], grad_gate)
        mixed_sent = [jnp.concatenate(pair, axis=0) for pair in zip(gate_sent[2:], up_sent[:2])]
        firsts = plus(piece(wg_grad, 3), h3), add(far_part, f2)
        return mixed_sent, up_sent[2:], wg_grad, weight_grad(hidden_in[:, :half], grad_up), firsts

    mixed_sent, up_sent, wg_grad, wu_grad, (gate_first, down_first) = whole(
        rest_of_grads, grad_gate, grad_up, hidden_in, gate_sent, h3, far_parts[2], f2
    )
    h2, theirs, came, mixed_sent, up_sent, wg_grad, wu_grad, kept, gate_first = sync(
        (h2, theirs, came, mixed_sent, up_sent, wg_grad, wu_grad, kept, gate_first)
    )
    pair = swap(mixed_sent[0])
    kept = add(kept, theirs)
    across = far(kept)
    came = around(plus(piece(wd_grad, 1), grown(2), came))
    gate_came = around(gate_first)
    across, pair, came, gate_came, kept, mixed_sent[1], up_sent, down_first = sync(
        (across, pair, came, gate_came, kept, mixed_sent[1], up_sent, down_first)
    )
    h1, v3 = pair[:count], pair[count:]
    pair = swap(mixed_sent[1])
    mine = add(kept, across)
    theirs = near(mine)
    gate_came = around(plus(piece(wg_grad, 2), h2, gate_came))
    up_came = around(plus(piece(wu_grad, 3), v3))
    f1 = around(down_first)

    def mixer_back(inputs, attn_sum, mine, theirs, grad_out, gains, full, saved):
        grad_hidden = together(mine, theirs)
        grad_resid, grad_attn, gain1, gain2 = attn_back(inputs, attn_sum, grad_hidden, grad_out, gains)
        grad_raw = attention_back(grad_attn, full, saved)
        given, kept = apart(dot("te,de->td", grad_raw, full[:, :width_qkv]).astype(low))
        return given, kept, grad_resid, grad_attn, gain1, gain2, grad_raw

    given, kept, grad_resid, grad_attn, grad_gain1, grad_gain2, grad_raw = whole(
        mixer_back, inputs, attn_sum, mine, theirs, grad_out, gains, full, saved
    )
    pair, gate_came, up_came, f1, given, kept, grad_resid, grad_attn, grad_raw, up_sent = sync(
        (pair, gate_came, up_came, f1, given, kept, grad_resid, grad_attn, grad_raw, up_sent)
    )
    h0, v2 = pair[:count], pair[count:]
    v1, theirs = swap(up_sent[0]), near(given)
    gate_came = around(plus(piece(wg_grad, 1), h1, gate_came))

    def mixer_grads(normed_low, mixed_low, grad_raw, grad_attn, far_part, f1):
        grads = weight_grad(normed_low, grad_raw), weight_grad(grad_attn, mixed_low)
        pairs = ((3, 2), (1, 0))
        mixer_sent = [jnp.concatenate([both(hops, half, grads) for hops in pair], axis=0) for pair in pairs]
        return mixer_sent, [both(hops, 0, grads) for hops in (3, 2, 1, 0)], add(far_part, f1)

    mixer_sent, mixer_own, down_last = whole(
        mixer_grads, saved[0], saved[-1], grad_raw, grad_attn, far_parts[3], f1
    )
    v1, theirs, gate_came, mixer_sent, mixer_own, kept, up_sent, down_last = sync(
        (v1, theirs, gate_came, mixer_sent, mixer_own, kept, up_sent, down_last)
    )
    v0, x32 = swap(up_sent[1]), swap(mixer_sent[0])
    kept = add(kept, theirs)
    across = far(kept)
    up_came = around(plus(piece(wu_grad, 2), v2, up_came))
    gate_late = tie(gate_came, up_came)
    sum_gate = plus(piece(wg_grad, 0), h0, gate_late, wide)
    up_came = around(plus(piece(wu_grad, 1), v1, up_came))
    v0, x32, up_came, across, kept, mixer_sent[1], inputs, down_last, sum_gate = sync(
        (v0, x32, up_came, across, kept, mixer_sent[1], inputs, down_last, sum_gate)
    )
    x10, b_far = swap(mixer_sent[1]), swap(down_last)
    m3 = around(plus(mixer_own[0], x32[:count]), 3)
    m2 = around(plus(mixer_own[1], x32[count:]), 2)
    mine = add(kept, across)
    theirs = near(mine)

    def finish(inputs, mine, theirs, grad_resid, attn_sum, ffn_parts, gains):
        block_out = layer_out(inputs, attn_sum, ffn_parts, gains, False)
        input_grad, gain0 = in_back(inputs, together(mine, theirs), grad_resid, gains)
        return block_out, input_grad, gain0

    block_out, input_grad, grad_gain0 = whole(
        finish, inputs, mine, theirs, grad_resid, attn_sum, ffn_parts, gains
    )
    x10, b_far, m3, m2, block_out, input_grad, grad_gain0 = sync(
        (x10, b_far, m3, m2, block_out, input_grad, grad_gain0)
    )
    mixed = plus(mixer_own[2], x10[:count])
    m1 = around(mixed)
    came = tie(came, mixed)
    grad_gains = jnp.concatenate([grad_gain0, grad_gain1, grad_gain2, grad_gain3], axis=0)
    gain_sum = grad_gains[:, :half] + swap(grad_gains[:, half:])
    gain_sum = gain_sum.reshape(4, outer, count)
    down_total = plus(piece(wd_grad, 0), jnp.concatenate([arrived[3 * cut :], b_far], axis=0), came, wide)
    new_down = update_down(behind(down_total)[0])
    sum_up = plus(piece(wu_grad, 0), v0, up_came, wide)
    new_gate_up = update_gate_up([sum_gate, sum_up])
    sum_gains = lax.dynamic_index_in_dim(gain_sum, place, 1, False)
    for hops in (1, 2, 3):
        given = lax.dynamic_index_in_dim(gain_sum, lax.rem(place + hops, outer), 1, False)
        sum_gains = sum_gains + around(given, hops)
    m1, sum_gains, new_down, new_gate_up = sync((m1, sum_gains, new_down, new_gate_up))
    sum_mixer = plus(mixer_own[3], x10[count:], m1, wide) + m2.astype(wide) + m3.astype(wide)
    return results(block_out, input_grad, update_mixer(sum_mixer), new_gate_up, new_down, sum_gains)


def solution(mesh):
    return jax.shard_map(
        shards,
        mesh=mesh,
        in_specs=(
            P("dp", None),
            P("dp"),
            P("dp", None),
            P("dp", "mp"),
            P(None, "dp", "mp"),
            P("mp", "dp"),
            P(None, "dp", "mp"),
            P("mp", "dp"),
            P(None, "dp"),
            P("dp", "mp"),
            P(None, "dp", "mp"),
            P("mp", "dp"),
            P(None, "dp", "mp"),
            P("mp", "dp"),
            P(None, "dp"),
            P("dp", "mp"),
            P(None, "dp", "mp"),
            P("mp", "dp"),
            P(None, "dp", "mp"),
            P("mp", "dp"),
            P(None, "dp"),
        ),
        out_specs=(
            P("dp", None),
            P("dp", None),
            P("dp", "mp"),
            P(None, "dp", "mp"),
            P("mp", "dp"),
            P(None, "dp", "mp"),
            P("mp", "dp"),
            P(None, "dp"),
            P("dp", "mp"),
            P(None, "dp", "mp"),
            P("mp", "dp"),
            P(None, "dp", "mp"),
            P("mp", "dp"),
            P(None, "dp"),
            P("dp", "mp"),
            P(None, "dp", "mp"),
            P("mp", "dp"),
            P(None, "dp", "mp"),
            P("mp", "dp"),
            P(None, "dp"),
            P("dp", "mp"),
            P(None, "dp", "mp"),
            P("mp", "dp"),
            P(None, "dp", "mp"),
            P("mp", "dp"),
            P(None, "dp"),
        ),
        check_vma=False,
    )
```
